32 devices in a mesh: src: 4 (over y, x), space: 8 (over z, core).
Axes of the slice: x: 2, y: 2, z: 4, core: 2. Of those that a mesh axis runs over, the one named last changes fastest.
Arguments:
- velocity: float32 [8, 512, 256], P('space'), may hold values from 0.5 to 2
- station_cells: int32 [4, 3], P('src'), may hold values from 0 to 511, as said below
- event_cells: int32 [3, 2048], replicated, may hold values from 0 to 511, as said below
- delays: float32 [4, 2048], P('src'), may hold values from -6 to 6
- active: int32 [2, 4, 8, 16], P(None, 'src', 'space'), may hold values from 0 to 1, as said below
Outputs:
- traveltimes: float32 [4, 8, 512, 256], P('src', 'space')
- kernel: float32 [8, 512, 256], P('space', 'src')
The draws below stay inside these ranges and needn't reach their ends.
Inputs may be any that keep to these rules, and one draw needn't show every extreme that they name: `station_cells`: stations lie in the top four layers: third coordinate below 4, first below 8, second below 512. `event_cells`: row 0 holds first coordinates below 8, row 1 second ones below 512, row 2 third ones below 256. `active`: 1 marks a tile whose cells are updated in that round for that station.
All inputs are finite; a program needn't handle non-finite values.
Results may differ from the reference program's by a relative error of at most 0.0003.
Values sent between devices are 32-bit elements; how exact they have to be, the bound alone decides.
No kernel may reach another device: no remote copies, remote signals or barrier semaphores. Data moves between devices by JAX's collectives and lax.ppermute only.
A program may use at most 64 MiB of HBM per device.

```python
import math
import jax
import jax.numpy as jnp
from jax import lax

CX = 1
NY = 512
NZ = 256
TY = 32
ROUNDS = 2
SWEEPS = 2
ADJ_SWEEPS = 4
SOURCES = 4
NX = 8
EVENTS = 2048
NTX = 8
TILES = 16


def station_helper(key):
    inner = jax.random.fold_in(key, 11)
    key_x, key_y, key_z = jax.random.split(inner, 3)
    station_x = jax.random.randint(key_x, (SOURCES,), 0, NX)
    station_y = jax.random.randint(key_y, (SOURCES,), 0, NY)
    station_z = jax.random.randint(key_z, (SOURCES,), 0, 4)
    station_x = station_x.at[0].set(NX - 1).at[1].set(0)
    station_y = station_y.at[0].set(NY - 1).at[1].set(0)
    station_z = station_z.at[0].set(0).at[1].set(0)
    return jnp.stack([station_x, station_y, station_z], axis=1).astype(jnp.int32)


def draw_station_cells(key, part):
    return station_helper(key)


def draw_event_cells(key, part):
    inner = jax.random.fold_in(key, 37)
    key_x, key_y, key_z = jax.random.split(inner, 3)
    event_x = jax.random.randint(key_x, (EVENTS,), 0, NX)
    event_y = jax.random.randint(key_y, (EVENTS,), 0, NY)
    event_z = jax.random.randint(key_z, (EVENTS,), 0, NZ)
    event_x = event_x.at[0].set(NX - 1).at[1].set(0)
    event_y = event_y.at[0].set(NY - 1).at[1].set(0)
    event_z = event_z.at[0].set(NZ - 1).at[1].set(0)
    return jnp.stack([event_x, event_y, event_z], axis=0).astype(jnp.int32)


def draw_active(key, part):
    stations = station_helper(key)
    tile_x = stations[:, 0] // CX
    inner = jax.random.fold_in(key, 23)
    rolls = jax.random.randint(inner, (ROUNDS, SOURCES, NTX, TILES), 0, 4)
    tiles = jnp.arange(NTX, dtype=jnp.int32)
    reach = max(NTX // 4, 1)
    near = jnp.abs(tiles[None, :] - tile_x[:, None]) <= reach
    level = jnp.where(near, 3, 1)[None, :, :, None]
    return (rolls < level).astype(jnp.int32)


def shard_levels(stream_key, dims, cuts, low, top_value):
    def one(position, shards_of):
        draws = jax.random.uniform(jax.random.fold_in(jax.random.fold_in(stream_key, 6), position), (shards_of,), jnp.float32, low / len(cuts), top_value / len(cuts))
        return jnp.repeat(jnp.exp(draws), dims[position] // shards_of).reshape((-1,) + (1,) * (len(dims) - position - 1))

    loudness = one(*cuts[0])
    for cut in cuts[1:]:
        loudness = loudness * one(*cut)
    return loudness


def gaussian(stream_key, extent, spread, bound, pieces=(), kind=jnp.bfloat16):
    entries = spread * jax.random.normal(stream_key, extent, jnp.float32)
    if pieces:
        entries = entries * shard_levels(stream_key, extent, pieces, -0.22, 0.18)
    return jnp.clip(entries, -bound, bound).astype(kind)


def setup_inputs(seed: int = 0) -> dict:
    keys = jax.random.split(jax.random.key(seed), 6)
    velocity = jnp.clip(jnp.exp(math.log(2.0) - 1.3862944 * jax.random.uniform(keys[0], (NX, NY, NZ), jnp.float32) ** shard_levels(keys[0], (NX, NY, NZ), ((0, 8),), -0.2, 0.2)), 0.5, 2.0)
    station_cells = draw_station_cells(jax.random.fold_in(keys[5], 71), 0)
    event_cells = draw_event_cells(jax.random.fold_in(keys[5], 71), 0)
    delays = gaussian(keys[3], (SOURCES, EVENTS), 1.0, 6.0, ((0, 4),), jnp.float32)
    active = draw_active(jax.random.fold_in(keys[5], 71), 0)
    return {"velocity": velocity, "station_cells": station_cells, "event_cells": event_cells, "delays": delays, "active": active}


BIG = 1000000.0

def godunov(near_x, near_y, near_z, cost_cell):
    lowest = jnp.minimum(jnp.minimum(near_x, near_y), near_z)
    highest = jnp.maximum(jnp.maximum(near_x, near_y), near_z)
    middle = jnp.maximum(jnp.minimum(near_x, near_y), jnp.minimum(jnp.maximum(near_x, near_y), near_z))
    first_gap = middle - lowest
    second_gap = highest - lowest
    single = lowest + cost_cell
    double = lowest + 0.5 * (first_gap + jnp.sqrt(jnp.maximum(2.0 * cost_cell * cost_cell - first_gap * first_gap, 0.0)))
    gaps = first_gap + second_gap
    triple = lowest + (gaps + jnp.sqrt(jnp.maximum(gaps * gaps - 3.0 * (first_gap * first_gap + second_gap * second_gap - cost_cell * cost_cell), 0.0))) / 3.0
    return jnp.where(single <= middle, single, jnp.where(double <= highest, double, triple))

def neighbours(field, fill):
    padded = jnp.pad(field, 1, constant_values=fill)
    return [padded[:-2, 1:-1, 1:-1], padded[2:, 1:-1, 1:-1], padded[1:-1, :-2, 1:-1], padded[1:-1, 2:, 1:-1], padded[1:-1, 1:-1, :-2], padded[1:-1, 1:-1, 2:]]

def smooth_along(extended, axis_index):
    length = extended.shape[axis_index]
    first = lax.slice_in_dim(extended, 0, length - 2, axis=axis_index)
    centre = lax.slice_in_dim(extended, 1, length - 1, axis=axis_index)
    after = lax.slice_in_dim(extended, 2, length, axis=axis_index)
    return (first + 2.0 * centre + after) * 0.25

def pad_zero(field, axis_index):
    widths = [(0, 0)] * field.ndim
    widths[axis_index] = (1, 1)
    return jnp.pad(field, widths)

def reference(velocity, station_cells, event_cells, delays, active):
    slowness = 1.0 / velocity
    grid_x = lax.broadcasted_iota(jnp.int32, (NX, NY, NZ), 0)
    grid_y = lax.broadcasted_iota(jnp.int32, (NX, NY, NZ), 1)
    grid_z = lax.broadcasted_iota(jnp.int32, (NX, NY, NZ), 2)
    event_x = event_cells[0]
    event_y = event_cells[1]
    event_z = event_cells[2]
    flat_index = (event_x * (NY * NZ) + event_y * NZ + event_z).astype(jnp.int32)

    def station_solve(carry, inputs):
        station, delay_row, active_rows = inputs
        station_x = station[0]
        station_y = station[1]
        station_z = station[2]
        diff_x = (grid_x - station_x).astype(jnp.float32)
        diff_y = (grid_y - station_y).astype(jnp.float32)
        diff_z = (grid_z - station_z).astype(jnp.float32)
        times = jnp.sqrt(diff_x * diff_x + diff_y * diff_y + diff_z * diff_z)
        station_mask = (grid_x == station_x) & (grid_y == station_y) & (grid_z == station_z)
        for round_index in range(ROUNDS):
            tile_mask = (active_rows[round_index] > 0)[:, None, :, None, None]
            for sweep in range(SWEEPS):
                beside_all = neighbours(times, BIG)
                update = godunov(jnp.minimum(beside_all[0], beside_all[1]), jnp.minimum(beside_all[2], beside_all[3]), jnp.minimum(beside_all[4], beside_all[5]), slowness)
                chosen = jnp.where(tile_mask, update.reshape(NX // CX, CX, NY // TY, TY, NZ), times.reshape(NX // CX, CX, NY // TY, TY, NZ)).reshape(NX, NY, NZ)
                times = jnp.where(station_mask, 0.0, chosen)
        picked = times.reshape(-1)[flat_index]
        event_dx = (event_x - station_x).astype(jnp.float32)
        event_dy = (event_y - station_y).astype(jnp.float32)
        event_dz = (event_z - station_z).astype(jnp.float32)
        direct = jnp.sqrt(event_dx * event_dx + event_dy * event_dy + event_dz * event_dz)
        misfit = picked - direct - delay_row
        source = jnp.zeros((NX * NY * NZ,), jnp.float32).at[flat_index].add(misfit).reshape(NX, NY, NZ)
        weights = [jnp.maximum(neighbour - times, 0.0) * velocity / 6.0 for neighbour in neighbours(times, BIG)]
        adjoint = source
        for sweep in range(ADJ_SWEEPS):
            summed = source
            for weight, neighbour in zip(weights, neighbours(adjoint, 0.0)):
                summed = summed + weight * neighbour
            adjoint = summed
        return (carry + adjoint, times)
    start = jnp.zeros((NX, NY, NZ), jnp.float32)
    adjoint_sum, travel = lax.scan(station_solve, start, (station_cells, delays, jnp.transpose(active, (1, 0, 2, 3))))
    density = slowness * adjoint_sum
    along_x = smooth_along(pad_zero(density, 0), 0)
    along_y = smooth_along(pad_zero(along_x, 1), 1)
    kernel = smooth_along(pad_zero(along_y, 2), 2)
    return (travel, kernel)
```

```python
import functools
import math

import jax
import jax.numpy as jnp
from jax import lax
from jax.experimental import pallas as pl
from jax.experimental.pallas import tpu as pltpu
from jax.sharding import PartitionSpec as P

TY = 32
ROUNDS = 2
SWEEPS = 2
ADJ_SWEEPS = 4
BIG = 1000000.0

HALO = ROUNDS * SWEEPS + ADJ_SWEEPS
ADJ_HALO = ADJ_SWEEPS + 1

VMEM = pltpu.VMEM
SMEM = pltpu.SMEM


def params(mib):
    return pltpu.CompilerParams(vmem_limit_bytes=mib * 1024 * 1024)


def spec(space):
    return pl.BlockSpec(memory_space=space)


def pack_kernel(rows, own_rows, scal, own, other, *outs):
    line_row, chip, core = scal[0], scal[1], scal[2]
    total = own.shape[0]
    chunk = math.gcd(own_rows, 8)
    for j, out in enumerate(outs):
        first = line_row + ((chip ^ j) * 2 + core) * own_rows - HALO
        for piece in range(rows // chunk):
            start = jnp.clip(first + piece * chunk, 0, total - chunk)
            start = pl.multiple_of(start, chunk)
            mine = own[pl.ds(start, chunk), :]
            theirs = other[pl.ds(start, chunk), :]
            out[0, piece * chunk : (piece + 1) * chunk, :] = jnp.where(core == 0, mine, theirs)
            out[1, piece * chunk : (piece + 1) * chunk, :] = jnp.where(core == 0, theirs, mine)


def scatter_kernel(layers, events, scal, cells, *refs):
    slots = len(refs) - 2
    pays, count, delay_sum = refs[:slots], refs[slots], refs[slots + 1]
    first_row = scal[3] + HALO - ADJ_HALO
    height, width = count.shape
    chunk = min(events, 512)
    cells_iota = lax.broadcasted_iota(jnp.int32, (height, chunk), 0)
    depth_iota = lax.broadcasted_iota(jnp.int32, (width, chunk), 0)
    contract = (((1,), (1,)), ((), ()))

    def step(index, carry):
        start = pl.multiple_of(index * chunk, chunk)
        where_x = cells[0:1, pl.ds(start, chunk)]
        where_y = cells[1:2, pl.ds(start, chunk)] - first_row
        where_z = cells[2:3, pl.ds(start, chunk)]
        at = jnp.where(where_y >= 0, where_y * layers + where_x, -1)
        hit = (cells_iota == at).astype(jnp.bfloat16)
        depth = (depth_iota == where_z).astype(jnp.bfloat16)

        def add(ref_index, value):
            if ref_index is None:
                count[...] += value
            else:
                delay_sum[ref_index] += value

        def dot(left):
            return lax.dot_general(left, depth, contract, preferred_element_type=jnp.float32)

        add(None, dot(hit))
        for slot in range(slots):
            delay = pays[slot][:, pl.ds(start, chunk)]
            high = delay.astype(jnp.bfloat16)
            low = (delay - high.astype(jnp.float32)).astype(jnp.bfloat16)
            add(slot, dot(hit * high) + dot(hit * low))
        return carry

    count[...] = jnp.zeros_like(count)
    delay_sum[...] = jnp.zeros_like(delay_sum)
    lax.fori_loop(0, events // chunk, step, 0)


def local_solve(near_x, near_y, near_z, cost, twice, one_half):
    small = jnp.minimum(near_x, near_y)
    large = jnp.maximum(near_x, near_y)
    lowest = jnp.minimum(small, near_z)
    highest = jnp.maximum(large, near_z)
    middle = jnp.maximum(small, jnp.minimum(large, near_z))
    first_gap = middle - lowest
    second_gap = highest - lowest
    single = lowest + cost
    double = lowest + 0.5 * (
        first_gap + jnp.sqrt(jnp.maximum(twice - first_gap * first_gap, 0.0))
    )
    rest = first_gap * first_gap + second_gap * (second_gap - first_gap)
    root = jnp.sqrt(jnp.maximum(one_half - rest, 0.0))
    triple = lowest + ((first_gap + second_gap) * (1.0 / 3.0) + root * (math.sqrt(2.0) / 3.0))
    return jnp.where(single <= middle, single, jnp.where(double <= highest, double, triple))


def solve_kernel(layers, own_rows, slots, chips, scal, *refs):
    rows = own_rows + 2 * HALO
    depth = refs[0].shape[-1]
    vel_in, refs = refs[:chips], refs[chips:]
    act_in, refs = refs[:chips], refs[chips:]
    count, delay_sum, refs = refs[0], refs[1], refs[2:]
    times_out, kernel_out, refs = refs[0], refs[1], refs[2:]
    speed, cost, twice, one_half, start, ping, pong, acts, mask, weight, src, adj_a, adj_b, total, flat = refs
    line, chip, y_first = scal[4], scal[1], scal[3]
    grid_rows = scal[5]
    block = math.gcd(own_rows, 2)

    shape3 = (block, layers, depth)
    layer_iota = lax.broadcasted_iota(jnp.int32, shape3, 1)
    depth_iota = lax.broadcasted_iota(jnp.int32, shape3, 2)
    layer_low, layer_high = layer_iota == 0, layer_iota == layers - 1
    depth_low, depth_high = depth_iota == 0, depth_iota == depth - 1

    def before(value, axis):
        return pltpu.roll(value, 1, axis)

    def after(value, axis):
        return pltpu.roll(value, value.shape[axis] - 1, axis)

    def loop(low, high, body, unroll=2):
        steps = (high - low) // block
        lax.fori_loop(
            0, steps, lambda i, carry: (body(low + i * block), carry)[1], 0, unroll=min(unroll, steps)
        )

    parts = depth // 128

    def scatter_layer(place, count_rows, value):
        for part in range(parts):
            flat.at[part][pl.ds(place, count_rows, stride=layers), :] = value[
                :, part * 128 : (part + 1) * 128
            ]

    def gather_layer(place, count_rows):
        return jnp.concatenate(
            [flat.at[part][pl.ds(place, count_rows, stride=layers), :] for part in range(parts)],
            axis=1,
        )

    def flat_span(row):
        return pl.ds(pl.multiple_of(row * layers, layers), block * layers)

    def take_rows(row):
        pieces = [flat[part, flat_span(row), :] for part in range(parts)]
        return jnp.concatenate(pieces, axis=1).reshape(shape3)

    def put_rows(row, value):
        value = value.reshape(block * layers, depth)
        for part in range(parts):
            flat[part, flat_span(row), :] = value[:, part * 128 : (part + 1) * 128]

    for place in range(layers):
        value = vel_in[0][place % 2]
        for j in range(1, chips):
            value = jnp.where((place // 2) ^ chip == j, vel_in[j][place % 2], value)
        scatter_layer(place, rows, value)
        row = act_in[0][place % 2 : place % 2 + 1, :]
        for j in range(1, chips):
            row = jnp.where(
                (place // 2) ^ chip == j, act_in[j][place % 2 : place % 2 + 1, :], row
            )
        acts[place : place + 1, :] = row

    def prepare(row):
        value = take_rows(row)
        slow = 1.0 / value
        square = slow * slow
        here = pl.ds(row, block)
        speed[here] = value * (1.0 / 6.0)
        cost[here] = slow
        twice[here] = 2.0 * square
        one_half[here] = 1.5 * square

    loop(0, rows, prepare)

    lanes = acts.shape[1]
    tiles = lanes // (slots * ROUNDS)
    lane_iota = lax.broadcasted_iota(jnp.int32, (layers, lanes), 1)
    tile_first = (y_first + TY) // TY - 1
    tile_span = (rows + TY - 2) // TY + 1

    for slot in range(slots):
        at_x, at_y, at_z = scal[6 + 3 * slot], scal[7 + 3 * slot], scal[8 + 3 * slot]
        flat_x = (layer_iota - at_x)[0:1].astype(jnp.float32)
        flat_z = (depth_iota - at_z)[0:1].astype(jnp.float32)
        across = flat_x * flat_x + flat_z * flat_z
        at_station = ((layer_iota == at_x) & (depth_iota == at_z))[0:1]

        def fill(i, carry):
            y = y_first - 1 + i
            gap = (y - at_y).astype(jnp.float32)
            far = jnp.where((y >= 0) & (y < grid_rows), gap * gap, BIG * BIG)
            start[pl.ds(i, 1)] = jnp.where(
                far < BIG * BIG, jnp.sqrt(across + far), BIG
            )
            return carry

        lax.fori_loop(0, rows + 2, fill, 0, unroll=2)

        for part in range(ROUNDS):
            columns = []
            for t in range(tile_span):
                tile = tile_first + t
                column = (slot * ROUNDS + part) * tiles + tile
                column = jnp.where((tile >= 0) & (tile < tiles), column, -1)
                picked = jnp.sum(jnp.where(lane_iota == column, acts[...], 0.0), axis=1, keepdims=True)
                columns.append(jnp.broadcast_to(picked, (layers, 128)))
            for i in range(rows):
                value = columns[0]
                for t in range(1, tile_span):
                    value = jnp.where(y_first + i >= (tile_first + t) * TY, columns[t], value)
                mask[part, i] = value

        def sweep(source, target, low, high, part):
            def body(row):
                field = source[pl.ds(row, block + 2)]
                here = field[1 : block + 1]
                near_y = jnp.minimum(field[:block], field[2:])
                near_x = jnp.minimum(
                    jnp.where(layer_low, BIG, before(here, 1)), jnp.where(layer_high, BIG, after(here, 1))
                )
                near_z = jnp.minimum(
                    jnp.where(depth_low, BIG, before(here, 2)), jnp.where(depth_high, BIG, after(here, 2))
                )
                span = pl.ds(row, block)
                update = local_solve(near_x, near_y, near_z, cost[span], twice[span], one_half[span])
                on = mask[part, span]
                on = jnp.concatenate([on] * (depth // 128), axis=2)
                target[pl.ds(row + 1, block)] = jnp.where(on > 0.0, update, here)

            loop(low, high, body)
            local = at_y - y_first

            @pl.when((local >= low) & (local < high))
            def _():
                line_here = pl.ds(local + 1, 1)
                target[line_here] = jnp.where(at_station, 0.0, target[line_here])

        fields = [start, ping, pong, ping, pong]
        for index in range(ROUNDS * SWEEPS):
            sweep(fields[index], fields[index + 1], index, rows - index, index // SWEEPS)
        final = fields[ROUNDS * SWEEPS]

        to_line = line ^ slot

        def flatten(row):
            put_rows(row, final[pl.ds(row + HALO + 1, block)])

        loop(0, own_rows, flatten)
        for place in range(layers):
            times_out[to_line, place] = gather_layer(place, own_rows)

        shift = HALO - ADJ_HALO
        adj_rows = own_rows + 2 * ADJ_HALO

        def make_source(row):
            span = pl.ds(pl.multiple_of(row * layers, layers), block * layers)
            moved = final[pl.ds(row + shift + 1, block)] - start[pl.ds(row + shift + 1, block)]
            src[pl.ds(row, block)] = count[span, :].reshape(shape3) * moved - delay_sum[
                slot, span, :
            ].reshape(shape3)

        loop(0, adj_rows, make_source)

        def make_weight(row):
            field = final[pl.ds(row + shift, block + 2)]
            here = field[1 : block + 1]
            scale = speed[pl.ds(row + shift, block)]
            span = pl.ds(row, block)

            def rise(value):
                return jnp.maximum(value - here, 0.0) * scale

            weight[0, span] = jnp.where(layer_low, 0.0, rise(before(here, 1)))
            weight[1, span] = jnp.where(layer_high, 0.0, rise(after(here, 1)))
            weight[2, span] = rise(field[:block])
            weight[3, span] = rise(field[2:])
            weight[4, span] = jnp.where(depth_low, 0.0, rise(before(here, 2)))
            weight[5, span] = jnp.where(depth_high, 0.0, rise(after(here, 2)))

        loop(1, adj_rows - 1, make_weight)

        def adjoint_sweep(source, target, low, high, last):
            def body(row):
                field = source[pl.ds(row - 1, block + 2)]
                here = field[1 : block + 1]
                span = pl.ds(row, block)
                value = src[span]
                value = value + weight[0, span] * before(here, 1)
                value = value + weight[1, span] * after(here, 1)
                value = value + weight[2, span] * field[:block]
                value = value + weight[3, span] * field[2:]
                value = value + weight[4, span] * before(here, 2)
                value = value + weight[5, span] * after(here, 2)
                if last and slot > 0:
                    value = value + target[span]
                target[span] = value

            loop(low, high, body)

        fields = [src, adj_a, adj_b, adj_a, total]
        for index in range(ADJ_SWEEPS):
            adjoint_sweep(
                fields[index],
                fields[index + 1],
                index + 1,
                adj_rows - 1 - index,
                index == ADJ_SWEEPS - 1,
            )

    def smooth(low, here, high):
        return (low + 2.0 * here + high) * 0.25

    def density(row):
        span = pl.ds(row, block)
        value = total[span] * cost[pl.ds(row + HALO - ADJ_HALO, block)]
        low = jnp.where(layer_low, 0.0, before(value, 1))
        high = jnp.where(layer_high, 0.0, after(value, 1))
        adj_a[span] = smooth(low, value, high)

    loop(ADJ_SWEEPS, ADJ_SWEEPS + own_rows + 2, density)

    def finish(row):
        field = adj_a[pl.ds(row + ADJ_SWEEPS, block + 2)]
        value = smooth(field[:block], field[1 : block + 1], field[2:])
        low = jnp.where(depth_low, 0.0, before(value, 2))
        high = jnp.where(depth_high, 0.0, after(value, 2))
        value = smooth(low, value, high)
        put_rows(row, value)

    loop(0, own_rows, finish)
    for place in range(layers):
        kernel_out[place] = gather_layer(place, own_rows)


def per_device(velocity, station_cells, event_cells, delays, active):
    _, grid_rows, depth = velocity.shape
    slots, layers = lax.axis_size("src"), lax.axis_size("space")
    chips = layers // 2
    events = event_cells.shape[1]
    tiles = active.shape[-1]
    line_rows = grid_rows // slots
    own_rows = line_rows // layers
    rows = own_rows + 2 * HALO
    adj_rows = own_rows + 2 * ADJ_HALO
    line, place = lax.axis_index("src"), lax.axis_index("space")
    chip, core = place // 2, place % 2

    def to_line(array, j):
        return lax.ppermute(array, "src", [(i, i ^ j) for i in range(slots)])

    def to_chip(array, j):
        return lax.ppermute(array, "space", [(i, i ^ (2 * j)) for i in range(layers)])

    def to_core(array):
        return lax.ppermute(array, "space", [(i, i ^ 1) for i in range(layers)])

    f32 = jnp.float32
    pad = -(-(3 + ROUNDS * tiles) // 128) * 128
    tail = jnp.concatenate(
        [station_cells.reshape(1, 3), active.reshape(1, ROUNDS * tiles)], axis=1
    ).astype(f32)
    tail = jnp.pad(tail, ((0, 0), (0, pad - tail.shape[1])))
    payload = jnp.concatenate([delays, tail], axis=1)
    pays = [payload] + [to_line(payload, j) for j in range(1, slots)]

    other = to_core(velocity[0])
    y_first = line * line_rows + place * own_rows - HALO
    here = jnp.stack([line * line_rows, chip, core, y_first, line, jnp.int32(grid_rows)]).astype(jnp.int32)
    block = jax.ShapeDtypeStruct((2, rows, depth), f32)
    packed = pl.pallas_call(
        functools.partial(pack_kernel, rows, own_rows),
        out_shape=[block] * chips,
        in_specs=[spec(SMEM), spec(VMEM), spec(VMEM)],
        out_specs=[spec(VMEM)] * chips,
        compiler_params=params(32),
        name="pack",
    )(here, velocity[0], other)
    vel = [packed[0]] + [to_chip(packed[j], j) for j in range(1, chips)]

    tails = [p[:, events:] for p in pays]
    act = jnp.concatenate([t[:, 3 : 3 + ROUNDS * tiles] for t in tails], axis=1)
    act_other = to_core(act)
    act_pair = jnp.where(
        core == 0, jnp.concatenate([act, act_other]), jnp.concatenate([act_other, act])
    )
    acts = [act_pair] + [to_chip(act_pair, j) for j in range(1, chips)]

    stations = jnp.concatenate([t[0, :3] for t in tails]).astype(jnp.int32)
    scal = jnp.concatenate([here, stations])

    count, delay_sum = pl.pallas_call(
        functools.partial(scatter_kernel, layers, events),
        out_shape=[
            jax.ShapeDtypeStruct((adj_rows * layers, depth), f32),
            jax.ShapeDtypeStruct((slots, adj_rows * layers, depth), f32),
        ],
        in_specs=[spec(SMEM), spec(VMEM)] + [spec(VMEM)] * slots,
        out_specs=[spec(VMEM)] * 2,
        compiler_params=params(32),
        cost_estimate=pl.CostEstimate(flops=2 * 10**9, bytes_accessed=2 * 10**6, transcendentals=0),
        name="events",
    )(here, event_cells, *pays)

    def field(*lead):
        return pltpu.VMEM((*lead, layers, depth), f32)

    times, kernel = pl.pallas_call(
        functools.partial(solve_kernel, layers, own_rows, slots, chips),
        out_shape=[
            jax.ShapeDtypeStruct((slots, layers, own_rows, depth), f32),
            jax.ShapeDtypeStruct((layers, own_rows, depth), f32),
        ],
        in_specs=[spec(SMEM)] + [spec(VMEM)] * (2 * chips + 2),
        out_specs=[spec(VMEM)] * 2,
        scratch_shapes=[
            field(rows),
            field(rows),
            field(rows),
            field(rows),
            field(rows + 2),
            field(rows + 2),
            field(rows + 2),
            pltpu.VMEM((layers, act.shape[1]), f32),
            pltpu.VMEM((ROUNDS, rows, layers, 128), f32),
            field(6, adj_rows),
            field(adj_rows),
            field(adj_rows),
            field(adj_rows),
            field(adj_rows),
            pltpu.VMEM((depth // 128, rows * layers, 128), f32),
        ],
        compiler_params=params(60),
        name="solve",
    )(scal, *vel, *acts, count, delay_sum)

    out = lax.all_to_all(
        times.reshape(slots * layers, own_rows, depth), ("src", "space"), 0, 0, tiled=True
    )
    kernel = lax.all_to_all(kernel, "space", 0, 0, tiled=True)
    return (out.reshape(1, 1, grid_rows, depth), kernel.reshape(1, line_rows, depth))


def solution(mesh):
    return jax.shard_map(
        per_device,
        mesh=mesh,
        in_specs=(
            P("space", None, None),
            P("src", None),
            P(),
            P("src", None),
            P(None, "src", "space", None),
        ),
        out_specs=(P("src", "space", None, None), P("space", "src", None)),
        check_vma=False,
    )
```

```python
import functools
import math

import jax
import jax.numpy as jnp
from jax import lax
from jax.experimental import pallas as pl
from jax.experimental.pallas import tpu as pltpu
from jax.sharding import PartitionSpec as P

TY = 32
ROUNDS = 2
SWEEPS = 2
ADJ_SWEEPS = 4
BIG = 1000000.0

HALO = ROUNDS * SWEEPS + ADJ_SWEEPS
ADJ_HALO = ADJ_SWEEPS + 1

VMEM = pltpu.VMEM
SMEM = pltpu.SMEM


def spec(space):
    return pl.BlockSpec(memory_space=space)


def call(body, name, outs, operands, scratch=(), microseconds=1.0):
    held = [*operands, *outs, *scratch]
    limit = 4 * 2**20 + sum(4 * math.prod((*a.shape[:-2], -(-math.prod(a.shape[-2:-1]) // 8) * 8, max(a.shape[-1], 128))) for a in held)
    return pl.pallas_call(
        body,
        out_shape=list(outs),
        in_specs=[spec(SMEM if a.ndim == 1 else VMEM) for a in operands],
        out_specs=[spec(VMEM)] * len(outs),
        scratch_shapes=list(scratch),
        compiler_params=pltpu.CompilerParams(vmem_limit_bytes=limit),
        cost_estimate=pl.CostEstimate(
            flops=0, bytes_accessed=int(microseconds * 3.5e6), transcendentals=0
        ),
        name=name,
    )(*operands)


def head_kernel(delays, station, active, active_other, out):
    events = delays.shape[1]
    out[:, :events] = delays[...]
    out[:, events:] = jnp.zeros((1, out.shape[1] - events), jnp.float32)
    at = events
    out[:, at : at + 3] = station[...].astype(jnp.float32)
    for source in (active, active_other):
        for part in range(ROUNDS):
            at += 128
            out[:, at : at + source.shape[-1]] = source[part].astype(jnp.float32)


def pack_kernel(rows, own_rows, scal, own, other, *outs):
    line_row, chip, core = scal[0], scal[1], scal[2]
    total = own.shape[0]
    chunk = math.gcd(own_rows, 8)
    for j, out in enumerate(outs):
        first = line_row + ((chip ^ j) * 2 + core) * own_rows - HALO
        for piece in range(rows // chunk):
            start = jnp.clip(first + piece * chunk, 0, total - chunk)
            start = pl.multiple_of(start, chunk)
            out[0, piece * chunk : (piece + 1) * chunk, :] = own[pl.ds(start, chunk), :]
            out[1, piece * chunk : (piece + 1) * chunk, :] = other[pl.ds(start, chunk), :]


def scatter_kernel(layers, events, scal, cells, *refs):
    slots = len(refs) - 2
    pays, count, delay_sum = refs[:slots], refs[slots], refs[slots + 1]
    first_row = scal[3] + HALO - ADJ_HALO
    height, width = count.shape
    chunk = min(events, 512)
    cells_iota = lax.broadcasted_iota(jnp.int32, (height, chunk), 0)
    depth_iota = lax.broadcasted_iota(jnp.int32, (width, chunk), 0)
    contract = (((1,), (1,)), ((), ()))

    def step(index, carry):
        start = pl.multiple_of(index * chunk, chunk)
        where_x = cells[0:1, pl.ds(start, chunk)]
        where_y = cells[1:2, pl.ds(start, chunk)] - first_row
        where_z = cells[2:3, pl.ds(start, chunk)]
        at = jnp.where(where_y >= 0, where_y * layers + where_x, -1)
        hit = (cells_iota == at).astype(jnp.bfloat16)
        depth = (depth_iota == where_z).astype(jnp.bfloat16)

        def add(ref_index, value):
            if ref_index is None:
                count[...] += value
            else:
                delay_sum[ref_index] += value

        def dot(left):
            return lax.dot_general(left, depth, contract, preferred_element_type=jnp.float32)

        add(None, dot(hit))
        for slot in range(slots):
            delay = pays[slot][:, pl.ds(start, chunk)]
            high = delay.astype(jnp.bfloat16)
            low = (delay - high.astype(jnp.float32)).astype(jnp.bfloat16)
            add(slot, dot(hit * high) + dot(hit * low))
        return carry

    count[...] = jnp.zeros_like(count)
    delay_sum[...] = jnp.zeros_like(delay_sum)
    lax.fori_loop(0, events // chunk, step, 0)


LANES = 128


def get(ref, row, size, *lead):
    index = (*lead, pl.ds(row, size))
    return [
        ref[(*index, slice(None), slice(p, p + LANES))] for p in range(0, ref.shape[-1], LANES)
    ]


def put(ref, row, size, value, *lead):
    index = (*lead, pl.ds(row, size))
    for p, piece in enumerate(value):
        ref[(*index, slice(None), slice(p * LANES, (p + 1) * LANES))] = piece


def each(function, *values):
    return [function(*pieces) for pieces in zip(*values)]


def loop(low, high, size, body, unroll=1):
    steps = (high - low) // size
    if steps:
        lax.fori_loop(
            0,
            steps,
            lambda i, carry: (body(low + i * size, size), carry)[1],
            0,
            unroll=min(unroll, steps),
        )
    if low + steps * size < high:
        loop(low + steps * size, high, max(size // 2, 1), body)


class Grid:
    def __init__(self, size, layers, depth):
        shape = (size, layers, LANES)
        layer = lax.broadcasted_iota(jnp.int32, shape, 1)
        lane = lax.broadcasted_iota(jnp.int32, shape, 2)
        self.layers = layers
        self.layer_low, self.layer_high = layer == 0, layer == layers - 1
        self.lane_low, self.lane_high = lane == 0, lane == LANES - 1

    def layer_before(self, value):
        return [pltpu.roll(piece, 1, 1) for piece in value]

    def layer_after(self, value):
        return [pltpu.roll(piece, self.layers - 1, 1) for piece in value]

    def depth_before(self, value, fill=None):
        moved = [pltpu.roll(piece, 1, 2) for piece in value]
        first = moved[0] if fill is None else jnp.where(self.lane_low, fill, moved[0])
        rest = [
            jnp.where(self.lane_low, low, here) for low, here in zip(moved[:-1], moved[1:])
        ]
        return [first] + rest

    def depth_after(self, value, fill=None):
        moved = [pltpu.roll(piece, LANES - 1, 2) for piece in value]
        last = moved[-1] if fill is None else jnp.where(self.lane_high, fill, moved[-1])
        rest = [
            jnp.where(self.lane_high, high, here) for here, high in zip(moved[:-1], moved[1:])
        ]
        return rest + [last]

    def no_low(self, value, fill):
        return [jnp.where(self.layer_low, fill, piece) for piece in value]

    def no_high(self, value, fill):
        return [jnp.where(self.layer_high, fill, piece) for piece in value]


class Flat:
    def __init__(self, ref, layers):
        self.ref, self.layers, self.parts = ref, layers, ref.shape[0]

    def put_layer(self, place, rows, value):
        for p in range(self.parts):
            self.ref.at[p][pl.ds(place, rows, stride=self.layers), :] = value[
                :, p * LANES : (p + 1) * LANES
            ]

    def get_layer(self, place, rows):
        pieces = [
            self.ref.at[p][pl.ds(place, rows, stride=self.layers), :] for p in range(self.parts)
        ]
        return jnp.concatenate(pieces, axis=1)

    def span(self, row, size):
        return pl.ds(pl.multiple_of(row * self.layers, self.layers), size * self.layers)

    def get(self, row, size):
        return [
            self.ref[p, self.span(row, size), :].reshape(size, self.layers, LANES)
            for p in range(self.parts)
        ]

    def put(self, row, size, value):
        for p in range(self.parts):
            self.ref[p, self.span(row, size), :] = value[p].reshape(size * self.layers, LANES)


def root_of(value):
    value = jnp.maximum(value, 1e-30)
    return value * lax.rsqrt(value)


def distance(layers, at, y, grid_rows, size, row, piece):
    shape = (size, layers, LANES)
    dx = (lax.broadcasted_iota(jnp.int32, shape, 1) - at[0]).astype(jnp.float32)
    dz = (lax.broadcasted_iota(jnp.int32, shape, 2) + (piece * LANES - at[2])).astype(jnp.float32)
    here = lax.broadcasted_iota(jnp.int32, shape, 0) + (y + row)
    dy = (here - at[1]).astype(jnp.float32)
    far = jnp.sqrt(dx * dx + dy * dy + dz * dz)
    return jnp.where((here >= 0) & (here < grid_rows), far, BIG)


def local_solve(near_x, near_y, near_z, cost, twice, one_half):
    small = jnp.minimum(near_x, near_y)
    large = jnp.maximum(near_x, near_y)
    lowest = jnp.minimum(small, near_z)
    highest = jnp.maximum(large, near_z)
    middle = jnp.maximum(small, jnp.minimum(large, near_z))
    first_gap = middle - lowest
    second_gap = highest - lowest
    square = first_gap * first_gap
    single = lowest + cost
    double = lowest + 0.5 * (first_gap + root_of(twice - square))
    rest = square + second_gap * (second_gap - first_gap)
    root = root_of(one_half - rest)
    triple = lowest + ((first_gap + second_gap) * (1.0 / 3.0) + root * (math.sqrt(2.0) / 3.0))
    return jnp.where(single <= middle, single, jnp.where(double <= highest, double, triple))


SWEEP_ROWS = 4
SWEEP_UNROLL = 2


def sweep_kernel(layers, own_rows, slots, chips, scal, *refs):
    rows = own_rows + 2 * HALO
    depth = refs[0].shape[-1]
    parts = depth // LANES
    vel_in, refs = refs[:chips], refs[chips:]
    act_in, refs = refs[:chips], refs[chips:]
    times_out, final, speed, refs = refs[0], refs[1], refs[2], refs[3:]
    cost, twice, one_half, ping, pong, acts, mask, flat = refs
    flat = Flat(flat, layers)
    line, chip, core, y_first, grid_rows = scal[4], scal[1], scal[2], scal[3], scal[5]
    stations = [[scal[6 + 3 * slot + i] for i in range(3)] for slot in range(slots)]

    for j in range(chips):
        for c in range(2):
            place = (chip ^ j) * 2 + (core ^ c)
            flat.put_layer(place, rows, vel_in[j][c])
            for slot in range(slots):
                for part in range(ROUNDS):
                    acts[slot * ROUNDS + part, pl.ds(place, 1), :] = act_in[j][
                        pl.ds((slot * 2 + c) * ROUNDS + part, 1), :
                    ]

    def prepare(row, size):
        value = flat.get(row, size)
        slow = each(lambda v: 1.0 / v, value)
        put(speed, row, size, value)
        put(cost, row, size, slow)
        put(twice, row, size, each(lambda f: 2.0 * (f * f), slow))
        put(one_half, row, size, each(lambda f: 1.5 * (f * f), slow))

    loop(0, rows, 4, prepare)

    def fill(row, size):
        for slot in range(slots):
            value = [
                distance(layers, stations[slot], y_first - 1, grid_rows, size, row, piece)
                for piece in range(parts)
            ]
            put(ping, row, size, value, slot)

    loop(0, rows + 2, 2, fill)

    lane_iota = lax.broadcasted_iota(jnp.int32, (layers, LANES), 1)
    tile_first = (y_first + TY) // TY - 1
    tile_span = (rows + TY - 2) // TY + 1
    for slot in range(slots):
        for part in range(ROUNDS):
            act = acts[slot * ROUNDS + part]
            columns = []
            for t in range(tile_span):
                here = lane_iota == tile_first + t
                picked = jnp.sum(jnp.where(here, act, 0.0), axis=1, keepdims=True)
                columns.append(jnp.broadcast_to(picked, (layers, LANES)))
            for i in range(rows):
                value = columns[0]
                for t in range(1, tile_span):
                    value = jnp.where(y_first + i >= (tile_first + t) * TY, columns[t], value)
                mask[slot, part, i] = value

    def sweep(source, target, low, high, part, shift):
        def body(row, size):
            grid = Grid(size, layers, depth)
            costs = get(cost, row, size), get(twice, row, size), get(one_half, row, size)
            for slot in range(slots):
                field = get(source, row, size + 2, slot)
                here = each(lambda f: f[1 : size + 1], field)
                near_y = each(lambda f: jnp.minimum(f[:size], f[2:]), field)
                near_x = each(
                    jnp.minimum,
                    grid.no_low(grid.layer_before(here), BIG),
                    grid.no_high(grid.layer_after(here), BIG),
                )
                near_z = each(
                    jnp.minimum, grid.depth_before(here, BIG), grid.depth_after(here, BIG)
                )
                update = each(local_solve, near_x, near_y, near_z, *costs)
                on = mask[slot, part, pl.ds(row, size)] > 0.0
                put(
                    target,
                    row + shift,
                    size,
                    each(lambda u, h: jnp.where(on, u, h), update, here),
                    slot,
                )

        loop(low, high, SWEEP_ROWS, body, SWEEP_UNROLL)
        for slot in range(slots):
            at_x, at_y, at_z = stations[slot]
            local = at_y - y_first

            @pl.when((local >= low) & (local < high))
            def _():
                shape = (1, layers, depth)
                there = (lax.broadcasted_iota(jnp.int32, shape, 1) == at_x) & (
                    lax.broadcasted_iota(jnp.int32, shape, 2) == at_z
                )
                here = slot, pl.ds(local + shift, 1)
                target[here] = jnp.where(there, 0.0, target[here])

    fields = [ping, pong]
    last = ROUNDS * SWEEPS - 1
    for index in range(last):
        sweep(fields[index % 2], fields[(index + 1) % 2], index, rows - index, index // SWEEPS, 1)
    sweep(fields[last % 2], final, last, rows - last, last // SWEEPS, -last)

    for slot in range(slots):
        loop(0, own_rows, 4, lambda row, size: flat.put(row, size, get(final, row + ADJ_HALO, size, slot)))
        for place in range(layers):
            times_out[line ^ slot, place] = flat.get_layer(place, own_rows)


ADJ_ROWS = 4
ADJ_UNROLL = 2


def adjoint_kernel(layers, own_rows, slots, scal, final, speed, count, delay_sum, *refs):
    depth = final.shape[-1]
    parts = depth // LANES
    kernel_out, refs = refs[:layers], refs[layers:]
    weight, src, adj_a, adj_b, density, flat = refs
    together = weight.shape[0]
    flat = Flat(flat, layers)
    y_first, grid_rows = scal[3], scal[5]
    stations = [[scal[6 + 3 * slot + i] for i in range(3)] for slot in range(slots)]
    shift = HALO - ADJ_HALO
    rows = own_rows + 2 * ADJ_HALO

    def sums(ref, row, size, *lead):
        span = pl.ds(pl.multiple_of(row * layers, layers), size * layers)
        return [
            ref[(*lead, span, slice(p * LANES, (p + 1) * LANES))].reshape(size, layers, LANES)
            for p in range(parts)
        ]

    def make_source(group, row, size):
        number = sums(count, row, size)
        for slot in group:
            straight = [
                distance(layers, stations[slot], y_first + shift, grid_rows, size, row, piece)
                for piece in range(parts)
            ]
            value = each(
                lambda n, t, d, s: n * (t - d) - s,
                number,
                get(final, row, size, slot),
                straight,
                sums(delay_sum, row, size, slot),
            )
            put(src, row, size, value, slot - group[0])

    def make_weight(group, row, size):
        grid = Grid(size, layers, depth)
        scale = each(lambda v: v * (1.0 / 6.0), get(speed, row + shift, size))
        for slot in group:
            field = get(final, row - 1, size + 2, slot)
            here = each(lambda f: f[1 : size + 1], field)

            def rise(value):
                return each(lambda v, h, s: jnp.maximum(v - h, 0.0) * s, value, here, scale)

            def keep(value, piece, edge):
                return [jnp.where(edge, 0.0, v) if p == piece else v for p, v in enumerate(value)]

            six = [
                grid.no_low(rise(grid.layer_before(here)), 0.0),
                grid.no_high(rise(grid.layer_after(here)), 0.0),
                rise(each(lambda f: f[:size], field)),
                rise(each(lambda f: f[2:], field)),
                keep(rise(grid.depth_before(here)), 0, grid.lane_low),
                keep(rise(grid.depth_after(here)), parts - 1, grid.lane_high),
            ]
            for n, value in enumerate(six):
                put(weight, row, size, value, slot - group[0], n)

    def multiply_add(value, factor, neighbour):
        return value + factor * neighbour

    def smooth(low, here, high):
        return (low + 2.0 * here + high) * 0.25

    def sweep(group, source, target, low, high):
        def body(row, size):
            grid = Grid(size, layers, depth)
            total = None if group[0] == 0 else get(density, row, size)
            for slot in range(len(group)):
                field = get(source, row - 1, size + 2, slot)
                here = each(lambda f: f[1 : size + 1], field)
                around = [
                    grid.layer_before(here),
                    grid.layer_after(here),
                    each(lambda f: f[:size], field),
                    each(lambda f: f[2:], field),
                    grid.depth_before(here),
                    grid.depth_after(here),
                ]
                value = get(src, row, size, slot)
                for n, neighbour in enumerate(around):
                    value = each(multiply_add, value, get(weight, row, size, slot, n), neighbour)
                if target is not None:
                    put(target, row, size, value, slot)
                else:
                    total = value if total is None else each(jnp.add, total, value)
            if target is None:
                if group[-1] == slots - 1:
                    value = each(lambda t, v: t / v, total, get(speed, row + shift, size))
                    low = grid.no_low(grid.layer_before(value), 0.0)
                    high = grid.no_high(grid.layer_after(value), 0.0)
                    total = each(smooth, low, value, high)
                put(density, row, size, total)

        loop(low, high, ADJ_ROWS, body, ADJ_UNROLL)

    for first in range(0, slots, together):
        group = range(first, min(first + together, slots))
        loop(0, rows, 2, functools.partial(make_source, group))
        loop(1, rows - 1, 2, functools.partial(make_weight, group))
        fields = [src] + [(adj_a, adj_b)[i % 2] for i in range(ADJ_SWEEPS - 1)] + [None]
        for index in range(ADJ_SWEEPS):
            sweep(group, fields[index], fields[index + 1], index + 1, rows - 1 - index)

    def finish(row, size):
        grid = Grid(size, layers, depth)
        field = get(density, row + ADJ_SWEEPS, size + 2)
        value = each(lambda f: smooth(f[:size], f[1 : size + 1], f[2:]), field)
        low, high = grid.depth_before(value, 0.0), grid.depth_after(value, 0.0)
        flat.put(row, size, each(smooth, low, value, high))

    loop(0, own_rows, 4, finish)
    for m, out in enumerate(kernel_out):
        out[...] = flat.get_layer(scal[1] * 2 + scal[2] ^ m, own_rows)


def join_kernel(scal, *refs):
    blocks, out = refs[:-1], refs[-1]
    rows = blocks[0].shape[0]
    for m, block in enumerate(blocks):
        out[0, pl.ds(pl.multiple_of(((scal[1] * 2 + scal[2]) ^ m) * rows, rows), rows), :] = block[...]


def per_device(velocity, station_cells, event_cells, delays, active):
    _, grid_rows, depth = velocity.shape
    slots, layers = lax.axis_size("src"), lax.axis_size("space")
    chips = layers // 2
    events = event_cells.shape[1]
    line_rows = grid_rows // slots
    own_rows = line_rows // layers
    rows = own_rows + 2 * HALO
    adj_rows = own_rows + 2 * ADJ_HALO
    line, place = lax.axis_index("src"), lax.axis_index("space")
    chip, core = place // 2, place % 2

    def to_line(array, j):
        return lax.ppermute(array, "src", [(i, i ^ j) for i in range(slots)])

    def to_chip(array, j):
        return lax.ppermute(array, "space", [(i, i ^ (2 * j)) for i in range(layers)])

    def to_core(array):
        return lax.ppermute(array, "space", [(i, i ^ 1) for i in range(layers)])

    f32 = jnp.float32
    def out(*shape):
        return jax.ShapeDtypeStruct(shape, f32)

    def scratch(*shape):
        return pltpu.VMEM(shape, f32)

    def field(*lead):
        return (*lead, layers, depth)

    y_first = line * line_rows + place * own_rows - HALO
    here = jnp.stack([line * line_rows, chip, core, y_first, line, jnp.int32(grid_rows)])
    here = here.astype(jnp.int32)

    other = to_core(velocity[0])
    active_other = to_core(active[:, 0])
    (payload,) = call(
        head_kernel,
        "head",
        [out(1, events + LANES * (1 + 2 * ROUNDS))],
        [delays, station_cells, active[:, 0], active_other],
    )
    pays = [payload] + [to_line(payload, j) for j in range(1, slots)]

    packed = call(
        functools.partial(pack_kernel, rows, own_rows),
        "pack",
        [out(2, rows, depth)] * chips,
        [here, velocity[0], other],
    )
    vel = [to_chip(packed[j], j) for j in range(1, chips)]

    pays, cells, own_block = lax.optimization_barrier((pays, event_cells, packed[0]))
    act = jnp.concatenate(
        [
            p[:, at : at + LANES]
            for p in pays
            for at in range(events + LANES, payload.shape[1], LANES)
        ]
    )
    acts = [act] + [to_chip(act, j) for j in range(1, chips)]
    stations = jnp.concatenate([p[0, events : events + 3] for p in pays]).astype(jnp.int32)
    scal = jnp.concatenate([here, stations])

    count, delay_sum = call(
        functools.partial(scatter_kernel, layers, events),
        "events",
        [out(adj_rows * layers, depth), out(slots, adj_rows * layers, depth)],
        [here, cells, *pays],
        microseconds=4.0,
    )

    together = min(slots, 4)
    flat = scratch(depth // LANES, rows * layers, LANES)
    times, final, speed = call(
        functools.partial(sweep_kernel, layers, own_rows, slots, chips),
        "sweeps",
        [
            out(slots, layers, own_rows, depth),
            out(*field(slots, adj_rows)),
            out(*field(rows)),
        ],
        [scal, own_block, *vel, *acts],
        [
            scratch(*field(rows)),
            scratch(*field(rows)),
            scratch(*field(rows)),
            scratch(*field(slots, rows + 2)),
            scratch(*field(slots, rows + 2)),
            scratch(slots * ROUNDS, layers, LANES),
            scratch(slots, ROUNDS, rows, layers, LANES),
            flat,
        ],
        microseconds=10.0,
    )
    kernel = call(
        functools.partial(adjoint_kernel, layers, own_rows, slots),
        "adjoint",
        [out(own_rows, depth)] * layers,
        [scal, final, speed, count, delay_sum],
        [
            scratch(*field(together, 6, adj_rows)),
            scratch(*field(together, adj_rows)),
            scratch(*field(together, adj_rows)),
            scratch(*field(together, adj_rows)),
            scratch(*field(adj_rows)),
            flat,
        ],
        microseconds=7.0,
    )

    times = lax.all_to_all(
        times.reshape(slots * layers, own_rows, depth), ("src", "space"), 0, 0, tiled=True
    )
    blocks = [kernel[0]] + [
        lax.ppermute(kernel[m], "space", [(i, i ^ m) for i in range(layers)])
        for m in range(1, layers)
    ]
    (kernel,) = call(join_kernel, "join", [out(1, line_rows, depth)], [here, *blocks])
    return (times.reshape(1, 1, grid_rows, depth), kernel)


def solution(mesh):
    return jax.shard_map(
        per_device,
        mesh=mesh,
        in_specs=(
            P("space", None, None),
            P("src", None),
            P(),
            P("src", None),
            P(None, "src", "space", None),
        ),
        out_specs=(P("src", "space", None, None), P("space", "src", None)),
        check_vma=False,
    )
```

```python
import functools
import math

import jax
import jax.numpy as jnp
from jax import lax
from jax.experimental import pallas as pl
from jax.experimental.pallas import tpu as pltpu
from jax.sharding import PartitionSpec as P

TY = 32
ROUNDS = 2
SWEEPS = 2
ADJ_SWEEPS = 4
BIG = 1000000.0
LANES = 128

HALO = ROUNDS * SWEEPS + ADJ_SWEEPS
ADJ_HALO = ADJ_SWEEPS + 1

VMEM = pltpu.VMEM
SMEM = pltpu.SMEM


def spec(space):
    return pl.BlockSpec(memory_space=space)


def call(body, name, outs, operands, scratch=(), microseconds=1.0):
    held = [*operands, *outs, *scratch]
    limit = 4 * 2**20 + sum(4 * math.prod((*a.shape[:-2], -(-math.prod(a.shape[-2:-1]) // 8) * 8, max(a.shape[-1], 128))) for a in held)
    return pl.pallas_call(
        body,
        out_shape=list(outs),
        in_specs=[spec(SMEM if a.ndim == 1 else VMEM) for a in operands],
        out_specs=[spec(VMEM)] * len(outs),
        scratch_shapes=list(scratch),
        compiler_params=pltpu.CompilerParams(vmem_limit_bytes=limit),
        cost_estimate=pl.CostEstimate(
            flops=0, bytes_accessed=int(microseconds * 3.5e6), transcendentals=0
        ),
        name=name,
    )(*operands)


def head_kernel(delays, station, active, active_other, out):
    events = delays.shape[1]
    out[:, :events] = delays[...]
    out[:, events:] = jnp.zeros((1, out.shape[1] - events), jnp.float32)
    at = events
    out[:, at : at + 3] = station[...].astype(jnp.float32)
    for source in (active, active_other):
        for part in range(ROUNDS):
            at += LANES
            out[:, at : at + source.shape[-1]] = source[part].astype(jnp.float32)


def pack_kernel(rows, own_rows, slots, scal, own, other, *refs):
    line_row, chip, core = scal[0], scal[1], scal[2]
    pays, outs = refs[:slots], refs[slots:]
    total = own.shape[0]
    chunk = math.gcd(own_rows, 8)
    at = pays[0].shape[1] - 2 * ROUNDS * LANES
    for j, out in enumerate(outs):
        first = line_row + ((chip ^ j) * 2 + core) * own_rows - HALO
        for piece in range(rows // chunk):
            start = jnp.clip(first + piece * chunk, 0, total - chunk)
            start = pl.multiple_of(start, chunk)
            out[piece * chunk : (piece + 1) * chunk, :] = own[pl.ds(start, chunk), :]
            out[rows + piece * chunk : rows + (piece + 1) * chunk, :] = other[pl.ds(start, chunk), :]
        out[2 * rows :, :] = jnp.zeros_like(out[2 * rows :, :])
        for slot, pay in enumerate(pays):
            for part in range(ROUNDS):
                row = 2 * rows + slot * ROUNDS + part
                for c in range(2):
                    tile = at + (c * ROUNDS + part) * LANES
                    out[row : row + 1, c * LANES : (c + 1) * LANES] = pay[:, tile : tile + LANES]


def scatter_kernel(layers, events, scal, cells, *refs):
    slots = len(refs) - 2
    pays, count, delay_sum = refs[:slots], refs[slots], refs[slots + 1]
    first_row = scal[3] + HALO - ADJ_HALO
    height, width = count.shape
    chunk = min(events, 512)
    cells_iota = lax.broadcasted_iota(jnp.int32, (height, chunk), 0)
    depth_iota = lax.broadcasted_iota(jnp.int32, (width, chunk), 0)
    contract = (((1,), (1,)), ((), ()))

    def step(index, carry):
        start = pl.multiple_of(index * chunk, chunk)
        where_x = cells[0:1, pl.ds(start, chunk)]
        where_y = cells[1:2, pl.ds(start, chunk)] - first_row
        where_z = cells[2:3, pl.ds(start, chunk)]
        at = jnp.where(where_y >= 0, where_y * layers + where_x, -1)
        hit = (cells_iota == at).astype(jnp.bfloat16)
        depth = (depth_iota == where_z).astype(jnp.bfloat16)

        def add(ref_index, value):
            if ref_index is None:
                count[...] += value
            else:
                delay_sum[ref_index] += value

        def dot(left):
            return lax.dot_general(left, depth, contract, preferred_element_type=jnp.float32)

        add(None, dot(hit))
        for slot in range(slots):
            delay = pays[slot][:, pl.ds(start, chunk)]
            high = delay.astype(jnp.bfloat16)
            low = (delay - high.astype(jnp.float32)).astype(jnp.bfloat16)
            add(slot, dot(hit * high) + dot(hit * low))
        return carry

    count[...] = jnp.zeros_like(count)
    delay_sum[...] = jnp.zeros_like(delay_sum)
    lax.fori_loop(0, events // chunk, step, 0)


def get(ref, row, size, *lead):
    index = (*lead, pl.ds(row, size))
    return [
        ref[(*index, slice(None), slice(p, p + LANES))] for p in range(0, ref.shape[-1], LANES)
    ]


def put(ref, row, size, value, *lead):
    index = (*lead, pl.ds(row, size))
    for p, piece in enumerate(value):
        ref[(*index, slice(None), slice(p * LANES, (p + 1) * LANES))] = piece


def each(function, *values):
    return [function(*pieces) for pieces in zip(*values)]


def loop(low, high, size, body, unroll=1):
    steps = (high - low) // size
    if steps:
        lax.fori_loop(
            0,
            steps,
            lambda i, carry: (body(low + i * size, size), carry)[1],
            0,
            unroll=min(unroll, steps),
        )
    if low + steps * size < high:
        loop(low + steps * size, high, max(size // 2, 1), body)


class Grid:
    def __init__(self, size, layers, depth):
        shape = (size, layers, LANES)
        layer = lax.broadcasted_iota(jnp.int32, shape, 1)
        lane = lax.broadcasted_iota(jnp.int32, shape, 2)
        self.layers = layers
        self.layer_low, self.layer_high = layer == 0, layer == layers - 1
        self.lane_low, self.lane_high = lane == 0, lane == LANES - 1

    def layer_before(self, value):
        return [pltpu.roll(piece, 1, 1) for piece in value]

    def layer_after(self, value):
        return [pltpu.roll(piece, self.layers - 1, 1) for piece in value]

    def depth_before(self, value, fill=None):
        moved = [pltpu.roll(piece, 1, 2) for piece in value]
        first = moved[0] if fill is None else jnp.where(self.lane_low, fill, moved[0])
        rest = [
            jnp.where(self.lane_low, low, here) for low, here in zip(moved[:-1], moved[1:])
        ]
        return [first] + rest

    def depth_after(self, value, fill=None):
        moved = [pltpu.roll(piece, LANES - 1, 2) for piece in value]
        last = moved[-1] if fill is None else jnp.where(self.lane_high, fill, moved[-1])
        rest = [
            jnp.where(self.lane_high, high, here) for here, high in zip(moved[:-1], moved[1:])
        ]
        return rest + [last]

    def no_low(self, value, fill):
        return [jnp.where(self.layer_low, fill, piece) for piece in value]

    def no_high(self, value, fill):
        return [jnp.where(self.layer_high, fill, piece) for piece in value]


class Flat:
    def __init__(self, ref, layers):
        self.ref, self.layers, self.parts = ref, layers, ref.shape[0]

    def put_layer(self, place, rows, value):
        for p in range(self.parts):
            self.ref.at[p][pl.ds(place, rows, stride=self.layers), :] = value[
                :, p * LANES : (p + 1) * LANES
            ]

    def get_layer(self, place, rows):
        pieces = [
            self.ref.at[p][pl.ds(place, rows, stride=self.layers), :] for p in range(self.parts)
        ]
        return jnp.concatenate(pieces, axis=1)

    def span(self, row, size):
        return pl.ds(pl.multiple_of(row * self.layers, self.layers), size * self.layers)

    def get(self, row, size):
        return [
            self.ref[p, self.span(row, size), :].reshape(size, self.layers, LANES)
            for p in range(self.parts)
        ]

    def put(self, row, size, value):
        for p in range(self.parts):
            self.ref[p, self.span(row, size), :] = value[p].reshape(size * self.layers, LANES)


def root_of(value):
    value = jnp.maximum(value, 1e-30)
    return value * lax.rsqrt(value)


def distance(layers, at, y, grid_rows, size, row, piece):
    shape = (size, layers, LANES)
    dx = (lax.broadcasted_iota(jnp.int32, shape, 1) - at[0]).astype(jnp.float32)
    dz = (lax.broadcasted_iota(jnp.int32, shape, 2) + (piece * LANES - at[2])).astype(jnp.float32)
    here = lax.broadcasted_iota(jnp.int32, shape, 0) + (y + row)
    dy = (here - at[1]).astype(jnp.float32)
    far = jnp.sqrt(dx * dx + dy * dy + dz * dz)
    return jnp.where((here >= 0) & (here < grid_rows), far, BIG)


def local_solve(near_x, near_y, near_z, cost, twice, one_half):
    small = jnp.minimum(near_x, near_y)
    large = jnp.maximum(near_x, near_y)
    lowest = jnp.minimum(small, near_z)
    highest = jnp.maximum(large, near_z)
    middle = jnp.maximum(small, jnp.minimum(large, near_z))
    first_gap = middle - lowest
    second_gap = highest - lowest
    square = first_gap * first_gap
    single = lowest + cost
    double = lowest + 0.5 * (first_gap + root_of(twice - square))
    rest = square + second_gap * (second_gap - first_gap)
    root = root_of(one_half - rest)
    triple = lowest + ((first_gap + second_gap) * (1.0 / 3.0) + root * (math.sqrt(2.0) / 3.0))
    return jnp.where(single <= middle, single, jnp.where(double <= highest, double, triple))


SWEEP_ROWS = 4
SWEEP_UNROLL = 2


def sweep_kernel(layers, own_rows, slots, chips, scal, *refs):
    rows = own_rows + 2 * HALO
    depth = refs[0].shape[-1]
    parts = depth // LANES
    vel_in, refs = refs[:chips], refs[chips:]
    times_out, final, speed, refs = refs[0], refs[1], refs[2], refs[3:]
    cost, twice, one_half, ping, pong, acts, mask, flat = refs
    flat = Flat(flat, layers)
    line, chip, core, y_first, grid_rows = scal[4], scal[1], scal[2], scal[3], scal[5]
    stations = [[scal[6 + 3 * slot + i] for i in range(3)] for slot in range(slots)]

    for j in range(chips):
        for c in range(2):
            place = (chip ^ j) * 2 + (core ^ c)
            flat.put_layer(place, rows, vel_in[j][c * rows : (c + 1) * rows, :])
            for slot in range(slots):
                for part in range(ROUNDS):
                    row = 2 * rows + slot * ROUNDS + part
                    acts[slot * ROUNDS + part, pl.ds(place, 1), :] = vel_in[j][
                        row : row + 1, c * LANES : (c + 1) * LANES
                    ]

    def prepare(row, size):
        value = flat.get(row, size)
        slow = each(lambda v: 1.0 / v, value)
        put(speed, row, size, value)
        put(cost, row, size, slow)
        put(twice, row, size, each(lambda f: 2.0 * (f * f), slow))
        put(one_half, row, size, each(lambda f: 1.5 * (f * f), slow))

    loop(0, rows, 4, prepare)

    def fill(row, size):
        for slot in range(slots):
            value = [
                distance(layers, stations[slot], y_first - 1, grid_rows, size, row, piece)
                for piece in range(parts)
            ]
            put(ping, row, size, value, slot)

    loop(0, rows + 2, 2, fill)

    lane_iota = lax.broadcasted_iota(jnp.int32, (layers, LANES), 1)
    tile_first = (y_first + TY) // TY - 1
    tile_span = (rows + TY - 2) // TY + 1
    for slot in range(slots):
        for part in range(ROUNDS):
            act = acts[slot * ROUNDS + part]
            columns = []
            for t in range(tile_span):
                here = lane_iota == tile_first + t
                picked = jnp.sum(jnp.where(here, act, 0.0), axis=1, keepdims=True)
                columns.append(jnp.broadcast_to(picked, (layers, LANES)))
            for i in range(rows):
                value = columns[0]
                for t in range(1, tile_span):
                    value = jnp.where(y_first + i >= (tile_first + t) * TY, columns[t], value)
                mask[slot, part, i] = value

    def sweep(source, target, low, high, part, shift):
        def body(row, size):
            grid = Grid(size, layers, depth)
            costs = get(cost, row, size), get(twice, row, size), get(one_half, row, size)
            for slot in range(slots):
                field = get(source, row, size + 2, slot)
                here = each(lambda f: f[1 : size + 1], field)
                near_y = each(lambda f: jnp.minimum(f[:size], f[2:]), field)
                near_x = each(
                    jnp.minimum,
                    grid.no_low(grid.layer_before(here), BIG),
                    grid.no_high(grid.layer_after(here), BIG),
                )
                near_z = each(
                    jnp.minimum, grid.depth_before(here, BIG), grid.depth_after(here, BIG)
                )
                update = each(local_solve, near_x, near_y, near_z, *costs)
                on = mask[slot, part, pl.ds(row, size)] > 0.0
                put(
                    target,
                    row + shift,
                    size,
                    each(lambda u, h: jnp.where(on, u, h), update, here),
                    slot,
                )

        loop(low, high, SWEEP_ROWS, body, SWEEP_UNROLL)
        for slot in range(slots):
            at_x, at_y, at_z = stations[slot]
            local = at_y - y_first

            @pl.when((local >= low) & (local < high))
            def _():
                shape = (1, layers, depth)
                there = (lax.broadcasted_iota(jnp.int32, shape, 1) == at_x) & (
                    lax.broadcasted_iota(jnp.int32, shape, 2) == at_z
                )
                here = slot, pl.ds(local + shift, 1)
                target[here] = jnp.where(there, 0.0, target[here])

    fields = [ping, pong]
    last = ROUNDS * SWEEPS - 1
    for index in range(last):
        sweep(fields[index % 2], fields[(index + 1) % 2], index, rows - index, index // SWEEPS, 1)
    sweep(fields[last % 2], final, last, rows - last, last // SWEEPS, -last)

    for slot in range(slots):
        loop(0, own_rows, 4, lambda row, size: flat.put(row, size, get(final, row + ADJ_HALO, size, slot)))
        for place in range(layers):
            times_out[line ^ slot, place] = flat.get_layer(place, own_rows)


ADJ_ROWS = 4
ADJ_UNROLL = 2


def adjoint_kernel(layers, own_rows, slots, scal, final, speed, count, delay_sum, *refs):
    depth = final.shape[-1]
    parts = depth // LANES
    kernel_out, refs = refs[:layers], refs[layers:]
    weight, src, adj_a, adj_b, density, flat = refs
    together = weight.shape[0]
    flat = Flat(flat, layers)
    y_first, grid_rows = scal[3], scal[5]
    stations = [[scal[6 + 3 * slot + i] for i in range(3)] for slot in range(slots)]
    shift = HALO - ADJ_HALO
    rows = own_rows + 2 * ADJ_HALO

    def sums(ref, row, size, *lead):
        span = pl.ds(pl.multiple_of(row * layers, layers), size * layers)
        return [
            ref[(*lead, span, slice(p * LANES, (p + 1) * LANES))].reshape(size, layers, LANES)
            for p in range(parts)
        ]

    def make_source(group, row, size):
        number = sums(count, row, size)
        for slot in group:
            straight = [
                distance(layers, stations[slot], y_first + shift, grid_rows, size, row, piece)
                for piece in range(parts)
            ]
            value = each(
                lambda n, t, d, s: n * (t - d) - s,
                number,
                get(final, row, size, slot),
                straight,
                sums(delay_sum, row, size, slot),
            )
            put(src, row, size, value, slot - group[0])

    def make_weight(group, row, size):
        grid = Grid(size, layers, depth)
        scale = each(lambda v: v * (1.0 / 6.0), get(speed, row + shift, size))
        for slot in group:
            field = get(final, row - 1, size + 2, slot)
            here = each(lambda f: f[1 : size + 1], field)

            def rise(value):
                return each(lambda v, h, s: jnp.maximum(v - h, 0.0) * s, value, here, scale)

            def keep(value, piece, edge):
                return [jnp.where(edge, 0.0, v) if p == piece else v for p, v in enumerate(value)]

            six = [
                grid.no_low(rise(grid.layer_before(here)), 0.0),
                grid.no_high(rise(grid.layer_after(here)), 0.0),
                rise(each(lambda f: f[:size], field)),
                rise(each(lambda f: f[2:], field)),
                keep(rise(grid.depth_before(here)), 0, grid.lane_low),
                keep(rise(grid.depth_after(here)), parts - 1, grid.lane_high),
            ]
            for n, value in enumerate(six):
                put(weight, row, size, value, slot - group[0], n)

    def multiply_add(value, factor, neighbour):
        return value + factor * neighbour

    def smooth(low, here, high):
        return (low + 2.0 * here + high) * 0.25

    def sweep(group, source, target, low, high):
        def body(row, size):
            grid = Grid(size, layers, depth)
            total = None if group[0] == 0 else get(density, row, size)
            for slot in range(len(group)):
                field = get(source, row - 1, size + 2, slot)
                here = each(lambda f: f[1 : size + 1], field)
                around = [
                    grid.layer_before(here),
                    grid.layer_after(here),
                    each(lambda f: f[:size], field),
                    each(lambda f: f[2:], field),
                    grid.depth_before(here),
                    grid.depth_after(here),
                ]
                value = get(src, row, size, slot)
                for n, neighbour in enumerate(around):
                    value = each(multiply_add, value, get(weight, row, size, slot, n), neighbour)
                if target is not None:
                    put(target, row, size, value, slot)
                else:
                    total = value if total is None else each(jnp.add, total, value)
            if target is None:
                if group[-1] == slots - 1:
                    value = each(lambda t, v: t / v, total, get(speed, row + shift, size))
                    low = grid.no_low(grid.layer_before(value), 0.0)
                    high = grid.no_high(grid.layer_after(value), 0.0)
                    total = each(smooth, low, value, high)
                put(density, row, size, total)

        loop(low, high, ADJ_ROWS, body, ADJ_UNROLL)

    for first in range(0, slots, together):
        group = range(first, min(first + together, slots))
        loop(0, rows, 2, functools.partial(make_source, group))
        loop(1, rows - 1, 2, functools.partial(make_weight, group))
        fields = [src] + [(adj_a, adj_b)[i % 2] for i in range(ADJ_SWEEPS - 1)] + [None]
        for index in range(ADJ_SWEEPS):
            sweep(group, fields[index], fields[index + 1], index + 1, rows - 1 - index)

    def finish(row, size):
        grid = Grid(size, layers, depth)
        field = get(density, row + ADJ_SWEEPS, size + 2)
        value = each(lambda f: smooth(f[:size], f[1 : size + 1], f[2:]), field)
        low, high = grid.depth_before(value, 0.0), grid.depth_after(value, 0.0)
        flat.put(row, size, each(smooth, low, value, high))

    loop(0, own_rows, 4, finish)
    for m, out in enumerate(kernel_out):
        out[...] = flat.get_layer(scal[1] * 2 + scal[2] ^ m, own_rows)


def join_kernel(scal, *refs):
    blocks, out = refs[:-1], refs[-1]
    rows = blocks[0].shape[0]
    for m, block in enumerate(blocks):
        out[0, pl.ds(pl.multiple_of(((scal[1] * 2 + scal[2]) ^ m) * rows, rows), rows), :] = block[...]


def per_device(velocity, station_cells, event_cells, delays, active):
    _, grid_rows, depth = velocity.shape
    slots, layers = lax.axis_size("src"), lax.axis_size("space")
    chips = layers // 2
    events = event_cells.shape[1]
    line_rows = grid_rows // slots
    own_rows = line_rows // layers
    rows = own_rows + 2 * HALO
    adj_rows = own_rows + 2 * ADJ_HALO
    line, place = lax.axis_index("src"), lax.axis_index("space")
    chip, core = place // 2, place % 2

    def to_line(array, j):
        return lax.ppermute(array, "src", [(i, i ^ j) for i in range(slots)])

    def to_chip(array, j):
        return lax.ppermute(array, "space", [(i, i ^ (2 * j)) for i in range(layers)])

    def to_core(array):
        return lax.ppermute(array, "space", [(i, i ^ 1) for i in range(layers)])

    f32 = jnp.float32
    def out(*shape):
        return jax.ShapeDtypeStruct(shape, f32)

    def scratch(*shape):
        return pltpu.VMEM(shape, f32)

    def field(*lead):
        return (*lead, layers, depth)

    y_first = line * line_rows + place * own_rows - HALO
    here = jnp.stack([line * line_rows, chip, core, y_first, line, jnp.int32(grid_rows)])
    here = here.astype(jnp.int32)

    other = to_core(velocity[0])
    active_other = to_core(active[:, 0])
    (payload,) = call(
        head_kernel,
        "head",
        [out(1, events + LANES * (1 + 2 * ROUNDS))],
        [delays, station_cells, active[:, 0], active_other],
    )
    pays = [payload] + [to_line(payload, j) for j in range(1, slots)]

    height = 2 * rows + -(-slots * ROUNDS // 8) * 8
    packed = call(
        functools.partial(pack_kernel, rows, own_rows, slots),
        "pack",
        [out(height, depth)] * chips,
        [here, velocity[0], other, *pays],
    )
    vel = [packed[0]] + [to_chip(packed[j], j) for j in range(1, chips)]

    pays, cells, _ = lax.optimization_barrier((pays, event_cells, packed[0]))
    stations = jnp.concatenate([p[0, events : events + 3] for p in pays]).astype(jnp.int32)
    scal = jnp.concatenate([here, stations])
    count, delay_sum = call(
        functools.partial(scatter_kernel, layers, events),
        "events",
        [out(adj_rows * layers, depth), out(slots, adj_rows * layers, depth)],
        [here, cells, *pays],
        microseconds=4.0,
    )

    scal, count, delay_sum = lax.optimization_barrier((scal, count, delay_sum))

    together = min(slots, 4)
    flat = scratch(depth // LANES, rows * layers, LANES)
    times, final, speed = call(
        functools.partial(sweep_kernel, layers, own_rows, slots, chips),
        "sweeps",
        [
            out(slots, layers, own_rows, depth),
            out(*field(slots, adj_rows)),
            out(*field(rows)),
        ],
        [scal, *vel],
        [
            scratch(*field(rows)),
            scratch(*field(rows)),
            scratch(*field(rows)),
            scratch(*field(slots, rows + 2)),
            scratch(*field(slots, rows + 2)),
            scratch(slots * ROUNDS, layers, LANES),
            scratch(slots, ROUNDS, rows, layers, LANES),
            flat,
        ],
        microseconds=10.0,
    )
    kernel = call(
        functools.partial(adjoint_kernel, layers, own_rows, slots),
        "adjoint",
        [out(own_rows, depth)] * layers,
        [scal, final, speed, count, delay_sum],
        [
            scratch(*field(together, 6, adj_rows)),
            scratch(*field(together, adj_rows)),
            scratch(*field(together, adj_rows)),
            scratch(*field(together, adj_rows)),
            scratch(*field(adj_rows)),
            flat,
        ],
        microseconds=7.0,
    )

    times = lax.all_to_all(
        times.reshape(slots * layers, own_rows, depth), ("src", "space"), 0, 0, tiled=True
    )
    blocks = [kernel[0]] + [
        lax.ppermute(kernel[m], "space", [(i, i ^ m) for i in range(layers)])
        for m in range(1, layers)
    ]
    (kernel,) = call(join_kernel, "join", [out(1, line_rows, depth)], [here, *blocks])
    return (times.reshape(1, 1, grid_rows, depth), kernel)


def solution(mesh):
    return jax.shard_map(
        per_device,
        mesh=mesh,
        in_specs=(
            P("space", None, None),
            P("src", None),
            P(),
            P("src", None),
            P(None, "src", "space", None),
        ),
        out_specs=(P("src", "space", None, None), P("space", "src", None)),
        check_vma=False,
    )
```

```python
import functools
import math

import jax
import jax.numpy as jnp
from jax import lax
from jax.experimental import pallas as pl
from jax.experimental.pallas import tpu as pltpu
from jax.sharding import PartitionSpec as P

TY = 32
ROUNDS = 2
SWEEPS = 2
ADJ_SWEEPS = 4
BIG = 1000000.0
LANES = 128

HALO = ROUNDS * SWEEPS + ADJ_SWEEPS
ADJ_HALO = ADJ_SWEEPS + 1

VMEM = pltpu.VMEM
SMEM = pltpu.SMEM


def spec(space):
    return pl.BlockSpec(memory_space=space)


def call(body, name, outs, operands, scratch=(), microseconds=1.0, in_place=(), hbm_in=(), hbm_out=()):
    held = [a for a in (*operands, *outs, *scratch) if len(a.shape) > 1]
    limit = 4 * 2**20 + sum(4 * math.prod((*a.shape[:-2], -(-math.prod(a.shape[-2:-1]) // 8) * 8, max(a.shape[-1], 128))) for a in held)
    return pl.pallas_call(
        body,
        out_shape=list(outs),
        in_specs=[
            spec(
                pltpu.HBM if i in hbm_in else pl.ANY if i in in_place else SMEM if a.ndim == 1 else VMEM
            )
            for i, a in enumerate(operands)
        ],
        out_specs=[spec(pltpu.HBM if i in hbm_out else VMEM) for i in range(len(outs))],
        scratch_shapes=list(scratch),
        compiler_params=pltpu.CompilerParams(vmem_limit_bytes=limit),
        cost_estimate=pl.CostEstimate(
            flops=0, bytes_accessed=int(microseconds * 3.5e6), transcendentals=0
        ),
        name=name,
    )(*[
        pltpu.with_memory_space_constraint(a, pltpu.HBM) if i in hbm_in else a
        for i, a in enumerate(operands)
    ])


def head_kernel(delays, velocity, station, active, active_other, out, layer, sems):
    events = delays.shape[1]
    copies = [
        pltpu.make_async_copy(delays, out.at[:, pl.ds(0, events)], sems.at[0]),
        pltpu.make_async_copy(velocity, layer, sems.at[1]),
    ]
    for copy in copies:
        copy.start()
    out[:, events:] = jnp.zeros((1, out.shape[1] - events), jnp.float32)
    at = events
    out[:, at : at + 3] = station[...].astype(jnp.float32)
    for source in (active, active_other):
        for part in range(ROUNDS):
            at += LANES
            out[:, at : at + source.shape[-1]] = source[part].astype(jnp.float32)
    for copy in copies:
        copy.wait()


def pack_kernel(rows, own_rows, slots, scal, own, other, *refs):
    line_row, chip, core = scal[0], scal[1], scal[2]
    pays, outs = refs[:slots], refs[slots:]
    total = own.shape[0]
    chunk = math.gcd(own_rows, 8)
    at = pays[0].shape[1] - 2 * ROUNDS * LANES
    for j, out in enumerate(outs):
        first = line_row + ((chip ^ j) * 2 + core) * own_rows - HALO
        for piece in range(rows // chunk):
            start = jnp.clip(first + piece * chunk, 0, total - chunk)
            start = pl.multiple_of(start, chunk)
            out[piece * chunk : (piece + 1) * chunk, :] = own[pl.ds(start, chunk), :]
            out[rows + piece * chunk : rows + (piece + 1) * chunk, :] = other[pl.ds(start, chunk), :]
        out[2 * rows :, :] = jnp.zeros_like(out[2 * rows :, :])
        for slot, pay in enumerate(pays):
            for part in range(ROUNDS):
                row = 2 * rows + slot * ROUNDS + part
                for c in range(2):
                    tile = at + (c * ROUNDS + part) * LANES
                    out[row : row + 1, c * LANES : (c + 1) * LANES] = pay[:, tile : tile + LANES]


EVENT_CHUNK = 2048


def scatter_kernel(layers, events, scal, cells, *refs):
    slots = len(refs) - 3
    pays, count, delay_sum, left = refs[:slots], refs[slots], refs[slots + 1], refs[slots + 2]
    first_row = scal[3] + HALO - ADJ_HALO
    height, width = count.shape
    chunk = left.shape[1]
    steps = events // chunk
    contract = (((1,), (1,)), ((), ()))

    def step(index, carry):
        start = pl.multiple_of(index * chunk, chunk)
        where_x = cells[0:1, pl.ds(start, chunk)]
        where_y = cells[1:2, pl.ds(start, chunk)] - first_row
        where_z = cells[2:3, pl.ds(start, chunk)]
        at = jnp.where(where_y >= 0, where_y * layers + where_x, -1)
        hit = lax.broadcasted_iota(jnp.int32, (height, chunk), 0) == at
        hit = hit.astype(jnp.bfloat16)
        left[:height, :] = hit
        for slot in range(slots):
            delay = pays[slot][:, pl.ds(start, chunk)]
            high = delay.astype(jnp.bfloat16)
            low = (delay - high.astype(jnp.float32)).astype(jnp.bfloat16)
            for half, factor in enumerate((high, low)):
                row = (1 + 2 * slot + half) * height
                left[row : row + height, :] = hit * factor
        depth = lax.broadcasted_iota(jnp.int32, (width, chunk), 0) == where_z
        depth = depth.astype(jnp.bfloat16)
        value = lax.dot_general(left[...], depth, contract, preferred_element_type=jnp.float32)
        pieces = [value[i * height : (i + 1) * height] for i in range(1 + 2 * slots)]
        sums = [pieces[1 + 2 * slot] + pieces[2 + 2 * slot] for slot in range(slots)]
        if steps == 1:
            count[...] = pieces[0]
            for slot in range(slots):
                delay_sum[slot] = sums[slot]
        else:
            count[...] += pieces[0]
            for slot in range(slots):
                delay_sum[slot] += sums[slot]
        return carry

    if steps == 1:
        step(0, 0)
    else:
        count[...] = jnp.zeros_like(count)
        delay_sum[...] = jnp.zeros_like(delay_sum)
        lax.fori_loop(0, steps, step, 0)


def get(ref, row, size, *lead):
    index = (*lead, pl.ds(row, size))
    return [
        ref[(*index, slice(None), slice(p, p + LANES))] for p in range(0, ref.shape[-1], LANES)
    ]


def put(ref, row, size, value, *lead):
    index = (*lead, pl.ds(row, size))
    for p, piece in enumerate(value):
        ref[(*index, slice(None), slice(p * LANES, (p + 1) * LANES))] = piece


def each(function, *values):
    return [function(*pieces) for pieces in zip(*values)]


def loop(low, high, size, body, unroll=1):
    steps = (high - low) // size
    if steps:
        lax.fori_loop(
            0,
            steps,
            lambda i, carry: (body(low + i * size, size), carry)[1],
            0,
            unroll=min(unroll, steps),
        )
    if low + steps * size < high:
        loop(low + steps * size, high, max(size // 2, 1), body)


class Grid:
    def __init__(self, size, layers, depth):
        shape = (size, layers, LANES)
        layer = lax.broadcasted_iota(jnp.int32, shape, 1)
        lane = lax.broadcasted_iota(jnp.int32, shape, 2)
        self.layers = layers
        self.layer_low, self.layer_high = layer == 0, layer == layers - 1
        self.lane_low, self.lane_high = lane == 0, lane == LANES - 1

    def layer_before(self, value):
        return [pltpu.roll(piece, 1, 1) for piece in value]

    def layer_after(self, value):
        return [pltpu.roll(piece, self.layers - 1, 1) for piece in value]

    def depth_before(self, value, fill=None):
        moved = [pltpu.roll(piece, 1, 2) for piece in value]
        first = moved[0] if fill is None else jnp.where(self.lane_low, fill, moved[0])
        rest = [
            jnp.where(self.lane_low, low, here) for low, here in zip(moved[:-1], moved[1:])
        ]
        return [first] + rest

    def depth_after(self, value, fill=None):
        moved = [pltpu.roll(piece, LANES - 1, 2) for piece in value]
        last = moved[-1] if fill is None else jnp.where(self.lane_high, fill, moved[-1])
        rest = [
            jnp.where(self.lane_high, high, here) for here, high in zip(moved[:-1], moved[1:])
        ]
        return rest + [last]

    def no_low(self, value, fill):
        return [jnp.where(self.layer_low, fill, piece) for piece in value]

    def no_high(self, value, fill):
        return [jnp.where(self.layer_high, fill, piece) for piece in value]


class Flat:
    def __init__(self, ref, layers):
        self.ref, self.layers, self.parts = ref, layers, ref.shape[0]

    def put_layer(self, place, rows, value):
        for p in range(self.parts):
            self.ref.at[p][pl.ds(place, rows, stride=self.layers), :] = value[
                :, p * LANES : (p + 1) * LANES
            ]

    def get_layer(self, place, rows):
        pieces = [
            self.ref.at[p][pl.ds(place, rows, stride=self.layers), :] for p in range(self.parts)
        ]
        return jnp.concatenate(pieces, axis=1)

    def span(self, row, size):
        return pl.ds(pl.multiple_of(row * self.layers, self.layers), size * self.layers)

    def get(self, row, size):
        return [
            self.ref[p, self.span(row, size), :].reshape(size, self.layers, LANES)
            for p in range(self.parts)
        ]

    def put(self, row, size, value):
        for p in range(self.parts):
            self.ref[p, self.span(row, size), :] = value[p].reshape(size * self.layers, LANES)


def root_of(value):
    value = jnp.maximum(value, 1e-30)
    return value * lax.rsqrt(value)


class Straight:
    def __init__(self, layers, parts, at, grid_rows):
        shape = (1, layers, LANES)
        self.at_y, self.grid_rows = at[1], grid_rows
        dx = (lax.broadcasted_iota(jnp.int32, shape, 1) - at[0]).astype(jnp.float32)
        self.across = []
        for p in range(parts):
            dz = lax.broadcasted_iota(jnp.int32, shape, 2) + (p * LANES - at[2])
            dz = dz.astype(jnp.float32)
            self.across.append(dx * dx + dz * dz)

    def row(self, y):
        gap = y - self.at_y
        far = (gap * gap).astype(jnp.float32)
        inside = (y >= 0) & (y < self.grid_rows)
        return [jnp.where(inside, root_of(a + far), BIG) for a in self.across]


def local_solve(near_x, near_y, near_z, cost, twice, one_half):
    small = jnp.minimum(near_x, near_y)
    large = jnp.maximum(near_x, near_y)
    lowest = jnp.minimum(small, near_z)
    highest = jnp.maximum(large, near_z)
    middle = jnp.maximum(small, jnp.minimum(large, near_z))
    first_gap = middle - lowest
    second_gap = highest - lowest
    square = first_gap * first_gap
    single = lowest + cost
    double = lowest + 0.5 * (first_gap + root_of(twice - square))
    rest = square + second_gap * (second_gap - first_gap)
    root = root_of(one_half - rest)
    triple = lowest + ((first_gap + second_gap) * (1.0 / 3.0) + root * (math.sqrt(2.0) / 3.0))
    return jnp.where(single <= middle, single, jnp.where(double <= highest, double, triple))


SWEEP_ROWS = 4
SWEEP_UNROLL = 2


def sweep_kernel(layers, own_rows, slots, chips, scal, *refs):
    rows = own_rows + 2 * HALO
    depth = refs[0].shape[-1]
    parts = depth // LANES
    vel_in, refs = refs[:chips], refs[chips:]
    times_out, final, speed, refs = refs[0], refs[1], refs[2], refs[3:]
    cost, twice, one_half, ping, pong, acts, mask, flat = refs
    flat = Flat(flat, layers)
    line, chip, core, y_first, grid_rows = scal[4], scal[1], scal[2], scal[3], scal[5]
    stations = [[scal[6 + 3 * slot + i] for i in range(3)] for slot in range(slots)]

    for j in range(chips):
        for c in range(2):
            place = (chip ^ j) * 2 + (core ^ c)
            flat.put_layer(place, rows, vel_in[j][c * rows : (c + 1) * rows, :])
            for slot in range(slots):
                for part in range(ROUNDS):
                    row = 2 * rows + slot * ROUNDS + part
                    acts[slot * ROUNDS + part, pl.ds(place, 1), :] = vel_in[j][
                        row : row + 1, c * LANES : (c + 1) * LANES
                    ]

    def prepare(row, size):
        value = flat.get(row, size)
        slow = each(lambda v: 1.0 / v, value)
        put(speed, row, size, value)
        put(cost, row, size, slow)
        put(twice, row, size, each(lambda f: 2.0 * (f * f), slow))
        put(one_half, row, size, each(lambda f: 1.5 * (f * f), slow))

    loop(0, rows, 4, prepare)

    straight = [Straight(layers, parts, stations[slot], grid_rows) for slot in range(slots)]

    def fill(row, size):
        for i in range(size):
            for slot in range(slots):
                put(ping, row + i, 1, straight[slot].row(y_first - 1 + row + i), slot)

    loop(0, rows + 2, 4, fill)

    lane_iota = lax.broadcasted_iota(jnp.int32, (layers, LANES), 1)
    tile_first = (y_first + TY) // TY - 1
    tile_span = (rows + TY - 2) // TY + 1
    for slot in range(slots):
        for part in range(ROUNDS):
            act = acts[slot * ROUNDS + part]
            columns = []
            for t in range(tile_span):
                here = lane_iota == tile_first + t
                picked = jnp.sum(jnp.where(here, act, 0.0), axis=1, keepdims=True)
                columns.append(jnp.broadcast_to(picked, (layers, LANES)))
            for i in range(rows):
                value = columns[0]
                for t in range(1, tile_span):
                    value = jnp.where(y_first + i >= (tile_first + t) * TY, columns[t], value)
                mask[slot, part, i] = value

    def sweep(source, target, low, high, part, shift):
        def body(row, size):
            grid = Grid(size, layers, depth)
            costs = get(cost, row, size), get(twice, row, size), get(one_half, row, size)
            for slot in range(slots):
                field = get(source, row, size + 2, slot)
                here = each(lambda f: f[1 : size + 1], field)
                near_y = each(lambda f: jnp.minimum(f[:size], f[2:]), field)
                near_x = each(
                    jnp.minimum,
                    grid.no_low(grid.layer_before(here), BIG),
                    grid.no_high(grid.layer_after(here), BIG),
                )
                near_z = each(
                    jnp.minimum, grid.depth_before(here, BIG), grid.depth_after(here, BIG)
                )
                update = each(local_solve, near_x, near_y, near_z, *costs)
                on = mask[slot, part, pl.ds(row, size)] > 0.0
                put(
                    target,
                    row + shift,
                    size,
                    each(lambda u, h: jnp.where(on, u, h), update, here),
                    slot,
                )

        loop(low, high, SWEEP_ROWS, body, SWEEP_UNROLL)
        for slot in range(slots):
            at_x, at_y, at_z = stations[slot]
            local = at_y - y_first

            @pl.when((local >= low) & (local < high))
            def _():
                shape = (1, layers, depth)
                there = (lax.broadcasted_iota(jnp.int32, shape, 1) == at_x) & (
                    lax.broadcasted_iota(jnp.int32, shape, 2) == at_z
                )
                here = slot, pl.ds(local + shift, 1)
                target[here] = jnp.where(there, 0.0, target[here])

    fields = [ping, pong]
    last = ROUNDS * SWEEPS - 1
    for index in range(last):
        sweep(fields[index % 2], fields[(index + 1) % 2], index, rows - index, index // SWEEPS, 1)
    sweep(fields[last % 2], final, last, rows - last, last // SWEEPS, -last)

    for slot in range(slots):
        loop(0, own_rows, 4, lambda row, size: flat.put(row, size, get(final, row + ADJ_HALO, size, slot)))
        for place in range(layers):
            times_out[line ^ slot, place] = flat.get_layer(place, own_rows)


ADJ_ROWS = 4
ADJ_UNROLL = 2


def adjoint_kernel(layers, own_rows, slots, scal, final, speed, count, delay_sum, *refs):
    depth = final.shape[-1]
    parts = depth // LANES
    kernel_out, refs = refs[:layers], refs[layers:]
    weight, src, adj_a, adj_b, density, flat = refs
    together = weight.shape[0]
    flat = Flat(flat, layers)
    y_first, grid_rows = scal[3], scal[5]
    stations = [[scal[6 + 3 * slot + i] for i in range(3)] for slot in range(slots)]
    straight = [Straight(layers, parts, stations[slot], grid_rows) for slot in range(slots)]
    shift = HALO - ADJ_HALO
    rows = own_rows + 2 * ADJ_HALO

    def sums(ref, row, size, *lead):
        span = pl.ds(pl.multiple_of(row * layers, layers), size * layers)
        return [
            ref[(*lead, span, slice(p * LANES, (p + 1) * LANES))].reshape(size, layers, LANES)
            for p in range(parts)
        ]

    def make_source(group, row, size):
        for i in range(size):
            number = sums(count, row + i, 1)
            for slot in group:
                value = each(
                    lambda n, t, d, s: n * (t - d) - s,
                    number,
                    get(final, row + i, 1, slot),
                    straight[slot].row(y_first + shift + row + i),
                    sums(delay_sum, row + i, 1, slot),
                )
                put(src, row + i, 1, value, slot - group[0])

    def make_weight(group, row, size):
        grid = Grid(size, layers, depth)
        scale = each(lambda v: v * (1.0 / 6.0), get(speed, row + shift, size))
        for slot in group:
            field = get(final, row - 1, size + 2, slot)
            here = each(lambda f: f[1 : size + 1], field)

            def rise(value):
                return each(lambda v, h, s: jnp.maximum(v - h, 0.0) * s, value, here, scale)

            def keep(value, piece, edge):
                return [jnp.where(edge, 0.0, v) if p == piece else v for p, v in enumerate(value)]

            six = [
                grid.no_low(rise(grid.layer_before(here)), 0.0),
                grid.no_high(rise(grid.layer_after(here)), 0.0),
                rise(each(lambda f: f[:size], field)),
                rise(each(lambda f: f[2:], field)),
                keep(rise(grid.depth_before(here)), 0, grid.lane_low),
                keep(rise(grid.depth_after(here)), parts - 1, grid.lane_high),
            ]
            for n, value in enumerate(six):
                put(weight, row, size, value, slot - group[0], n)

    def multiply_add(value, factor, neighbour):
        return value + factor * neighbour

    def smooth(low, here, high):
        return (low + 2.0 * here + high) * 0.25

    def sweep(group, source, target, low, high):
        def body(row, size):
            grid = Grid(size, layers, depth)
            total = None if group[0] == 0 else get(density, row, size)
            for slot in range(len(group)):
                field = get(source, row - 1, size + 2, slot)
                here = each(lambda f: f[1 : size + 1], field)
                around = [
                    grid.layer_before(here),
                    grid.layer_after(here),
                    each(lambda f: f[:size], field),
                    each(lambda f: f[2:], field),
                    grid.depth_before(here),
                    grid.depth_after(here),
                ]
                value = get(src, row, size, slot)
                for n, neighbour in enumerate(around):
                    value = each(multiply_add, value, get(weight, row, size, slot, n), neighbour)
                if target is not None:
                    put(target, row, size, value, slot)
                else:
                    total = value if total is None else each(jnp.add, total, value)
            if target is None:
                if group[-1] == slots - 1:
                    value = each(lambda t, v: t / v, total, get(speed, row + shift, size))
                    low = grid.no_low(grid.layer_before(value), 0.0)
                    high = grid.no_high(grid.layer_after(value), 0.0)
                    total = each(smooth, low, value, high)
                put(density, row, size, total)

        loop(low, high, ADJ_ROWS, body, ADJ_UNROLL)

    for first in range(0, slots, together):
        group = range(first, min(first + together, slots))
        loop(0, rows, 4, functools.partial(make_source, group))
        loop(1, rows - 1, 2, functools.partial(make_weight, group))
        fields = [src] + [(adj_a, adj_b)[i % 2] for i in range(ADJ_SWEEPS - 1)] + [None]
        for index in range(ADJ_SWEEPS):
            sweep(group, fields[index], fields[index + 1], index + 1, rows - 1 - index)

    def finish(row, size):
        grid = Grid(size, layers, depth)
        field = get(density, row + ADJ_SWEEPS, size + 2)
        value = each(lambda f: smooth(f[:size], f[1 : size + 1], f[2:]), field)
        low, high = grid.depth_before(value, 0.0), grid.depth_after(value, 0.0)
        flat.put(row, size, each(smooth, low, value, high))

    loop(0, own_rows, 4, finish)
    for m, out in enumerate(kernel_out):
        out[...] = flat.get_layer(scal[1] * 2 + scal[2] ^ m, own_rows)


def join_kernel(scal, times, *refs):
    blocks, (times_out, out, sems) = refs[:-3], refs[-3:]
    rows = blocks[0].shape[0]
    copies = [pltpu.make_async_copy(times, times_out, sems.at[0])]
    for m, block in enumerate(blocks):
        start = pl.multiple_of(((scal[1] * 2 + scal[2]) ^ m) * rows, rows)
        copies.append(pltpu.make_async_copy(block, out.at[pl.ds(start, rows)], sems.at[m + 1]))
    for copy in copies:
        copy.start()
    for copy in copies:
        copy.wait()


def per_device(velocity, station_cells, event_cells, delays, active):
    _, grid_rows, depth = velocity.shape
    slots, layers = lax.axis_size("src"), lax.axis_size("space")
    chips = layers // 2
    events = event_cells.shape[1]
    line_rows = grid_rows // slots
    own_rows = line_rows // layers
    rows = own_rows + 2 * HALO
    adj_rows = own_rows + 2 * ADJ_HALO
    line, place = lax.axis_index("src"), lax.axis_index("space")
    chip, core = place // 2, place % 2

    def to_line(array, j):
        return lax.ppermute(array, "src", [(i, i ^ j) for i in range(slots)])

    def to_chip(array, j):
        return lax.ppermute(array, "space", [(i, i ^ (2 * j)) for i in range(layers)])

    def to_core(array):
        return lax.ppermute(array, "space", [(i, i ^ 1) for i in range(layers)])

    f32 = jnp.float32
    def out(*shape):
        return jax.ShapeDtypeStruct(shape, f32)

    def scratch(*shape):
        return pltpu.VMEM(shape, f32)

    def field(*lead):
        return (*lead, layers, depth)

    y_first = line * line_rows + place * own_rows - HALO
    here = jnp.stack([line * line_rows, chip, core, y_first, line, jnp.int32(grid_rows)])
    here = here.astype(jnp.int32)

    other = to_core(velocity[0])
    active_other = to_core(active[:, 0])
    payload, layer = call(
        head_kernel,
        "head",
        [out(1, events + LANES * (1 + 2 * ROUNDS)), out(grid_rows, depth)],
        [delays, velocity[0], station_cells, active[:, 0], active_other],
        [pltpu.SemaphoreType.DMA((2,))],
        hbm_in=(0, 1),
    )
    pays = [payload] + [to_line(payload, j) for j in range(1, slots)]

    height = 2 * rows + -(-slots * ROUNDS // 8) * 8
    packed = call(
        functools.partial(pack_kernel, rows, own_rows, slots),
        "pack",
        [out(height, depth)] * chips,
        [here, layer, other, *pays],
    )
    vel = [packed[0]] + [to_chip(packed[j], j) for j in range(1, chips)]

    pays, cells, _ = lax.optimization_barrier((pays, event_cells, packed[0]))
    stations = jnp.concatenate([p[0, events : events + 3] for p in pays]).astype(jnp.int32)
    scal = jnp.concatenate([here, stations])
    chunk = events
    while (1 + 2 * slots) * adj_rows * layers * chunk > EVENT_CHUNK * 2**11:
        chunk //= 2
    count, delay_sum = call(
        functools.partial(scatter_kernel, layers, events),
        "events",
        [out(adj_rows * layers, depth), out(slots, adj_rows * layers, depth)],
        [here, cells, *pays],
        [pltpu.VMEM(((1 + 2 * slots) * adj_rows * layers, chunk), jnp.bfloat16)],
        microseconds=3.0,
    )

    scal, count, delay_sum = lax.optimization_barrier((scal, count, delay_sum))

    together = min(slots, 4)
    flat = scratch(depth // LANES, rows * layers, LANES)
    times, final, speed = call(
        functools.partial(sweep_kernel, layers, own_rows, slots, chips),
        "sweeps",
        [
            out(slots, layers, own_rows, depth),
            out(*field(slots, adj_rows)),
            out(*field(rows)),
        ],
        [scal, *vel],
        [
            scratch(*field(rows)),
            scratch(*field(rows)),
            scratch(*field(rows)),
            scratch(*field(slots, rows + 2)),
            scratch(*field(slots, rows + 2)),
            scratch(slots * ROUNDS, layers, LANES),
            scratch(slots, ROUNDS, rows, layers, LANES),
            flat,
        ],
        microseconds=10.0,
    )
    kernel = call(
        functools.partial(adjoint_kernel, layers, own_rows, slots),
        "adjoint",
        [out(own_rows, depth)] * layers,
        [scal, final, speed, count, delay_sum],
        [
            scratch(*field(together, 6, adj_rows)),
            scratch(*field(together, adj_rows)),
            scratch(*field(together, adj_rows)),
            scratch(*field(together, adj_rows)),
            scratch(*field(adj_rows)),
            flat,
        ],
        microseconds=7.0,
    )

    times = lax.all_to_all(
        times.reshape(slots * layers, own_rows, depth), ("src", "space"), 0, 0, tiled=True
    )
    blocks = [kernel[0]] + [
        lax.ppermute(kernel[m], "space", [(i, i ^ m) for i in range(layers)])
        for m in range(1, layers)
    ]
    times, kernel = call(
        join_kernel,
        "join",
        [out(grid_rows, depth), out(line_rows, depth)],
        [here, times.reshape(grid_rows, depth), *blocks],
        [pltpu.SemaphoreType.DMA((1 + layers,))],
        in_place=range(1, 2 + layers),
        hbm_out=(0, 1),
    )
    return (times.reshape(1, 1, grid_rows, depth), kernel.reshape(1, line_rows, depth))


def solution(mesh):
    return jax.shard_map(
        per_device,
        mesh=mesh,
        in_specs=(
            P("space", None, None),
            P("src", None),
            P(),
            P("src", None),
            P(None, "src", "space", None),
        ),
        out_specs=(P("src", "space", None, None), P("space", "src", None)),
        check_vma=False,
    )
```

```python
import functools
import math

import jax
import jax.numpy as jnp
from jax import lax
from jax.experimental import pallas as pl
from jax.experimental.pallas import tpu as pltpu
from jax.sharding import PartitionSpec as P

TY = 32
ROUNDS = 2
SWEEPS = 2
ADJ_SWEEPS = 4
BIG = 1000000.0
LANES = 128

HALO = ROUNDS * SWEEPS + ADJ_SWEEPS
ADJ_HALO = ADJ_SWEEPS + 1

VMEM = pltpu.VMEM
SMEM = pltpu.SMEM


def spec(space):
    return pl.BlockSpec(memory_space=space)


def call(body, name, outs, operands, scratch=(), microseconds=1.0, in_place=(), hbm_in=(), hbm_out=()):
    held = [a for a in (*operands, *outs, *scratch) if len(a.shape) > 1]
    limit = 4 * 2**20 + sum(4 * math.prod((*a.shape[:-2], -(-math.prod(a.shape[-2:-1]) // 8) * 8, max(a.shape[-1], 128))) for a in held)
    return pl.pallas_call(
        body,
        out_shape=list(outs),
        in_specs=[
            spec(
                pltpu.HBM if i in hbm_in else pl.ANY if i in in_place else SMEM if a.ndim == 1 else VMEM
            )
            for i, a in enumerate(operands)
        ],
        out_specs=[spec(pltpu.HBM if i in hbm_out else VMEM) for i in range(len(outs))],
        scratch_shapes=list(scratch),
        compiler_params=pltpu.CompilerParams(vmem_limit_bytes=limit),
        cost_estimate=pl.CostEstimate(
            flops=0, bytes_accessed=int(microseconds * 3.5e6), transcendentals=0
        ),
        name=name,
    )(*[
        pltpu.with_memory_space_constraint(a, pltpu.HBM) if i in hbm_in else a
        for i, a in enumerate(operands)
    ])


def where_am_i(own_rows):
    place = lax.axis_index("space")
    line_row = lax.axis_index("src") * (lax.axis_size("space") * own_rows)
    first = line_row + place * own_rows - HALO
    return lax.div(place, 2), lax.rem(place, 2), line_row, first


def fetch_kernel(*refs):
    ins, (*outs, sems) = refs[: len(refs) // 2], refs[len(refs) // 2 :]
    copies = [pltpu.make_async_copy(a, b, sems.at[i]) for i, (a, b) in enumerate(zip(ins, outs))]
    for copy in copies:
        copy.start()
    for copy in copies:
        copy.wait()


def head_kernel(delays, station, active, active_other, out):
    events = delays.shape[1]
    out[:, :events] = delays[...]
    out[:, events:] = jnp.zeros((1, out.shape[1] - events), jnp.float32)
    at = events
    out[:, at : at + 3] = station[...].astype(jnp.float32)
    for source in (active, active_other):
        for part in range(ROUNDS):
            at += LANES
            out[:, at : at + source.shape[-1]] = source[part].astype(jnp.float32)


def pack_kernel(rows, own_rows, slots, own, other, *refs):
    chip, core, line_row, _ = where_am_i(own_rows)
    pays, outs = refs[:slots], refs[slots:]
    total = own.shape[0]
    chunk = math.gcd(own_rows, 8)
    at = pays[0].shape[1] - 2 * ROUNDS * LANES
    for j, out in enumerate(outs):
        first = line_row + ((chip ^ j) * 2 + core) * own_rows - HALO
        for piece in range(rows // chunk):
            start = jnp.clip(first + piece * chunk, 0, total - chunk)
            start = pl.multiple_of(start, chunk)
            out[piece * chunk : (piece + 1) * chunk, :] = own[pl.ds(start, chunk), :]
            out[rows + piece * chunk : rows + (piece + 1) * chunk, :] = other[pl.ds(start, chunk), :]
        out[2 * rows :, :] = jnp.zeros_like(out[2 * rows :, :])
        for slot, pay in enumerate(pays):
            for part in range(ROUNDS):
                row = 2 * rows + slot * ROUNDS + part
                for c in range(2):
                    tile = at + (c * ROUNDS + part) * LANES
                    out[row : row + 1, c * LANES : (c + 1) * LANES] = pay[:, tile : tile + LANES]


EVENT_CHUNK = 2048


def scatter_kernel(layers, own_rows, events, cells, *refs):
    slots = len(refs) - 3
    pays, count, delay_sum, left = refs[:slots], refs[slots], refs[slots + 1], refs[slots + 2]
    first_row = where_am_i(own_rows)[3] + HALO - ADJ_HALO
    height, width = count.shape
    chunk = left.shape[1]
    steps = events // chunk
    contract = (((1,), (1,)), ((), ()))

    def step(index, carry):
        start = pl.multiple_of(index * chunk, chunk)
        where_x = cells[0:1, pl.ds(start, chunk)]
        where_y = cells[1:2, pl.ds(start, chunk)] - first_row
        where_z = cells[2:3, pl.ds(start, chunk)]
        at = jnp.where(where_y >= 0, where_y * layers + where_x, -1)
        hit = lax.broadcasted_iota(jnp.int32, (height, chunk), 0) == at
        hit = hit.astype(jnp.bfloat16)
        left[:height, :] = hit
        for slot in range(slots):
            delay = pays[slot][:, pl.ds(start, chunk)]
            high = delay.astype(jnp.bfloat16)
            low = (delay - high.astype(jnp.float32)).astype(jnp.bfloat16)
            for half, factor in enumerate((high, low)):
                row = (1 + 2 * slot + half) * height
                left[row : row + height, :] = hit * factor
        depth = lax.broadcasted_iota(jnp.int32, (width, chunk), 0) == where_z
        depth = depth.astype(jnp.bfloat16)
        value = lax.dot_general(left[...], depth, contract, preferred_element_type=jnp.float32)
        pieces = [value[i * height : (i + 1) * height] for i in range(1 + 2 * slots)]
        sums = [pieces[1 + 2 * slot] + pieces[2 + 2 * slot] for slot in range(slots)]
        if steps == 1:
            count[...] = pieces[0]
            for slot in range(slots):
                delay_sum[slot] = sums[slot]
        else:
            count[...] += pieces[0]
            for slot in range(slots):
                delay_sum[slot] += sums[slot]
        return carry

    if steps == 1:
        step(0, 0)
    else:
        count[...] = jnp.zeros_like(count)
        delay_sum[...] = jnp.zeros_like(delay_sum)
        lax.fori_loop(0, steps, step, 0)


def get(ref, row, size, *lead):
    index = (*lead, pl.ds(row, size))
    return [
        ref[(*index, slice(None), slice(p, p + LANES))] for p in range(0, ref.shape[-1], LANES)
    ]


def put(ref, row, size, value, *lead):
    index = (*lead, pl.ds(row, size))
    for p, piece in enumerate(value):
        ref[(*index, slice(None), slice(p * LANES, (p + 1) * LANES))] = piece


def each(function, *values):
    return [function(*pieces) for pieces in zip(*values)]


def loop(low, high, size, body, unroll=16):
    steps = (high - low) // size
    if steps <= unroll:
        for i in range(steps):
            body(low + i * size, size)
    else:
        lax.fori_loop(
            0,
            steps,
            lambda i, carry: (body(low + i * size, size), carry)[1],
            0,
            unroll=unroll,
        )
    if low + steps * size < high:
        loop(low + steps * size, high, max(size // 2, 1), body)


class Grid:
    def __init__(self, size, layers, depth):
        shape = (size, layers, LANES)
        layer = lax.broadcasted_iota(jnp.int32, shape, 1)
        lane = lax.broadcasted_iota(jnp.int32, shape, 2)
        self.layers = layers
        self.layer_low, self.layer_high = layer == 0, layer == layers - 1
        self.lane_low, self.lane_high = lane == 0, lane == LANES - 1

    def layer_before(self, value):
        return [pltpu.roll(piece, 1, 1) for piece in value]

    def layer_after(self, value):
        return [pltpu.roll(piece, self.layers - 1, 1) for piece in value]

    def depth_before(self, value, fill=None):
        moved = [pltpu.roll(piece, 1, 2) for piece in value]
        first = moved[0] if fill is None else jnp.where(self.lane_low, fill, moved[0])
        rest = [
            jnp.where(self.lane_low, low, here) for low, here in zip(moved[:-1], moved[1:])
        ]
        return [first] + rest

    def depth_after(self, value, fill=None):
        moved = [pltpu.roll(piece, LANES - 1, 2) for piece in value]
        last = moved[-1] if fill is None else jnp.where(self.lane_high, fill, moved[-1])
        rest = [
            jnp.where(self.lane_high, high, here) for here, high in zip(moved[:-1], moved[1:])
        ]
        return rest + [last]

    def no_low(self, value, fill):
        return [jnp.where(self.layer_low, fill, piece) for piece in value]

    def no_high(self, value, fill):
        return [jnp.where(self.layer_high, fill, piece) for piece in value]


class Flat:
    def __init__(self, ref, layers):
        self.ref, self.layers, self.parts = ref, layers, ref.shape[0]

    def put_layer(self, place, rows, value):
        for p in range(self.parts):
            self.ref.at[p][pl.ds(place, rows, stride=self.layers), :] = value[
                :, p * LANES : (p + 1) * LANES
            ]

    def get_layer(self, place, rows):
        pieces = [
            self.ref.at[p][pl.ds(place, rows, stride=self.layers), :] for p in range(self.parts)
        ]
        return jnp.concatenate(pieces, axis=1)

    def span(self, row, size):
        return pl.ds(pl.multiple_of(row * self.layers, self.layers), size * self.layers)

    def get(self, row, size):
        return [
            self.ref[p, self.span(row, size), :].reshape(size, self.layers, LANES)
            for p in range(self.parts)
        ]

    def put(self, row, size, value):
        for p in range(self.parts):
            self.ref[p, self.span(row, size), :] = value[p].reshape(size * self.layers, LANES)


def root_of(value):
    value = jnp.maximum(value, 1e-30)
    return value * lax.rsqrt(value)


class Straight:
    def __init__(self, layers, parts, at, grid_rows):
        shape = (1, layers, LANES)
        self.at_y, self.grid_rows = at[1], grid_rows
        dx = (lax.broadcasted_iota(jnp.int32, shape, 1) - at[0]).astype(jnp.float32)
        self.across = []
        for p in range(parts):
            dz = lax.broadcasted_iota(jnp.int32, shape, 2) + (p * LANES - at[2])
            dz = dz.astype(jnp.float32)
            self.across.append(dx * dx + dz * dz)

    def row(self, y):
        gap = y - self.at_y
        far = (gap * gap).astype(jnp.float32)
        inside = (y >= 0) & (y < self.grid_rows)
        return [jnp.where(inside, root_of(a + far), BIG) for a in self.across]


def local_solve(near_x, near_y, near_z, cost, twice, one_half):
    small = jnp.minimum(near_x, near_y)
    large = jnp.maximum(near_x, near_y)
    lowest = jnp.minimum(small, near_z)
    highest = jnp.maximum(large, near_z)
    middle = jnp.maximum(small, jnp.minimum(large, near_z))
    first_gap = middle - lowest
    second_gap = highest - lowest
    square = first_gap * first_gap
    single = lowest + cost
    double = lowest + 0.5 * (first_gap + root_of(twice - square))
    rest = square + second_gap * (second_gap - first_gap)
    root = root_of(one_half - rest)
    triple = lowest + ((first_gap + second_gap) * (1.0 / 3.0) + root * (math.sqrt(2.0) / 3.0))
    return jnp.where(single <= middle, single, jnp.where(double <= highest, double, triple))


SWEEP_ROWS = 4
SWEEP_UNROLL = 8


def sweep_kernel(layers, own_rows, grid_rows, slots, chips, scal, *refs):
    rows = own_rows + 2 * HALO
    depth = refs[0].shape[-1]
    parts = depth // LANES
    vel_in, refs = refs[:chips], refs[chips:]
    times_out, final, speed, refs = refs[0], refs[1], refs[2], refs[3:]
    cost, twice, one_half, ping, pong, acts, mask, flat = refs
    flat = Flat(flat, layers)
    line = lax.axis_index("src")
    chip, core, _, y_first = where_am_i(own_rows)
    stations = [[scal[3 * slot + i] for i in range(3)] for slot in range(slots)]

    for j in range(chips):
        for c in range(2):
            place = (chip ^ j) * 2 + (core ^ c)
            flat.put_layer(place, rows, vel_in[j][c * rows : (c + 1) * rows, :])
            for slot in range(slots):
                for part in range(ROUNDS):
                    row = 2 * rows + slot * ROUNDS + part
                    acts[slot * ROUNDS + part, pl.ds(place, 1), :] = vel_in[j][
                        row : row + 1, c * LANES : (c + 1) * LANES
                    ]

    def prepare(row, size):
        value = flat.get(row, size)
        slow = each(lambda v: 1.0 / v, value)
        put(speed, row, size, value)
        put(cost, row, size, slow)
        put(twice, row, size, each(lambda f: 2.0 * (f * f), slow))
        put(one_half, row, size, each(lambda f: 1.5 * (f * f), slow))

    loop(0, rows, 4, prepare)

    straight = [Straight(layers, parts, stations[slot], grid_rows) for slot in range(slots)]

    def fill(row, size):
        for i in range(size):
            for slot in range(slots):
                put(ping, row + i, 1, straight[slot].row(y_first - 1 + row + i), slot)

    loop(0, rows + 2, 4, fill)

    lane_iota = lax.broadcasted_iota(jnp.int32, (layers, LANES), 1)
    tile_first = (y_first + TY) // TY - 1
    tile_span = (rows + TY - 2) // TY + 1
    for slot in range(slots):
        for part in range(ROUNDS):
            act = acts[slot * ROUNDS + part]
            columns = []
            for t in range(tile_span):
                here = lane_iota == tile_first + t
                picked = jnp.sum(jnp.where(here, act, 0.0), axis=1, keepdims=True)
                columns.append(jnp.broadcast_to(picked, (layers, LANES)))
            for i in range(rows):
                value = columns[0]
                for t in range(1, tile_span):
                    value = jnp.where(y_first + i >= (tile_first + t) * TY, columns[t], value)
                mask[slot, part, i] = value

    def sweep(source, target, low, high, part, shift):
        def body(row, size):
            grid = Grid(size, layers, depth)
            costs = get(cost, row, size), get(twice, row, size), get(one_half, row, size)
            for slot in range(slots):
                field = get(source, row, size + 2, slot)
                here = each(lambda f: f[1 : size + 1], field)
                near_y = each(lambda f: jnp.minimum(f[:size], f[2:]), field)
                near_x = each(
                    jnp.minimum,
                    grid.no_low(grid.layer_before(here), BIG),
                    grid.no_high(grid.layer_after(here), BIG),
                )
                near_z = each(
                    jnp.minimum, grid.depth_before(here, BIG), grid.depth_after(here, BIG)
                )
                update = each(local_solve, near_x, near_y, near_z, *costs)
                on = mask[slot, part, pl.ds(row, size)] > 0.0
                put(
                    target,
                    row + shift,
                    size,
                    each(lambda u, h: jnp.where(on, u, h), update, here),
                    slot,
                )

        loop(low, high, SWEEP_ROWS, body, SWEEP_UNROLL if slots <= 4 else 1)
        for slot in range(slots):
            at_x, at_y, at_z = stations[slot]
            local = at_y - y_first

            @pl.when((local >= low) & (local < high))
            def _():
                shape = (1, layers, depth)
                there = (lax.broadcasted_iota(jnp.int32, shape, 1) == at_x) & (
                    lax.broadcasted_iota(jnp.int32, shape, 2) == at_z
                )
                here = slot, pl.ds(local + shift, 1)
                target[here] = jnp.where(there, 0.0, target[here])

    fields = [ping, pong]
    last = ROUNDS * SWEEPS - 1
    for index in range(last):
        sweep(fields[index % 2], fields[(index + 1) % 2], index, rows - index, index // SWEEPS, 1)
    sweep(fields[last % 2], final, last, rows - last, last // SWEEPS, -last)

    for slot in range(slots):
        loop(0, own_rows, 4, lambda row, size: flat.put(row, size, get(final, row + ADJ_HALO, size, slot)))
        for place in range(layers):
            times_out[line ^ slot, place] = flat.get_layer(place, own_rows)


ADJ_ROWS = 4
ADJ_UNROLL = 8


def adjoint_kernel(layers, own_rows, grid_rows, slots, scal, final, speed, count, delay_sum, *refs):
    depth = final.shape[-1]
    parts = depth // LANES
    kernel_out, refs = refs[:layers], refs[layers:]
    weight, src, adj_a, adj_b, density, flat = refs
    together = weight.shape[0]
    flat = Flat(flat, layers)
    y_first = where_am_i(own_rows)[3]
    stations = [[scal[3 * slot + i] for i in range(3)] for slot in range(slots)]
    straight = [Straight(layers, parts, stations[slot], grid_rows) for slot in range(slots)]
    shift = HALO - ADJ_HALO
    rows = own_rows + 2 * ADJ_HALO

    def sums(ref, row, size, *lead):
        span = pl.ds(pl.multiple_of(row * layers, layers), size * layers)
        return [
            ref[(*lead, span, slice(p * LANES, (p + 1) * LANES))].reshape(size, layers, LANES)
            for p in range(parts)
        ]

    def make_source(group, row, size):
        for i in range(size):
            number = sums(count, row + i, 1)
            for slot in group:
                value = each(
                    lambda n, t, d, s: n * (t - d) - s,
                    number,
                    get(final, row + i, 1, slot),
                    straight[slot].row(y_first + shift + row + i),
                    sums(delay_sum, row + i, 1, slot),
                )
                put(src, row + i, 1, value, slot - group[0])

    def make_weight(group, row, size):
        grid = Grid(size, layers, depth)
        scale = each(lambda v: v * (1.0 / 6.0), get(speed, row + shift, size))
        for slot in group:
            field = get(final, row - 1, size + 2, slot)
            here = each(lambda f: f[1 : size + 1], field)

            def rise(value):
                return each(lambda v, h, s: jnp.maximum(v - h, 0.0) * s, value, here, scale)

            def keep(value, piece, edge):
                return [jnp.where(edge, 0.0, v) if p == piece else v for p, v in enumerate(value)]

            six = [
                grid.no_low(rise(grid.layer_before(here)), 0.0),
                grid.no_high(rise(grid.layer_after(here)), 0.0),
                rise(each(lambda f: f[:size], field)),
                rise(each(lambda f: f[2:], field)),
                keep(rise(grid.depth_before(here)), 0, grid.lane_low),
                keep(rise(grid.depth_after(here)), parts - 1, grid.lane_high),
            ]
            for n, value in enumerate(six):
                put(weight, row, size, value, slot - group[0], n)

    def multiply_add(value, factor, neighbour):
        return value + factor * neighbour

    def smooth(low, here, high):
        return (low + 2.0 * here + high) * 0.25

    def sweep(group, source, target, low, high):
        def body(row, size):
            grid = Grid(size, layers, depth)
            total = None if group[0] == 0 else get(density, row, size)
            for slot in range(len(group)):
                field = get(source, row - 1, size + 2, slot)
                here = each(lambda f: f[1 : size + 1], field)
                around = [
                    grid.layer_before(here),
                    grid.layer_after(here),
                    each(lambda f: f[:size], field),
                    each(lambda f: f[2:], field),
                    grid.depth_before(here),
                    grid.depth_after(here),
                ]
                value = get(src, row, size, slot)
                for n, neighbour in enumerate(around):
                    value = each(multiply_add, value, get(weight, row, size, slot, n), neighbour)
                if target is not None:
                    put(target, row, size, value, slot)
                else:
                    total = value if total is None else each(jnp.add, total, value)
            if target is None:
                if group[-1] == slots - 1:
                    value = each(lambda t, v: t / v, total, get(speed, row + shift, size))
                    low = grid.no_low(grid.layer_before(value), 0.0)
                    high = grid.no_high(grid.layer_after(value), 0.0)
                    total = each(smooth, low, value, high)
                put(density, row, size, total)

        loop(low, high, ADJ_ROWS, body, ADJ_UNROLL if slots <= 4 else 1)

    for first in range(0, slots, together):
        group = range(first, min(first + together, slots))
        loop(0, rows, 4, functools.partial(make_source, group))
        loop(1, rows - 1, 4, functools.partial(make_weight, group))
        fields = [src] + [(adj_a, adj_b)[i % 2] for i in range(ADJ_SWEEPS - 1)] + [None]
        for index in range(ADJ_SWEEPS):
            sweep(group, fields[index], fields[index + 1], index + 1, rows - 1 - index)

    def finish(row, size):
        grid = Grid(size, layers, depth)
        field = get(density, row + ADJ_SWEEPS, size + 2)
        value = each(lambda f: smooth(f[:size], f[1 : size + 1], f[2:]), field)
        low, high = grid.depth_before(value, 0.0), grid.depth_after(value, 0.0)
        flat.put(row, size, each(smooth, low, value, high))

    loop(0, own_rows, 4, finish)
    for m, out in enumerate(kernel_out):
        out[...] = flat.get_layer(lax.axis_index("space") ^ m, own_rows)


def join_kernel(times, *refs):
    blocks, (times_out, out, sems) = refs[:-3], refs[-3:]
    rows = blocks[0].shape[0]
    copies = [pltpu.make_async_copy(times, times_out, sems.at[0])]
    for m, block in enumerate(blocks):
        start = pl.multiple_of((lax.axis_index("space") ^ m) * rows, rows)
        copies.append(pltpu.make_async_copy(block, out.at[pl.ds(start, rows)], sems.at[m + 1]))
    for copy in copies:
        copy.start()
    for copy in copies:
        copy.wait()


def per_device(velocity, station_cells, event_cells, delays, active):
    _, grid_rows, depth = velocity.shape
    slots, layers = lax.axis_size("src"), lax.axis_size("space")
    chips = layers // 2
    events = event_cells.shape[1]
    line_rows = grid_rows // slots
    own_rows = line_rows // layers
    rows = own_rows + 2 * HALO
    adj_rows = own_rows + 2 * ADJ_HALO

    def to_line(array, j):
        return lax.ppermute(array, "src", [(i, i ^ j) for i in range(slots)])

    def to_chip(array, j):
        return lax.ppermute(array, "space", [(i, i ^ (2 * j)) for i in range(layers)])

    def to_core(array):
        return lax.ppermute(array, "space", [(i, i ^ 1) for i in range(layers)])

    f32 = jnp.float32
    def out(*shape):
        return jax.ShapeDtypeStruct(shape, f32)

    def scratch(*shape):
        return pltpu.VMEM(shape, f32)

    def field(*lead):
        return (*lead, layers, depth)

    other = to_core(velocity[0])
    active_other = to_core(active[:, 0])
    mine = [velocity[0], delays, station_cells, active[:, 0]]
    layer, delays, station_cells, active = call(
        fetch_kernel,
        "fetch",
        [jax.ShapeDtypeStruct(a.shape, a.dtype) for a in mine],
        mine,
        [pltpu.SemaphoreType.DMA((len(mine),))],
        hbm_in=range(len(mine)),
    )
    (payload,) = call(
        head_kernel,
        "head",
        [out(1, events + LANES * (1 + 2 * ROUNDS))],
        [delays, station_cells, active, active_other],
    )
    pays = [payload] + [to_line(payload, j) for j in range(1, slots)]

    height = 2 * rows + -(-slots * ROUNDS // 8) * 8
    packed = call(
        functools.partial(pack_kernel, rows, own_rows, slots),
        "pack",
        [out(height, depth)] * chips,
        [layer, other, *pays],
    )
    vel = [packed[0]] + [to_chip(packed[j], j) for j in range(1, chips)]

    pays, cells, _ = lax.optimization_barrier((pays, event_cells, packed[0]))
    scal = jnp.concatenate([p[0, events : events + 3] for p in pays]).astype(jnp.int32)
    chunk = events
    while (1 + 2 * slots) * adj_rows * layers * chunk > EVENT_CHUNK * 2**11:
        chunk //= 2
    count, delay_sum = call(
        functools.partial(scatter_kernel, layers, own_rows, events),
        "events",
        [out(adj_rows * layers, depth), out(slots, adj_rows * layers, depth)],
        [cells, *pays],
        [pltpu.VMEM(((1 + 2 * slots) * adj_rows * layers, chunk), jnp.bfloat16)],
        microseconds=3.0,
    )

    scal, count, delay_sum = lax.optimization_barrier((scal, count, delay_sum))

    together = min(slots, 4)
    flat = scratch(depth // LANES, rows * layers, LANES)
    times, final, speed = call(
        functools.partial(sweep_kernel, layers, own_rows, grid_rows, slots, chips),
        "sweeps",
        [
            out(slots, layers, own_rows, depth),
            out(*field(slots, adj_rows)),
            out(*field(rows)),
        ],
        [scal, *vel],
        [
            scratch(*field(rows)),
            scratch(*field(rows)),
            scratch(*field(rows)),
            scratch(*field(slots, rows + 2)),
            scratch(*field(slots, rows + 2)),
            scratch(slots * ROUNDS, layers, LANES),
            scratch(slots, ROUNDS, rows, layers, LANES),
            flat,
        ],
        microseconds=10.0,
    )
    kernel = call(
        functools.partial(adjoint_kernel, layers, own_rows, grid_rows, slots),
        "adjoint",
        [out(own_rows, depth)] * layers,
        [scal, final, speed, count, delay_sum],
        [
            scratch(*field(together, 6, adj_rows)),
            scratch(*field(together, adj_rows)),
            scratch(*field(together, adj_rows)),
            scratch(*field(together, adj_rows)),
            scratch(*field(adj_rows)),
            flat,
        ],
        microseconds=7.0,
    )

    times = lax.all_to_all(
        times.reshape(slots * layers, own_rows, depth), ("src", "space"), 0, 0, tiled=True
    )
    blocks = [kernel[0]] + [
        lax.ppermute(kernel[m], "space", [(i, i ^ m) for i in range(layers)])
        for m in range(1, layers)
    ]
    times, kernel = call(
        join_kernel,
        "join",
        [out(grid_rows, depth), out(line_rows, depth)],
        [times.reshape(grid_rows, depth), *blocks],
        [pltpu.SemaphoreType.DMA((1 + layers,))],
        in_place=range(1 + layers),
        hbm_out=(0, 1),
    )
    return (times.reshape(1, 1, grid_rows, depth), kernel.reshape(1, line_rows, depth))


def solution(mesh):
    return jax.shard_map(
        per_device,
        mesh=mesh,
        in_specs=(
            P("space", None, None),
            P("src", None),
            P(),
            P("src", None),
            P(None, "src", "space", None),
        ),
        out_specs=(P("src", "space", None, None), P("space", "src", None)),
        check_vma=False,
    )
```

```python
import functools
import math

import jax
import jax.numpy as jnp
from jax import lax
from jax.experimental import pallas as pl
from jax.experimental.pallas import tpu as pltpu
from jax.sharding import PartitionSpec as P

TY = 32
ROUNDS = 2
SWEEPS = 2
ADJ_SWEEPS = 4
BIG = 1000000.0
LANES = 128

HALO = ROUNDS * SWEEPS + ADJ_SWEEPS
ADJ_HALO = ADJ_SWEEPS + 1

VMEM = pltpu.VMEM
SMEM = pltpu.SMEM


def spec(space):
    return pl.BlockSpec(memory_space=space)


def call(body, name, outs, operands, scratch=(), microseconds=1.0, in_place=(), hbm_in=(), hbm_out=()):
    held = [a for a in (*operands, *outs, *scratch) if len(a.shape) > 1]
    limit = 4 * 2**20 + sum(4 * math.prod((*a.shape[:-2], -(-math.prod(a.shape[-2:-1]) // 8) * 8, max(a.shape[-1], 128))) for a in held)
    return pl.pallas_call(
        body,
        out_shape=list(outs),
        in_specs=[
            spec(
                pltpu.HBM if i in hbm_in else pl.ANY if i in in_place else SMEM if a.ndim == 1 else VMEM
            )
            for i, a in enumerate(operands)
        ],
        out_specs=[spec(pltpu.HBM if i in hbm_out else VMEM) for i in range(len(outs))],
        scratch_shapes=list(scratch),
        compiler_params=pltpu.CompilerParams(vmem_limit_bytes=limit),
        cost_estimate=pl.CostEstimate(
            flops=0, bytes_accessed=int(microseconds * 3.5e6), transcendentals=0
        ),
        name=name,
    )(*[
        pltpu.with_memory_space_constraint(a, pltpu.HBM) if i in hbm_in else a
        for i, a in enumerate(operands)
    ])


def where_am_i(own_rows):
    place = lax.axis_index("space")
    line_row = lax.axis_index("src") * (lax.axis_size("space") * own_rows)
    first = line_row + place * own_rows - HALO
    return lax.div(place, 2), lax.rem(place, 2), line_row, first


def station_of(pay, events):
    cell = pay[0:1, events : events + LANES].astype(jnp.int32)
    return [cell[0, i] for i in range(3)]


def fetch_kernel(*refs):
    ins, (*outs, sems) = refs[: len(refs) // 2], refs[len(refs) // 2 :]
    copies = [pltpu.make_async_copy(a, b, sems.at[i]) for i, (a, b) in enumerate(zip(ins, outs))]
    for copy in copies:
        copy.start()
    for copy in copies:
        copy.wait()


def head_kernel(delays, station, active, active_other, out):
    events = delays.shape[1]
    out[:, :events] = delays[...]
    out[:, events:] = jnp.zeros((1, out.shape[1] - events), jnp.float32)
    at = events
    out[:, at : at + 3] = station[...].astype(jnp.float32)
    for source in (active, active_other):
        for part in range(ROUNDS):
            at += LANES
            out[:, at : at + source.shape[-1]] = source[part].astype(jnp.float32)


def pack_kernel(rows, own_rows, slots, own, other, *refs):
    chip, core, line_row, _ = where_am_i(own_rows)
    pays, outs = refs[:slots], refs[slots:]
    total = own.shape[0]
    chunk = math.gcd(own_rows, 8)
    at = pays[0].shape[1] - 2 * ROUNDS * LANES
    for j, out in enumerate(outs):
        first = line_row + ((chip ^ j) * 2 + core) * own_rows - HALO
        for piece in range(rows // chunk):
            start = jnp.clip(first + piece * chunk, 0, total - chunk)
            start = pl.multiple_of(start, chunk)
            out[piece * chunk : (piece + 1) * chunk, :] = own[pl.ds(start, chunk), :]
            out[rows + piece * chunk : rows + (piece + 1) * chunk, :] = other[pl.ds(start, chunk), :]
        out[2 * rows :, :] = jnp.zeros_like(out[2 * rows :, :])
        for slot, pay in enumerate(pays):
            for part in range(ROUNDS):
                row = 2 * rows + slot * ROUNDS + part
                for c in range(2):
                    tile = at + (c * ROUNDS + part) * LANES
                    out[row : row + 1, c * LANES : (c + 1) * LANES] = pay[:, tile : tile + LANES]


EVENT_CHUNK = 2048


def scatter_kernel(layers, own_rows, events, cells, *refs):
    slots = len(refs) - 3
    pays, count, delay_sum, left = refs[:slots], refs[slots], refs[slots + 1], refs[slots + 2]
    first_row = where_am_i(own_rows)[3] + HALO - ADJ_HALO
    height, width = count.shape
    chunk = left.shape[1]
    steps = events // chunk
    contract = (((1,), (1,)), ((), ()))

    def step(index, carry):
        start = pl.multiple_of(index * chunk, chunk)
        where_x = cells[0:1, pl.ds(start, chunk)]
        where_y = cells[1:2, pl.ds(start, chunk)] - first_row
        where_z = cells[2:3, pl.ds(start, chunk)]
        at = jnp.where(where_y >= 0, where_y * layers + where_x, -1)
        hit = lax.broadcasted_iota(jnp.int32, (height, chunk), 0) == at
        hit = hit.astype(jnp.bfloat16)
        left[:height, :] = hit
        for slot in range(slots):
            delay = pays[slot][:, pl.ds(start, chunk)]
            high = delay.astype(jnp.bfloat16)
            low = (delay - high.astype(jnp.float32)).astype(jnp.bfloat16)
            for half, factor in enumerate((high, low)):
                row = (1 + 2 * slot + half) * height
                left[row : row + height, :] = hit * factor
        depth = lax.broadcasted_iota(jnp.int32, (width, chunk), 0) == where_z
        depth = depth.astype(jnp.bfloat16)
        value = lax.dot_general(left[...], depth, contract, preferred_element_type=jnp.float32)
        pieces = [value[i * height : (i + 1) * height] for i in range(1 + 2 * slots)]
        sums = [pieces[1 + 2 * slot] + pieces[2 + 2 * slot] for slot in range(slots)]
        if steps == 1:
            count[...] = pieces[0]
            for slot in range(slots):
                delay_sum[slot] = sums[slot]
        else:
            count[...] += pieces[0]
            for slot in range(slots):
                delay_sum[slot] += sums[slot]
        return carry

    if steps == 1:
        step(0, 0)
    else:
        count[...] = jnp.zeros_like(count)
        delay_sum[...] = jnp.zeros_like(delay_sum)
        lax.fori_loop(0, steps, step, 0)


def get(ref, row, size, *lead):
    index = (*lead, pl.ds(row, size))
    return [
        ref[(*index, slice(None), slice(p, p + LANES))] for p in range(0, ref.shape[-1], LANES)
    ]


def put(ref, row, size, value, *lead):
    index = (*lead, pl.ds(row, size))
    for p, piece in enumerate(value):
        ref[(*index, slice(None), slice(p * LANES, (p + 1) * LANES))] = piece


def each(function, *values):
    return [function(*pieces) for pieces in zip(*values)]


def loop(low, high, size, body, unroll=16):
    steps = (high - low) // size
    if steps <= unroll:
        for i in range(steps):
            body(low + i * size, size)
    else:
        lax.fori_loop(
            0,
            steps,
            lambda i, carry: (body(low + i * size, size), carry)[1],
            0,
            unroll=unroll,
        )
    if low + steps * size < high:
        loop(low + steps * size, high, max(size // 2, 1), body)


class Grid:
    def __init__(self, size, layers, depth):
        shape = (size, layers, LANES)
        layer = lax.broadcasted_iota(jnp.int32, shape, 1)
        lane = lax.broadcasted_iota(jnp.int32, shape, 2)
        self.layers = layers
        self.layer_low, self.layer_high = layer == 0, layer == layers - 1
        self.lane_low, self.lane_high = lane == 0, lane == LANES - 1

    def layer_before(self, value):
        return [pltpu.roll(piece, 1, 1) for piece in value]

    def layer_after(self, value):
        return [pltpu.roll(piece, self.layers - 1, 1) for piece in value]

    def depth_before(self, value, fill=None):
        moved = [pltpu.roll(piece, 1, 2) for piece in value]
        first = moved[0] if fill is None else jnp.where(self.lane_low, fill, moved[0])
        rest = [
            jnp.where(self.lane_low, low, here) for low, here in zip(moved[:-1], moved[1:])
        ]
        return [first] + rest

    def depth_after(self, value, fill=None):
        moved = [pltpu.roll(piece, LANES - 1, 2) for piece in value]
        last = moved[-1] if fill is None else jnp.where(self.lane_high, fill, moved[-1])
        rest = [
            jnp.where(self.lane_high, high, here) for here, high in zip(moved[:-1], moved[1:])
        ]
        return rest + [last]

    def no_low(self, value, fill):
        return [jnp.where(self.layer_low, fill, piece) for piece in value]

    def no_high(self, value, fill):
        return [jnp.where(self.layer_high, fill, piece) for piece in value]


class Flat:
    def __init__(self, ref, layers):
        self.ref, self.layers, self.parts = ref, layers, ref.shape[0]

    def put_layer(self, place, rows, value):
        for p in range(self.parts):
            self.ref.at[p][pl.ds(place, rows, stride=self.layers), :] = value[
                :, p * LANES : (p + 1) * LANES
            ]

    def get_layer(self, place, rows):
        pieces = [
            self.ref.at[p][pl.ds(place, rows, stride=self.layers), :] for p in range(self.parts)
        ]
        return jnp.concatenate(pieces, axis=1)

    def span(self, row, size):
        return pl.ds(pl.multiple_of(row * self.layers, self.layers), size * self.layers)

    def get(self, row, size):
        return [
            self.ref[p, self.span(row, size), :].reshape(size, self.layers, LANES)
            for p in range(self.parts)
        ]

    def put(self, row, size, value):
        for p in range(self.parts):
            self.ref[p, self.span(row, size), :] = value[p].reshape(size * self.layers, LANES)


def root_of(value):
    value = jnp.maximum(value, 1e-30)
    return value * lax.rsqrt(value)


class Straight:
    def __init__(self, layers, parts, at, grid_rows):
        shape = (1, layers, LANES)
        self.at_y, self.grid_rows = at[1], grid_rows
        dx = (lax.broadcasted_iota(jnp.int32, shape, 1) - at[0]).astype(jnp.float32)
        self.across = []
        for p in range(parts):
            dz = lax.broadcasted_iota(jnp.int32, shape, 2) + (p * LANES - at[2])
            dz = dz.astype(jnp.float32)
            self.across.append(dx * dx + dz * dz)

    def row(self, y):
        gap = y - self.at_y
        far = (gap * gap).astype(jnp.float32)
        inside = (y >= 0) & (y < self.grid_rows)
        return [jnp.where(inside, root_of(a + far), BIG) for a in self.across]


def local_solve(near_x, near_y, near_z, cost, twice, one_half):
    small = jnp.minimum(near_x, near_y)
    large = jnp.maximum(near_x, near_y)
    lowest = jnp.minimum(small, near_z)
    highest = jnp.maximum(large, near_z)
    middle = jnp.maximum(small, jnp.minimum(large, near_z))
    first_gap = middle - lowest
    second_gap = highest - lowest
    square = first_gap * first_gap
    single = lowest + cost
    double = lowest + 0.5 * (first_gap + root_of(twice - square))
    rest = square + second_gap * (second_gap - first_gap)
    root = root_of(one_half - rest)
    triple = lowest + ((first_gap + second_gap) * (1.0 / 3.0) + root * (math.sqrt(2.0) / 3.0))
    return jnp.where(single <= middle, single, jnp.where(double <= highest, double, triple))


SWEEP_ROWS = 4
SWEEP_UNROLL = 8


def sweep_kernel(layers, own_rows, grid_rows, slots, chips, events, *refs):
    rows = own_rows + 2 * HALO
    pays, refs = refs[:slots], refs[slots:]
    depth = refs[0].shape[-1]
    parts = depth // LANES
    vel_in, refs = refs[:chips], refs[chips:]
    times_out, final, speed, refs = refs[0], refs[1], refs[2], refs[3:]
    cost, twice, one_half, ping, pong, acts, mask, flat, staged, sems = refs
    flat = Flat(flat, layers)
    line = lax.axis_index("src")
    chip, core, _, y_first = where_am_i(own_rows)
    stations = [station_of(pay, events) for pay in pays]

    for j in range(chips):
        for c in range(2):
            place = (chip ^ j) * 2 + (core ^ c)
            flat.put_layer(place, rows, vel_in[j][c * rows : (c + 1) * rows, :])
            for slot in range(slots):
                for part in range(ROUNDS):
                    row = 2 * rows + slot * ROUNDS + part
                    acts[slot * ROUNDS + part, pl.ds(place, 1), :] = vel_in[j][
                        row : row + 1, c * LANES : (c + 1) * LANES
                    ]

    def prepare(row, size):
        value = flat.get(row, size)
        slow = each(lambda v: 1.0 / v, value)
        put(speed, row, size, value)
        put(cost, row, size, slow)
        put(twice, row, size, each(lambda f: 2.0 * (f * f), slow))
        put(one_half, row, size, each(lambda f: 1.5 * (f * f), slow))

    loop(0, rows, 4, prepare)

    straight = [Straight(layers, parts, stations[slot], grid_rows) for slot in range(slots)]

    def fill(row, size):
        for i in range(size):
            for slot in range(slots):
                put(ping, row + i, 1, straight[slot].row(y_first - 1 + row + i), slot)

    loop(0, rows + 2, 4, fill)

    lane_iota = lax.broadcasted_iota(jnp.int32, (layers, LANES), 1)
    tile_first = (y_first + TY) // TY - 1
    tile_span = (rows + TY - 2) // TY + 1
    for slot in range(slots):
        for part in range(ROUNDS):
            act = acts[slot * ROUNDS + part]
            columns = []
            for t in range(tile_span):
                here = lane_iota == tile_first + t
                picked = jnp.sum(jnp.where(here, act, 0.0), axis=1, keepdims=True)
                columns.append(jnp.broadcast_to(picked, (layers, LANES)))
            for i in range(rows):
                value = columns[0]
                for t in range(1, tile_span):
                    value = jnp.where(y_first + i >= (tile_first + t) * TY, columns[t], value)
                mask[slot, part, i] = value

    def sweep(source, target, low, high, part, shift, group):
        def body(row, size):
            grid = Grid(size, layers, depth)
            costs = get(cost, row, size), get(twice, row, size), get(one_half, row, size)
            for slot in group:
                field = get(source, row, size + 2, slot)
                here = each(lambda f: f[1 : size + 1], field)
                near_y = each(lambda f: jnp.minimum(f[:size], f[2:]), field)
                near_x = each(
                    jnp.minimum,
                    grid.no_low(grid.layer_before(here), BIG),
                    grid.no_high(grid.layer_after(here), BIG),
                )
                near_z = each(
                    jnp.minimum, grid.depth_before(here, BIG), grid.depth_after(here, BIG)
                )
                update = each(local_solve, near_x, near_y, near_z, *costs)
                on = mask[slot, part, pl.ds(row, size)] > 0.0
                put(
                    target,
                    row + shift,
                    size,
                    each(lambda u, h: jnp.where(on, u, h), update, here),
                    slot,
                )

        loop(low, high, SWEEP_ROWS, body, SWEEP_UNROLL if slots <= 4 else 1)
        for slot in group:
            at_x, at_y, at_z = stations[slot]
            local = at_y - y_first

            @pl.when((local >= low) & (local < high))
            def _():
                shape = (1, layers, depth)
                there = (lax.broadcasted_iota(jnp.int32, shape, 1) == at_x) & (
                    lax.broadcasted_iota(jnp.int32, shape, 2) == at_z
                )
                here = slot, pl.ds(local + shift, 1)
                target[here] = jnp.where(there, 0.0, target[here])

    fields = [ping, pong]
    last = ROUNDS * SWEEPS - 1
    every = range(slots)
    for index in range(last):
        sweep(fields[index % 2], fields[(index + 1) % 2], index, rows - index, index // SWEEPS, 1, every)
    copies = []
    for slot in every:
        sweep(fields[last % 2], final, last, rows - last, last // SWEEPS, -last, [slot])
        loop(0, own_rows, 4, lambda row, size: flat.put(row, size, get(final, row + ADJ_HALO, size, slot)))
        for place in range(layers):
            staged[slot, place] = flat.get_layer(place, own_rows)
        copies.append(pltpu.make_async_copy(staged.at[slot], times_out.at[line ^ slot], sems.at[slot]))
        copies[-1].start()
    for copy in copies:
        copy.wait()


ADJ_ROWS = 4
ADJ_UNROLL = 8


def adjoint_kernel(layers, own_rows, grid_rows, slots, events, *refs):
    pays, (final, speed, count, delay_sum), refs = refs[:slots], refs[slots : slots + 4], refs[slots + 4 :]
    depth = final.shape[-1]
    parts = depth // LANES
    kernel_out, refs = refs[:layers], refs[layers:]
    weight, src, adj_a, adj_b, density, flat = refs
    together = weight.shape[0]
    flat = Flat(flat, layers)
    y_first = where_am_i(own_rows)[3]
    stations = [station_of(pay, events) for pay in pays]
    straight = [Straight(layers, parts, stations[slot], grid_rows) for slot in range(slots)]
    shift = HALO - ADJ_HALO
    rows = own_rows + 2 * ADJ_HALO

    def sums(ref, row, size, *lead):
        span = pl.ds(pl.multiple_of(row * layers, layers), size * layers)
        return [
            ref[(*lead, span, slice(p * LANES, (p + 1) * LANES))].reshape(size, layers, LANES)
            for p in range(parts)
        ]

    def make_source(group, row, size):
        for i in range(size):
            number = sums(count, row + i, 1)
            for slot in group:
                value = each(
                    lambda n, t, d, s: n * (t - d) - s,
                    number,
                    get(final, row + i, 1, slot),
                    straight[slot].row(y_first + shift + row + i),
                    sums(delay_sum, row + i, 1, slot),
                )
                put(src, row + i, 1, value, slot - group[0])

    def make_weight(group, row, size):
        grid = Grid(size, layers, depth)
        scale = each(lambda v: v * (1.0 / 6.0), get(speed, row + shift, size))
        for slot in group:
            field = get(final, row - 1, size + 2, slot)
            here = each(lambda f: f[1 : size + 1], field)

            def rise(value):
                return each(lambda v, h, s: jnp.maximum(v - h, 0.0) * s, value, here, scale)

            def keep(value, piece, edge):
                return [jnp.where(edge, 0.0, v) if p == piece else v for p, v in enumerate(value)]

            six = [
                grid.no_low(rise(grid.layer_before(here)), 0.0),
                grid.no_high(rise(grid.layer_after(here)), 0.0),
                rise(each(lambda f: f[:size], field)),
                rise(each(lambda f: f[2:], field)),
                keep(rise(grid.depth_before(here)), 0, grid.lane_low),
                keep(rise(grid.depth_after(here)), parts - 1, grid.lane_high),
            ]
            for n, value in enumerate(six):
                put(weight, row, size, value, slot - group[0], n)

    def multiply_add(value, factor, neighbour):
        return value + factor * neighbour

    def smooth(low, here, high):
        return (low + 2.0 * here + high) * 0.25

    def sweep(group, source, target, low, high):
        def body(row, size):
            grid = Grid(size, layers, depth)
            total = None if group[0] == 0 else get(density, row, size)
            for slot in range(len(group)):
                field = get(source, row - 1, size + 2, slot)
                here = each(lambda f: f[1 : size + 1], field)
                around = [
                    grid.layer_before(here),
                    grid.layer_after(here),
                    each(lambda f: f[:size], field),
                    each(lambda f: f[2:], field),
                    grid.depth_before(here),
                    grid.depth_after(here),
                ]
                value = get(src, row, size, slot)
                for n, neighbour in enumerate(around):
                    value = each(multiply_add, value, get(weight, row, size, slot, n), neighbour)
                if target is not None:
                    put(target, row, size, value, slot)
                else:
                    total = value if total is None else each(jnp.add, total, value)
            if target is None:
                if group[-1] == slots - 1:
                    value = each(lambda t, v: t / v, total, get(speed, row + shift, size))
                    low = grid.no_low(grid.layer_before(value), 0.0)
                    high = grid.no_high(grid.layer_after(value), 0.0)
                    total = each(smooth, low, value, high)
                put(density, row, size, total)

        loop(low, high, ADJ_ROWS, body, ADJ_UNROLL if slots <= 4 else 1)

    for first in range(0, slots, together):
        group = range(first, min(first + together, slots))
        loop(0, rows, 4, functools.partial(make_source, group))
        loop(1, rows - 1, 4, functools.partial(make_weight, group))
        fields = [src] + [(adj_a, adj_b)[i % 2] for i in range(ADJ_SWEEPS - 1)] + [None]
        for index in range(ADJ_SWEEPS):
            sweep(group, fields[index], fields[index + 1], index + 1, rows - 1 - index)

    def finish(row, size):
        grid = Grid(size, layers, depth)
        field = get(density, row + ADJ_SWEEPS, size + 2)
        value = each(lambda f: smooth(f[:size], f[1 : size + 1], f[2:]), field)
        low, high = grid.depth_before(value, 0.0), grid.depth_after(value, 0.0)
        flat.put(row, size, each(smooth, low, value, high))

    loop(0, own_rows, 4, finish)
    for m, out in enumerate(kernel_out):
        out[...] = flat.get_layer(lax.axis_index("space") ^ m, own_rows)


def join_kernel(times, *refs):
    blocks, (times_out, out, sems) = refs[:-3], refs[-3:]
    rows = blocks[0].shape[0]
    copies = [pltpu.make_async_copy(times, times_out, sems.at[0])]
    for m, block in enumerate(blocks):
        start = pl.multiple_of((lax.axis_index("space") ^ m) * rows, rows)
        copies.append(pltpu.make_async_copy(block, out.at[pl.ds(start, rows)], sems.at[m + 1]))
    for copy in copies:
        copy.start()
    for copy in copies:
        copy.wait()


def per_device(velocity, station_cells, event_cells, delays, active):
    _, grid_rows, depth = velocity.shape
    slots, layers = lax.axis_size("src"), lax.axis_size("space")
    chips = layers // 2
    events = event_cells.shape[1]
    line_rows = grid_rows // slots
    own_rows = line_rows // layers
    rows = own_rows + 2 * HALO
    adj_rows = own_rows + 2 * ADJ_HALO

    def to_line(array, j):
        return lax.ppermute(array, "src", [(i, i ^ j) for i in range(slots)])

    def to_chip(array, j):
        return lax.ppermute(array, "space", [(i, i ^ (2 * j)) for i in range(layers)])

    def to_core(array):
        return lax.ppermute(array, "space", [(i, i ^ 1) for i in range(layers)])

    f32 = jnp.float32
    def out(*shape):
        return jax.ShapeDtypeStruct(shape, f32)

    def scratch(*shape):
        return pltpu.VMEM(shape, f32)

    def field(*lead):
        return (*lead, layers, depth)

    other = to_core(velocity[0])
    active_other = to_core(active[:, 0])
    mine = [velocity[0], delays, station_cells, active[:, 0]]
    layer, delays, station_cells, active = call(
        fetch_kernel,
        "fetch",
        [jax.ShapeDtypeStruct(a.shape, a.dtype) for a in mine],
        mine,
        [pltpu.SemaphoreType.DMA((len(mine),))],
        hbm_in=range(len(mine)),
    )
    (payload,) = call(
        head_kernel,
        "head",
        [out(1, events + LANES * (1 + 2 * ROUNDS))],
        [delays, station_cells, active, active_other],
    )
    pays = [payload] + [to_line(payload, j) for j in range(1, slots)]

    height = 2 * rows + -(-slots * ROUNDS // 8) * 8
    packed = call(
        functools.partial(pack_kernel, rows, own_rows, slots),
        "pack",
        [out(height, depth)] * chips,
        [layer, other, *pays],
    )
    vel = [packed[0]] + [to_chip(packed[j], j) for j in range(1, chips)]

    pays, cells, _ = lax.optimization_barrier((pays, event_cells, packed[0]))
    chunk = events
    while (1 + 2 * slots) * adj_rows * layers * chunk > EVENT_CHUNK * 2**11:
        chunk //= 2
    count, delay_sum = call(
        functools.partial(scatter_kernel, layers, own_rows, events),
        "events",
        [out(adj_rows * layers, depth), out(slots, adj_rows * layers, depth)],
        [cells, *pays],
        [pltpu.VMEM(((1 + 2 * slots) * adj_rows * layers, chunk), jnp.bfloat16)],
        microseconds=3.0,
    )

    pays, count, delay_sum = lax.optimization_barrier((pays, count, delay_sum))

    together = min(slots, 4)
    flat = scratch(depth // LANES, rows * layers, LANES)
    times, final, speed = call(
        functools.partial(sweep_kernel, layers, own_rows, grid_rows, slots, chips, events),
        "sweeps",
        [
            out(slots, layers, own_rows, depth),
            out(*field(slots, adj_rows)),
            out(*field(rows)),
        ],
        [*pays, *vel],
        [
            scratch(*field(rows)),
            scratch(*field(rows)),
            scratch(*field(rows)),
            scratch(*field(slots, rows + 2)),
            scratch(*field(slots, rows + 2)),
            scratch(slots * ROUNDS, layers, LANES),
            scratch(slots, ROUNDS, rows, layers, LANES),
            flat,
            scratch(slots, layers, own_rows, depth),
            pltpu.SemaphoreType.DMA((slots,)),
        ],
        hbm_out=(0,),
        microseconds=10.0,
    )
    kernel = call(
        functools.partial(adjoint_kernel, layers, own_rows, grid_rows, slots, events),
        "adjoint",
        [out(own_rows, depth)] * layers,
        [*pays, final, speed, count, delay_sum],
        [
            scratch(*field(together, 6, adj_rows)),
            scratch(*field(together, adj_rows)),
            scratch(*field(together, adj_rows)),
            scratch(*field(together, adj_rows)),
            scratch(*field(adj_rows)),
            flat,
        ],
        microseconds=7.0,
    )

    times = lax.all_to_all(
        times.reshape(slots * layers, own_rows, depth), ("src", "space"), 0, 0, tiled=True
    )
    blocks = [kernel[0]] + [
        lax.ppermute(kernel[m], "space", [(i, i ^ m) for i in range(layers)])
        for m in range(1, layers)
    ]
    times, kernel = call(
        join_kernel,
        "join",
        [out(grid_rows, depth), out(line_rows, depth)],
        [times.reshape(grid_rows, depth), *blocks],
        [pltpu.SemaphoreType.DMA((1 + layers,))],
        in_place=range(1 + layers),
        hbm_out=(0, 1),
    )
    return (times.reshape(1, 1, grid_rows, depth), kernel.reshape(1, line_rows, depth))


def solution(mesh):
    return jax.shard_map(
        per_device,
        mesh=mesh,
        in_specs=(
            P("space", None, None),
            P("src", None),
            P(),
            P("src", None),
            P(None, "src", "space", None),
        ),
        out_specs=(P("src", "space", None, None), P("space", "src", None)),
        check_vma=False,
    )
```

```python
import functools
import math

import jax
import jax.numpy as jnp
from jax import lax
from jax.experimental import pallas as pl
from jax.experimental.pallas import tpu as pltpu
from jax.sharding import PartitionSpec as P

TY = 32
ROUNDS = 2
SWEEPS = 2
ADJ_SWEEPS = 4
BIG = 1000000.0
LANES = 128

HALO = ROUNDS * SWEEPS + ADJ_SWEEPS
ADJ_HALO = ADJ_SWEEPS + 1

VMEM = pltpu.VMEM
SMEM = pltpu.SMEM


def spec(space):
    return pl.BlockSpec(memory_space=space)


def call(body, name, outs, operands, scratch=(), microseconds=1.0, in_place=(), hbm_in=(), hbm_out=()):
    held = [a for a in (*operands, *outs, *scratch) if len(a.shape) > 1]
    limit = 4 * 2**20 + sum(4 * math.prod((*a.shape[:-2], -(-math.prod(a.shape[-2:-1]) // 8) * 8, max(a.shape[-1], 128))) for a in held)
    return pl.pallas_call(
        body,
        out_shape=list(outs),
        in_specs=[
            spec(
                pltpu.HBM if i in hbm_in else pl.ANY if i in in_place else SMEM if a.ndim == 1 else VMEM
            )
            for i, a in enumerate(operands)
        ],
        out_specs=[spec(pltpu.HBM if i in hbm_out else VMEM) for i in range(len(outs))],
        scratch_shapes=list(scratch),
        compiler_params=pltpu.CompilerParams(vmem_limit_bytes=limit),
        cost_estimate=pl.CostEstimate(
            flops=0, bytes_accessed=int(microseconds * 3.5e6), transcendentals=0
        ),
        name=name,
    )(*[
        pltpu.with_memory_space_constraint(a, pltpu.HBM) if i in hbm_in else a
        for i, a in enumerate(operands)
    ])


def where_am_i(own_rows):
    place = lax.axis_index("space")
    line_row = lax.axis_index("src") * (lax.axis_size("space") * own_rows)
    first = line_row + place * own_rows - HALO
    return lax.div(place, 2), lax.rem(place, 2), line_row, first


def station_of(pay, events):
    cell = pay[0:1, events : events + LANES].astype(jnp.int32)
    return [cell[0, i] for i in range(3)]


def fetch_kernel(*refs):
    ins, (*outs, sems) = refs[: len(refs) // 2], refs[len(refs) // 2 :]
    copies = [pltpu.make_async_copy(a, b, sems.at[i]) for i, (a, b) in enumerate(zip(ins, outs))]
    for copy in copies:
        copy.start()
    for copy in copies:
        copy.wait()


def head_kernel(delays, station, active, active_other, out):
    events = delays.shape[1]
    out[:, :events] = delays[...]
    out[:, events:] = jnp.zeros((1, out.shape[1] - events), jnp.float32)
    at = events
    out[:, at : at + 3] = station[...].astype(jnp.float32)
    for source in (active, active_other):
        for part in range(ROUNDS):
            at += LANES
            out[:, at : at + source.shape[-1]] = source[part].astype(jnp.float32)


def pack_kernel(rows, own_rows, slots, own, other, *refs):
    chip, core, line_row, _ = where_am_i(own_rows)
    pays, outs = refs[:slots], refs[slots:]
    total = own.shape[0]
    chunk = math.gcd(own_rows, 8)
    at = pays[0].shape[1] - 2 * ROUNDS * LANES
    for j, out in enumerate(outs):
        first = line_row + ((chip ^ j) * 2 + core) * own_rows - HALO
        for piece in range(rows // chunk):
            start = jnp.clip(first + piece * chunk, 0, total - chunk)
            start = pl.multiple_of(start, chunk)
            out[piece * chunk : (piece + 1) * chunk, :] = own[pl.ds(start, chunk), :]
            out[rows + piece * chunk : rows + (piece + 1) * chunk, :] = other[pl.ds(start, chunk), :]
        out[2 * rows :, :] = jnp.zeros_like(out[2 * rows :, :])
        for slot, pay in enumerate(pays):
            for part in range(ROUNDS):
                row = 2 * rows + slot * ROUNDS + part
                for c in range(2):
                    tile = at + (c * ROUNDS + part) * LANES
                    out[row : row + 1, c * LANES : (c + 1) * LANES] = pay[:, tile : tile + LANES]


EVENT_CHUNK = 2048


def scatter_kernel(layers, own_rows, grid_rows, events, cells, *refs):
    slots = len(refs) - 4
    pays, (count, delay_sum, start, left) = refs[:slots], refs[slots:]
    y_first = where_am_i(own_rows)[3]
    first_row = y_first + HALO - ADJ_HALO
    rows, parts = own_rows + 2 * HALO, start.shape[-1] // LANES

    straight = [Straight(layers, parts, station_of(pays[slot], events), grid_rows) for slot in range(slots)]

    def fill(row, size):
        for i in range(size):
            for slot in range(slots):
                put(start, row + i, 1, straight[slot].row(y_first - 1 + row + i), slot)

    loop(0, rows + 2, 4, fill)

    height, width = count.shape
    chunk = left.shape[1]
    steps = events // chunk
    contract = (((1,), (1,)), ((), ()))

    def step(index, carry):
        start = pl.multiple_of(index * chunk, chunk)
        where_x = cells[0:1, pl.ds(start, chunk)]
        where_y = cells[1:2, pl.ds(start, chunk)] - first_row
        where_z = cells[2:3, pl.ds(start, chunk)]
        at = jnp.where(where_y >= 0, where_y * layers + where_x, -1)
        hit = lax.broadcasted_iota(jnp.int32, (height, chunk), 0) == at
        hit = hit.astype(jnp.bfloat16)
        left[:height, :] = hit
        for slot in range(slots):
            delay = pays[slot][:, pl.ds(start, chunk)]
            high = delay.astype(jnp.bfloat16)
            low = (delay - high.astype(jnp.float32)).astype(jnp.bfloat16)
            for half, factor in enumerate((high, low)):
                row = (1 + 2 * slot + half) * height
                left[row : row + height, :] = hit * factor
        depth = lax.broadcasted_iota(jnp.int32, (width, chunk), 0) == where_z
        depth = depth.astype(jnp.bfloat16)
        value = lax.dot_general(left[...], depth, contract, preferred_element_type=jnp.float32)
        pieces = [value[i * height : (i + 1) * height] for i in range(1 + 2 * slots)]
        sums = [pieces[1 + 2 * slot] + pieces[2 + 2 * slot] for slot in range(slots)]
        if steps == 1:
            count[...] = pieces[0]
            for slot in range(slots):
                delay_sum[slot] = sums[slot]
        else:
            count[...] += pieces[0]
            for slot in range(slots):
                delay_sum[slot] += sums[slot]
        return carry

    if steps == 1:
        step(0, 0)
    else:
        count[...] = jnp.zeros_like(count)
        delay_sum[...] = jnp.zeros_like(delay_sum)
        lax.fori_loop(0, steps, step, 0)


def get(ref, row, size, *lead):
    index = (*lead, pl.ds(row, size))
    return [
        ref[(*index, slice(None), slice(p, p + LANES))] for p in range(0, ref.shape[-1], LANES)
    ]


def put(ref, row, size, value, *lead):
    index = (*lead, pl.ds(row, size))
    for p, piece in enumerate(value):
        ref[(*index, slice(None), slice(p * LANES, (p + 1) * LANES))] = piece


def each(function, *values):
    return [function(*pieces) for pieces in zip(*values)]


def loop(low, high, size, body, unroll=16):
    steps = (high - low) // size
    if steps <= unroll:
        for i in range(steps):
            body(low + i * size, size)
    else:
        lax.fori_loop(
            0,
            steps,
            lambda i, carry: (body(low + i * size, size), carry)[1],
            0,
            unroll=unroll,
        )
    if low + steps * size < high:
        loop(low + steps * size, high, max(size // 2, 1), body)


class Grid:
    def __init__(self, size, layers, depth):
        shape = (size, layers, LANES)
        layer = lax.broadcasted_iota(jnp.int32, shape, 1)
        lane = lax.broadcasted_iota(jnp.int32, shape, 2)
        self.layers = layers
        self.layer_low, self.layer_high = layer == 0, layer == layers - 1
        self.lane_low, self.lane_high = lane == 0, lane == LANES - 1

    def layer_before(self, value):
        return [pltpu.roll(piece, 1, 1) for piece in value]

    def layer_after(self, value):
        return [pltpu.roll(piece, self.layers - 1, 1) for piece in value]

    def depth_before(self, value, fill=None):
        moved = [pltpu.roll(piece, 1, 2) for piece in value]
        first = moved[0] if fill is None else jnp.where(self.lane_low, fill, moved[0])
        rest = [
            jnp.where(self.lane_low, low, here) for low, here in zip(moved[:-1], moved[1:])
        ]
        return [first] + rest

    def depth_after(self, value, fill=None):
        moved = [pltpu.roll(piece, LANES - 1, 2) for piece in value]
        last = moved[-1] if fill is None else jnp.where(self.lane_high, fill, moved[-1])
        rest = [
            jnp.where(self.lane_high, high, here) for here, high in zip(moved[:-1], moved[1:])
        ]
        return rest + [last]

    def no_low(self, value, fill):
        return [jnp.where(self.layer_low, fill, piece) for piece in value]

    def no_high(self, value, fill):
        return [jnp.where(self.layer_high, fill, piece) for piece in value]


class Flat:
    def __init__(self, ref, layers):
        self.ref, self.layers, self.parts = ref, layers, ref.shape[0]

    def put_layer(self, place, rows, value):
        for p in range(self.parts):
            self.ref.at[p][pl.ds(place, rows, stride=self.layers), :] = value[
                :, p * LANES : (p + 1) * LANES
            ]

    def get_layer(self, place, rows):
        pieces = [
            self.ref.at[p][pl.ds(place, rows, stride=self.layers), :] for p in range(self.parts)
        ]
        return jnp.concatenate(pieces, axis=1)

    def span(self, row, size):
        return pl.ds(pl.multiple_of(row * self.layers, self.layers), size * self.layers)

    def get(self, row, size):
        return [
            self.ref[p, self.span(row, size), :].reshape(size, self.layers, LANES)
            for p in range(self.parts)
        ]

    def put(self, row, size, value):
        for p in range(self.parts):
            self.ref[p, self.span(row, size), :] = value[p].reshape(size * self.layers, LANES)


def root_of(value):
    value = jnp.maximum(value, 1e-30)
    return value * lax.rsqrt(value)


class Straight:
    def __init__(self, layers, parts, at, grid_rows):
        shape = (1, layers, LANES)
        self.at_y, self.grid_rows = at[1], grid_rows
        dx = (lax.broadcasted_iota(jnp.int32, shape, 1) - at[0]).astype(jnp.float32)
        self.across = []
        for p in range(parts):
            dz = lax.broadcasted_iota(jnp.int32, shape, 2) + (p * LANES - at[2])
            dz = dz.astype(jnp.float32)
            self.across.append(dx * dx + dz * dz)

    def row(self, y):
        gap = y - self.at_y
        far = (gap * gap).astype(jnp.float32)
        inside = (y >= 0) & (y < self.grid_rows)
        return [jnp.where(inside, root_of(a + far), BIG) for a in self.across]


def local_solve(near_x, near_y, near_z, cost, twice, one_half):
    small = jnp.minimum(near_x, near_y)
    large = jnp.maximum(near_x, near_y)
    lowest = jnp.minimum(small, near_z)
    highest = jnp.maximum(large, near_z)
    middle = jnp.maximum(small, jnp.minimum(large, near_z))
    first_gap = middle - lowest
    second_gap = highest - lowest
    square = first_gap * first_gap
    double = 0.5 * (first_gap + root_of(twice - square))
    rest = square + second_gap * (second_gap - first_gap)
    root = root_of(one_half - rest)
    triple = (first_gap + second_gap) * (1.0 / 3.0) + root * (math.sqrt(2.0) / 3.0)
    over = jnp.where(double <= second_gap, double, triple)
    return lowest + jnp.where(cost <= first_gap, cost, over)


SWEEP_ROWS = 2
SWEEP_UNROLL = 16


def sweep_kernel(layers, own_rows, grid_rows, slots, chips, events, *refs):
    rows = own_rows + 2 * HALO
    pays, start, refs = refs[:slots], refs[slots], refs[slots + 1 :]
    depth = start.shape[-1]
    parts = depth // LANES
    vel_in, refs = refs[:chips][::-1], refs[chips:]
    times_out, final, speed, refs = refs[0], refs[1], refs[2], refs[3:]
    cost, twice, one_half, ping, pong, acts, mask, flat, staged, sems = refs
    flat = Flat(flat, layers)
    line = lax.axis_index("src")
    chip, core, _, y_first = where_am_i(own_rows)
    stations = [station_of(pay, events) for pay in pays]

    for j in range(chips):
        for c in range(2):
            place = (chip ^ j) * 2 + (core ^ c)
            flat.put_layer(place, rows, vel_in[j][c * rows : (c + 1) * rows, :])
            for slot in range(slots):
                for part in range(ROUNDS):
                    row = 2 * rows + slot * ROUNDS + part
                    acts[slot * ROUNDS + part, pl.ds(place, 1), :] = vel_in[j][
                        row : row + 1, c * LANES : (c + 1) * LANES
                    ]

    def prepare(row, size):
        value = flat.get(row, size)
        slow = each(lambda v: 1.0 / v, value)
        put(speed, row, size, value)
        put(cost, row, size, slow)
        put(twice, row, size, each(lambda f: 2.0 * (f * f), slow))
        put(one_half, row, size, each(lambda f: 1.5 * (f * f), slow))

    loop(0, rows, 4, prepare)

    lane_iota = lax.broadcasted_iota(jnp.int32, (layers, LANES), 1)
    tile_first = (y_first + TY) // TY - 1
    tile_span = (rows + TY - 2) // TY + 1
    for slot in range(slots):
        for part in range(ROUNDS):
            act = acts[slot * ROUNDS + part]
            columns = []
            for t in range(tile_span):
                here = lane_iota == tile_first + t
                picked = jnp.sum(jnp.where(here, act, 0.0), axis=1, keepdims=True)
                columns.append(jnp.broadcast_to(picked, (layers, LANES)))
            for i in range(rows):
                value = columns[0]
                for t in range(1, tile_span):
                    value = jnp.where(y_first + i >= (tile_first + t) * TY, columns[t], value)
                mask[slot, part, i] = value

    def sweep(source, target, low, high, part, shift, group):
        def body(row, size):
            grid = Grid(size, layers, depth)
            costs = get(cost, row, size), get(twice, row, size), get(one_half, row, size)
            for slot in group:
                field = get(source, row, size + 2, slot)
                here = each(lambda f: f[1 : size + 1], field)
                near_y = each(lambda f: jnp.minimum(f[:size], f[2:]), field)
                near_x = each(
                    jnp.minimum,
                    grid.no_low(grid.layer_before(here), BIG),
                    grid.no_high(grid.layer_after(here), BIG),
                )
                near_z = each(
                    jnp.minimum, grid.depth_before(here, BIG), grid.depth_after(here, BIG)
                )
                update = each(local_solve, near_x, near_y, near_z, *costs)
                on = mask[slot, part, pl.ds(row, size)] > 0.0
                put(
                    target,
                    row + shift,
                    size,
                    each(lambda u, h: jnp.where(on, u, h), update, here),
                    slot,
                )

        loop(low, high, SWEEP_ROWS, body, SWEEP_UNROLL if slots <= 4 else 1)
        for slot in group:
            at_x, at_y, at_z = stations[slot]
            local = at_y - y_first

            @pl.when((local >= low) & (local < high))
            def _():
                shape = (1, layers, depth)
                there = (lax.broadcasted_iota(jnp.int32, shape, 1) == at_x) & (
                    lax.broadcasted_iota(jnp.int32, shape, 2) == at_z
                )
                here = slot, pl.ds(local + shift, 1)
                target[here] = jnp.where(there, 0.0, target[here])

    fields = [start] + [(pong, ping)[i % 2] for i in range(ROUNDS * SWEEPS - 1)]
    last = ROUNDS * SWEEPS - 1
    every = range(slots)
    for index in range(last):
        sweep(fields[index], fields[index + 1], index, rows - index, index // SWEEPS, 1, every)
    copies = []
    for slot in every:
        sweep(fields[last], final, last, rows - last, last // SWEEPS, -last, [slot])
        loop(0, own_rows, 4, lambda row, size: flat.put(row, size, get(final, row + ADJ_HALO, size, slot)))
        for place in range(layers):
            staged[slot, place] = flat.get_layer(place, own_rows)
        copies.append(pltpu.make_async_copy(staged.at[slot], times_out.at[line ^ slot], sems.at[slot]))
        copies[-1].start()
    for copy in copies:
        copy.wait()


ADJ_ROWS = 4
ADJ_UNROLL = 8


def adjoint_kernel(layers, own_rows, grid_rows, slots, events, *refs):
    pays, (final, speed, count, delay_sum), refs = refs[:slots], refs[slots : slots + 4], refs[slots + 4 :]
    depth = final.shape[-1]
    parts = depth // LANES
    kernel_out, refs = refs[:layers], refs[layers:]
    weight, src, adj_a, adj_b, density, flat = refs
    together = weight.shape[0]
    flat = Flat(flat, layers)
    y_first = where_am_i(own_rows)[3]
    stations = [station_of(pay, events) for pay in pays]
    straight = [Straight(layers, parts, stations[slot], grid_rows) for slot in range(slots)]
    shift = HALO - ADJ_HALO
    rows = own_rows + 2 * ADJ_HALO

    def sums(ref, row, size, *lead):
        span = pl.ds(pl.multiple_of(row * layers, layers), size * layers)
        return [
            ref[(*lead, span, slice(p * LANES, (p + 1) * LANES))].reshape(size, layers, LANES)
            for p in range(parts)
        ]

    def make_source(group, row, size):
        for i in range(size):
            number = sums(count, row + i, 1)
            for slot in group:
                value = each(
                    lambda n, t, d, s: n * (t - d) - s,
                    number,
                    get(final, row + i, 1, slot),
                    straight[slot].row(y_first + shift + row + i),
                    sums(delay_sum, row + i, 1, slot),
                )
                put(src, row + i, 1, value, slot - group[0])

    def make_weight(group, row, size):
        grid = Grid(size, layers, depth)
        scale = each(lambda v: v * (1.0 / 6.0), get(speed, row + shift, size))
        for slot in group:
            field = get(final, row - 1, size + 2, slot)
            here = each(lambda f: f[1 : size + 1], field)

            def rise(value):
                return each(lambda v, h, s: jnp.maximum(v - h, 0.0) * s, value, here, scale)

            def keep(value, piece, edge):
                return [jnp.where(edge, 0.0, v) if p == piece else v for p, v in enumerate(value)]

            six = [
                grid.no_low(rise(grid.layer_before(here)), 0.0),
                grid.no_high(rise(grid.layer_after(here)), 0.0),
                rise(each(lambda f: f[:size], field)),
                rise(each(lambda f: f[2:], field)),
                keep(rise(grid.depth_before(here)), 0, grid.lane_low),
                keep(rise(grid.depth_after(here)), parts - 1, grid.lane_high),
            ]
            for n, value in enumerate(six):
                put(weight, row, size, value, slot - group[0], n)

    def multiply_add(value, factor, neighbour):
        return value + factor * neighbour

    def smooth(low, here, high):
        return (low + 2.0 * here + high) * 0.25

    def sweep(group, source, target, low, high):
        def body(row, size):
            grid = Grid(size, layers, depth)
            total = None if group[0] == 0 else get(density, row, size)
            for slot in range(len(group)):
                field = get(source, row - 1, size + 2, slot)
                here = each(lambda f: f[1 : size + 1], field)
                around = [
                    grid.layer_before(here),
                    grid.layer_after(here),
                    each(lambda f: f[:size], field),
                    each(lambda f: f[2:], field),
                    grid.depth_before(here),
                    grid.depth_after(here),
                ]
                value = get(src, row, size, slot)
                for n, neighbour in enumerate(around):
                    value = each(multiply_add, value, get(weight, row, size, slot, n), neighbour)
                if target is not None:
                    put(target, row, size, value, slot)
                else:
                    total = value if total is None else each(jnp.add, total, value)
            if target is None:
                if group[-1] == slots - 1:
                    value = each(lambda t, v: t / v, total, get(speed, row + shift, size))
                    low = grid.no_low(grid.layer_before(value), 0.0)
                    high = grid.no_high(grid.layer_after(value), 0.0)
                    total = each(smooth, low, value, high)
                put(density, row, size, total)

        loop(low, high, ADJ_ROWS, body, ADJ_UNROLL if slots <= 4 else 1)

    for first in range(0, slots, together):
        group = range(first, min(first + together, slots))
        loop(0, rows, 4, functools.partial(make_source, group))
        loop(1, rows - 1, 4, functools.partial(make_weight, group))
        fields = [src] + [(adj_a, adj_b)[i % 2] for i in range(ADJ_SWEEPS - 1)] + [None]
        for index in range(ADJ_SWEEPS):
            sweep(group, fields[index], fields[index + 1], index + 1, rows - 1 - index)

    def finish(row, size):
        grid = Grid(size, layers, depth)
        field = get(density, row + ADJ_SWEEPS, size + 2)
        value = each(lambda f: smooth(f[:size], f[1 : size + 1], f[2:]), field)
        low, high = grid.depth_before(value, 0.0), grid.depth_after(value, 0.0)
        flat.put(row, size, each(smooth, low, value, high))

    loop(0, own_rows, 4, finish)
    for m, out in enumerate(kernel_out):
        out[...] = flat.get_layer(lax.axis_index("space") ^ m, own_rows)


def join_kernel(times, *refs):
    blocks, (times_out, out, sems) = refs[:-3], refs[-3:]
    rows = blocks[0].shape[0]
    copies = [pltpu.make_async_copy(times, times_out, sems.at[0])]
    for m, block in enumerate(blocks):
        start = pl.multiple_of((lax.axis_index("space") ^ m) * rows, rows)
        copies.append(pltpu.make_async_copy(block, out.at[pl.ds(start, rows)], sems.at[m + 1]))
    for copy in copies:
        copy.start()
    for copy in copies:
        copy.wait()


def per_device(velocity, station_cells, event_cells, delays, active):
    _, grid_rows, depth = velocity.shape
    slots, layers = lax.axis_size("src"), lax.axis_size("space")
    chips = layers // 2
    events = event_cells.shape[1]
    line_rows = grid_rows // slots
    own_rows = line_rows // layers
    rows = own_rows + 2 * HALO
    adj_rows = own_rows + 2 * ADJ_HALO

    def to_line(array, j):
        return lax.ppermute(array, "src", [(i, i ^ j) for i in range(slots)])

    def to_chip(array, j):
        return lax.ppermute(array, "space", [(i, i ^ (2 * j)) for i in range(layers)])

    def to_core(array):
        return lax.ppermute(array, "space", [(i, i ^ 1) for i in range(layers)])

    f32 = jnp.float32
    def out(*shape):
        return jax.ShapeDtypeStruct(shape, f32)

    def scratch(*shape):
        return pltpu.VMEM(shape, f32)

    def field(*lead):
        return (*lead, layers, depth)

    other = to_core(velocity[0])
    active_other = to_core(active[:, 0])
    mine = [velocity[0], delays, station_cells, active[:, 0]]
    layer, delays, station_cells, active = call(
        fetch_kernel,
        "fetch",
        [jax.ShapeDtypeStruct(a.shape, a.dtype) for a in mine],
        mine,
        [pltpu.SemaphoreType.DMA((len(mine),))],
        hbm_in=range(len(mine)),
    )
    (payload,) = call(
        head_kernel,
        "head",
        [out(1, events + LANES * (1 + 2 * ROUNDS))],
        [delays, station_cells, active, active_other],
    )
    pays = [payload] + [to_line(payload, j) for j in range(1, slots)]

    height = 2 * rows + -(-slots * ROUNDS // 8) * 8
    packed = call(
        functools.partial(pack_kernel, rows, own_rows, slots),
        "pack",
        [out(height, depth)] * chips,
        [layer, other, *pays],
    )
    vel = [to_chip(packed[j], j) for j in range(chips - 1, 0, -1)] + [packed[0]]

    pays, cells, _ = lax.optimization_barrier((pays, event_cells, packed[0]))
    chunk = events
    while (1 + 2 * slots) * adj_rows * layers * chunk > EVENT_CHUNK * 2**11:
        chunk //= 2
    count, delay_sum, start = call(
        functools.partial(scatter_kernel, layers, own_rows, grid_rows, events),
        "events",
        [
            out(adj_rows * layers, depth),
            out(slots, adj_rows * layers, depth),
            out(*field(slots, rows + 2)),
        ],
        [cells, *pays],
        [pltpu.VMEM(((1 + 2 * slots) * adj_rows * layers, chunk), jnp.bfloat16)],
        microseconds=3.0,
    )

    pays, count, delay_sum, start = lax.optimization_barrier((pays, count, delay_sum, start))

    together = min(slots, 4)
    flat = scratch(depth // LANES, rows * layers, LANES)
    times, final, speed = call(
        functools.partial(sweep_kernel, layers, own_rows, grid_rows, slots, chips, events),
        "sweeps",
        [
            out(slots, layers, own_rows, depth),
            out(*field(slots, adj_rows)),
            out(*field(rows)),
        ],
        [*pays, start, *vel],
        [
            scratch(*field(rows)),
            scratch(*field(rows)),
            scratch(*field(rows)),
            scratch(*field(slots, rows + 2)),
            scratch(*field(slots, rows + 2)),
            scratch(slots * ROUNDS, layers, LANES),
            scratch(slots, ROUNDS, rows, layers, LANES),
            flat,
            scratch(slots, layers, own_rows, depth),
            pltpu.SemaphoreType.DMA((slots,)),
        ],
        hbm_out=(0,),
        microseconds=10.0,
    )
    kernel = call(
        functools.partial(adjoint_kernel, layers, own_rows, grid_rows, slots, events),
        "adjoint",
        [out(own_rows, depth)] * layers,
        [*pays, final, speed, count, delay_sum],
        [
            scratch(*field(together, 6, adj_rows)),
            scratch(*field(together, adj_rows)),
            scratch(*field(together, adj_rows)),
            scratch(*field(together, adj_rows)),
            scratch(*field(adj_rows)),
            flat,
        ],
        microseconds=7.0,
    )

    times = lax.all_to_all(
        times.reshape(slots * layers, own_rows, depth), ("src", "space"), 0, 0, tiled=True
    )
    blocks = [kernel[0]] + [
        lax.ppermute(kernel[m], "space", [(i, i ^ m) for i in range(layers)])
        for m in range(1, layers)
    ]
    times, kernel = call(
        join_kernel,
        "join",
        [out(grid_rows, depth), out(line_rows, depth)],
        [times.reshape(grid_rows, depth), *blocks],
        [pltpu.SemaphoreType.DMA((1 + layers,))],
        in_place=range(1 + layers),
        hbm_out=(0, 1),
    )
    return (times.reshape(1, 1, grid_rows, depth), kernel.reshape(1, line_rows, depth))


def solution(mesh):
    return jax.shard_map(
        per_device,
        mesh=mesh,
        in_specs=(
            P("space", None, None),
            P("src", None),
            P(),
            P("src", None),
            P(None, "src", "space", None),
        ),
        out_specs=(P("src", "space", None, None), P("space", "src", None)),
        check_vma=False,
    )
```

```python
import functools
import math

import jax
import jax.numpy as jnp
from jax import lax
from jax.experimental import pallas as pl
from jax.experimental.pallas import tpu as pltpu
from jax.sharding import PartitionSpec as P

TY = 32
ROUNDS = 2
SWEEPS = 2
ADJ_SWEEPS = 4
BIG = 1000000.0
LANES = 128

HALO = ROUNDS * SWEEPS + ADJ_SWEEPS
ADJ_HALO = ADJ_SWEEPS + 1

VMEM = pltpu.VMEM
SMEM = pltpu.SMEM


def spec(space):
    return pl.BlockSpec(memory_space=space)


def call(body, name, outs, operands, scratch=(), microseconds=1.0, in_place=(), hbm_in=(), hbm_out=()):
    held = [a for a in (*operands, *outs, *scratch) if len(a.shape) > 1]
    limit = 4 * 2**20 + sum(4 * math.prod((*a.shape[:-2], -(-math.prod(a.shape[-2:-1]) // 8) * 8, max(a.shape[-1], 128))) for a in held)
    return pl.pallas_call(
        body,
        out_shape=list(outs),
        in_specs=[
            spec(
                pltpu.HBM if i in hbm_in else pl.ANY if i in in_place else SMEM if a.ndim == 1 else VMEM
            )
            for i, a in enumerate(operands)
        ],
        out_specs=[spec(pltpu.HBM if i in hbm_out else VMEM) for i in range(len(outs))],
        scratch_shapes=list(scratch),
        compiler_params=pltpu.CompilerParams(vmem_limit_bytes=limit),
        cost_estimate=pl.CostEstimate(
            flops=0, bytes_accessed=int(microseconds * 3.5e6), transcendentals=0
        ),
        name=name,
    )(*[
        pltpu.with_memory_space_constraint(a, pltpu.HBM) if i in hbm_in else a
        for i, a in enumerate(operands)
    ])


def where_am_i(own_rows):
    place = lax.axis_index("space")
    line_row = lax.axis_index("src") * (lax.axis_size("space") * own_rows)
    first = line_row + place * own_rows - HALO
    return lax.div(place, 2), lax.rem(place, 2), line_row, first


def station_of(pay, events):
    cell = pay[0:1, events : events + LANES].astype(jnp.int32)
    return [cell[0, i] for i in range(3)]


def fetch_kernel(*refs):
    ins, (*outs, sems) = refs[: len(refs) // 2], refs[len(refs) // 2 :]
    copies = [pltpu.make_async_copy(a, b, sems.at[i]) for i, (a, b) in enumerate(zip(ins, outs))]
    for copy in copies:
        copy.start()
    for copy in copies:
        copy.wait()


def head_kernel(delays, station, active, active_other, out):
    events = delays.shape[1]
    out[:, :events] = delays[...]
    out[:, events:] = jnp.zeros((1, out.shape[1] - events), jnp.float32)
    at = events
    out[:, at : at + 3] = station[...].astype(jnp.float32)
    for source in (active, active_other):
        for part in range(ROUNDS):
            at += LANES
            out[:, at : at + source.shape[-1]] = source[part].astype(jnp.float32)


def pack_kernel(rows, own_rows, slots, own, other, *refs):
    chip, core, line_row, _ = where_am_i(own_rows)
    pays, outs = refs[:slots], refs[slots:]
    total = own.shape[0]
    chunk = math.gcd(own_rows, 8)
    at = pays[0].shape[1] - 2 * ROUNDS * LANES
    for j, out in enumerate(outs):
        first = line_row + ((chip ^ j) * 2 + core) * own_rows - HALO
        for piece in range(rows // chunk):
            start = jnp.clip(first + piece * chunk, 0, total - chunk)
            start = pl.multiple_of(start, chunk)
            out[piece * chunk : (piece + 1) * chunk, :] = own[pl.ds(start, chunk), :]
            out[rows + piece * chunk : rows + (piece + 1) * chunk, :] = other[pl.ds(start, chunk), :]
        out[2 * rows :, :] = jnp.zeros_like(out[2 * rows :, :])
        for slot, pay in enumerate(pays):
            for part in range(ROUNDS):
                row = 2 * rows + slot * ROUNDS + part
                for c in range(2):
                    tile = at + (c * ROUNDS + part) * LANES
                    out[row : row + 1, c * LANES : (c + 1) * LANES] = pay[:, tile : tile + LANES]


EVENT_CHUNK = 2048


def scatter_kernel(layers, own_rows, grid_rows, events, cells, *refs):
    slots = len(refs) - 4
    pays, (count, delay_sum, start, left) = refs[:slots], refs[slots:]
    y_first = where_am_i(own_rows)[3]
    first_row = y_first + HALO - ADJ_HALO
    rows, parts = own_rows + 2 * HALO, start.shape[-1] // LANES

    straight = [Straight(layers, parts, station_of(pays[slot], events), grid_rows) for slot in range(slots)]

    def fill(row, size):
        for i in range(size):
            for slot in range(slots):
                put(start, row + i, 1, straight[slot].row(y_first - 1 + row + i), slot)

    loop(0, rows + 2, 4, fill)

    height, width = count.shape
    chunk = left.shape[1]
    steps = events // chunk
    contract = (((1,), (1,)), ((), ()))

    def step(index, carry):
        start = pl.multiple_of(index * chunk, chunk)
        where_x = cells[0:1, pl.ds(start, chunk)]
        where_y = cells[1:2, pl.ds(start, chunk)] - first_row
        where_z = cells[2:3, pl.ds(start, chunk)]
        at = jnp.where(where_y >= 0, where_y * layers + where_x, -1)
        hit = lax.broadcasted_iota(jnp.int32, (height, chunk), 0) == at
        hit = hit.astype(jnp.bfloat16)
        left[:height, :] = hit
        for slot in range(slots):
            delay = pays[slot][:, pl.ds(start, chunk)]
            high = delay.astype(jnp.bfloat16)
            low = (delay - high.astype(jnp.float32)).astype(jnp.bfloat16)
            for half, factor in enumerate((high, low)):
                row = (1 + 2 * slot + half) * height
                left[row : row + height, :] = hit * factor
        depth = lax.broadcasted_iota(jnp.int32, (width, chunk), 0) == where_z
        depth = depth.astype(jnp.bfloat16)
        value = lax.dot_general(left[...], depth, contract, preferred_element_type=jnp.float32)
        pieces = [value[i * height : (i + 1) * height] for i in range(1 + 2 * slots)]
        sums = [pieces[1 + 2 * slot] + pieces[2 + 2 * slot] for slot in range(slots)]
        if steps == 1:
            count[...] = pieces[0]
            for slot in range(slots):
                delay_sum[slot] = sums[slot]
        else:
            count[...] += pieces[0]
            for slot in range(slots):
                delay_sum[slot] += sums[slot]
        return carry

    if steps == 1:
        step(0, 0)
    else:
        count[...] = jnp.zeros_like(count)
        delay_sum[...] = jnp.zeros_like(delay_sum)
        lax.fori_loop(0, steps, step, 0)


def get(ref, row, size, *lead):
    index = (*lead, pl.ds(row, size))
    return [
        ref[(*index, slice(None), slice(p, p + LANES))] for p in range(0, ref.shape[-1], LANES)
    ]


def put(ref, row, size, value, *lead):
    index = (*lead, pl.ds(row, size))
    for p, piece in enumerate(value):
        ref[(*index, slice(None), slice(p * LANES, (p + 1) * LANES))] = piece


def each(function, *values):
    return [function(*pieces) for pieces in zip(*values)]


def loop(low, high, size, body, unroll=16):
    steps = (high - low) // size
    if steps <= unroll:
        for i in range(steps):
            body(low + i * size, size)
    else:
        lax.fori_loop(
            0,
            steps,
            lambda i, carry: (body(low + i * size, size), carry)[1],
            0,
            unroll=unroll,
        )
    if low + steps * size < high:
        loop(low + steps * size, high, max(size // 2, 1), body)


class Grid:
    def __init__(self, size, layers, depth):
        shape = (size, layers, LANES)
        layer = lax.broadcasted_iota(jnp.int32, shape, 1)
        lane = lax.broadcasted_iota(jnp.int32, shape, 2)
        self.layers = layers
        self.layer_low, self.layer_high = layer == 0, layer == layers - 1
        self.lane_low, self.lane_high = lane == 0, lane == LANES - 1

    def layer_before(self, value):
        return [pltpu.roll(piece, 1, 1) for piece in value]

    def layer_after(self, value):
        return [pltpu.roll(piece, self.layers - 1, 1) for piece in value]

    def depth_before(self, value, fill=None):
        moved = [pltpu.roll(piece, 1, 2) for piece in value]
        first = moved[0] if fill is None else jnp.where(self.lane_low, fill, moved[0])
        rest = [
            jnp.where(self.lane_low, low, here) for low, here in zip(moved[:-1], moved[1:])
        ]
        return [first] + rest

    def depth_after(self, value, fill=None):
        moved = [pltpu.roll(piece, LANES - 1, 2) for piece in value]
        last = moved[-1] if fill is None else jnp.where(self.lane_high, fill, moved[-1])
        rest = [
            jnp.where(self.lane_high, high, here) for here, high in zip(moved[:-1], moved[1:])
        ]
        return rest + [last]

    def no_low(self, value, fill):
        return [jnp.where(self.layer_low, fill, piece) for piece in value]

    def no_high(self, value, fill):
        return [jnp.where(self.layer_high, fill, piece) for piece in value]


class Flat:
    def __init__(self, ref, layers):
        self.ref, self.layers, self.parts = ref, layers, ref.shape[0]

    def put_layer(self, place, rows, value):
        for p in range(self.parts):
            self.ref.at[p][pl.ds(place, rows, stride=self.layers), :] = value[
                :, p * LANES : (p + 1) * LANES
            ]

    def get_layer(self, place, rows):
        pieces = [
            self.ref.at[p][pl.ds(place, rows, stride=self.layers), :] for p in range(self.parts)
        ]
        return jnp.concatenate(pieces, axis=1)

    def span(self, row, size):
        return pl.ds(pl.multiple_of(row * self.layers, self.layers), size * self.layers)

    def get(self, row, size):
        return [
            self.ref[p, self.span(row, size), :].reshape(size, self.layers, LANES)
            for p in range(self.parts)
        ]

    def put(self, row, size, value):
        for p in range(self.parts):
            self.ref[p, self.span(row, size), :] = value[p].reshape(size * self.layers, LANES)


def root_of(value):
    value = jnp.maximum(value, 1e-30)
    return value * lax.rsqrt(value)


class Straight:
    def __init__(self, layers, parts, at, grid_rows):
        shape = (1, layers, LANES)
        self.at_y, self.grid_rows = at[1], grid_rows
        dx = (lax.broadcasted_iota(jnp.int32, shape, 1) - at[0]).astype(jnp.float32)
        self.across = []
        for p in range(parts):
            dz = lax.broadcasted_iota(jnp.int32, shape, 2) + (p * LANES - at[2])
            dz = dz.astype(jnp.float32)
            self.across.append(dx * dx + dz * dz)

    def row(self, y):
        gap = y - self.at_y
        far = (gap * gap).astype(jnp.float32)
        inside = (y >= 0) & (y < self.grid_rows)
        return [jnp.where(inside, root_of(a + far), BIG) for a in self.across]


def local_solve(near_x, near_y, near_z, cost, twice, one_half):
    small = jnp.minimum(near_x, near_y)
    large = jnp.maximum(near_x, near_y)
    lowest = jnp.minimum(small, near_z)
    highest = jnp.maximum(large, near_z)
    middle = jnp.maximum(small, jnp.minimum(large, near_z))
    first_gap = middle - lowest
    second_gap = highest - lowest
    square = first_gap * first_gap
    double = 0.5 * (first_gap + root_of(twice - square))
    rest = square + second_gap * (second_gap - first_gap)
    root = root_of(one_half - rest)
    triple = (first_gap + second_gap) * (1.0 / 3.0) + root * (math.sqrt(2.0) / 3.0)
    over = jnp.where(double <= second_gap, double, triple)
    return lowest + jnp.where(cost <= first_gap, cost, over)


SWEEP_ROWS = 2
SWEEP_UNROLL = 16


def sweep_kernel(layers, own_rows, grid_rows, slots, chips, events, *refs):
    rows = own_rows + 2 * HALO
    pays, start, refs = refs[:slots], refs[slots], refs[slots + 1 :]
    depth = start.shape[-1]
    parts = depth // LANES
    vel_in, refs = refs[:chips][::-1], refs[chips:]
    times_out, final, speed, refs = refs[0], refs[1], refs[2], refs[3:]
    cost, twice, one_half, ping, pong, acts, mask, flat, staged, sems = refs
    flat = Flat(flat, layers)
    line = lax.axis_index("src")
    chip, core, _, y_first = where_am_i(own_rows)
    stations = [station_of(pay, events) for pay in pays]

    for j in range(chips):
        for c in range(2):
            place = (chip ^ j) * 2 + (core ^ c)
            flat.put_layer(place, rows, vel_in[j][c * rows : (c + 1) * rows, :])
            for slot in range(slots):
                for part in range(ROUNDS):
                    row = 2 * rows + slot * ROUNDS + part
                    acts[slot * ROUNDS + part, pl.ds(place, 1), :] = vel_in[j][
                        row : row + 1, c * LANES : (c + 1) * LANES
                    ]

    def prepare(row, size):
        value = flat.get(row, size)
        slow = each(lambda v: 1.0 / v, value)
        put(speed, row, size, value)
        put(cost, row, size, slow)
        put(twice, row, size, each(lambda f: 2.0 * (f * f), slow))
        put(one_half, row, size, each(lambda f: 1.5 * (f * f), slow))

    loop(0, rows, 4, prepare)

    lane_iota = lax.broadcasted_iota(jnp.int32, (layers, LANES), 1)
    tile_first = (y_first + TY) // TY - 1
    tile_span = (rows + TY - 2) // TY + 1
    for slot in range(slots):
        for part in range(ROUNDS):
            act = acts[slot * ROUNDS + part]
            columns = []
            for t in range(tile_span):
                here = lane_iota == tile_first + t
                picked = jnp.sum(jnp.where(here, act, 0.0), axis=1, keepdims=True)
                columns.append(jnp.broadcast_to(picked, (layers, LANES)))
            for i in range(rows):
                value = columns[0]
                for t in range(1, tile_span):
                    value = jnp.where(y_first + i >= (tile_first + t) * TY, columns[t], value)
                mask[slot, part, i] = value

    def sweep(source, target, low, high, part, shift, group):
        def body(row, size):
            grid = Grid(size, layers, depth)
            costs = get(cost, row, size), get(twice, row, size), get(one_half, row, size)
            for slot in group:
                field = get(source, row, size + 2, slot)
                here = each(lambda f: f[1 : size + 1], field)
                near_y = each(lambda f: jnp.minimum(f[:size], f[2:]), field)
                near_x = each(
                    jnp.minimum,
                    grid.no_low(grid.layer_before(here), BIG),
                    grid.no_high(grid.layer_after(here), BIG),
                )
                near_z = each(
                    jnp.minimum, grid.depth_before(here, BIG), grid.depth_after(here, BIG)
                )
                update = each(local_solve, near_x, near_y, near_z, *costs)
                on = mask[slot, part, pl.ds(row, size)] > 0.0
                put(
                    target,
                    row + shift,
                    size,
                    each(lambda u, h: jnp.where(on, u, h), update, here),
                    slot,
                )

        loop(low, high, SWEEP_ROWS, body, SWEEP_UNROLL if slots <= 4 else 1)
        for slot in group:
            at_x, at_y, at_z = stations[slot]
            local = at_y - y_first

            @pl.when((local >= low) & (local < high))
            def _():
                shape = (1, layers, depth)
                there = (lax.broadcasted_iota(jnp.int32, shape, 1) == at_x) & (
                    lax.broadcasted_iota(jnp.int32, shape, 2) == at_z
                )
                here = slot, pl.ds(local + shift, 1)
                target[here] = jnp.where(there, 0.0, target[here])

    fields = [start] + [(pong, ping)[i % 2] for i in range(ROUNDS * SWEEPS - 1)]
    last = ROUNDS * SWEEPS - 1
    every = range(slots)
    for index in range(last):
        sweep(fields[index], fields[index + 1], index, rows - index, index // SWEEPS, 1, every)
    copies = []
    for slot in every:
        sweep(fields[last], final, last, rows - last, last // SWEEPS, -last, [slot])
        loop(0, own_rows, 4, lambda row, size: flat.put(row, size, get(final, row + ADJ_HALO, size, slot)))
        for place in range(layers):
            staged[slot, place] = flat.get_layer(place, own_rows)
        copies.append(pltpu.make_async_copy(staged.at[slot], times_out.at[line ^ slot], sems.at[slot]))
        copies[-1].start()
    for copy in copies:
        copy.wait()


ADJ_ROWS = 4
ADJ_UNROLL = 8


def adjoint_kernel(layers, own_rows, grid_rows, slots, events, *refs):
    pays, (final, speed, count, delay_sum), refs = refs[:slots], refs[slots : slots + 4], refs[slots + 4 :]
    depth = final.shape[-1]
    parts = depth // LANES
    kernel_out, refs = refs[:layers], refs[layers:]
    weight, src, adj_a, adj_b, density, flat = refs
    together = weight.shape[0]
    flat = Flat(flat, layers)
    y_first = where_am_i(own_rows)[3]
    stations = [station_of(pay, events) for pay in pays]
    straight = [Straight(layers, parts, stations[slot], grid_rows) for slot in range(slots)]
    shift = HALO - ADJ_HALO
    rows = own_rows + 2 * ADJ_HALO

    def sums(ref, row, size, *lead):
        span = pl.ds(pl.multiple_of(row * layers, layers), size * layers)
        return [
            ref[(*lead, span, slice(p * LANES, (p + 1) * LANES))].reshape(size, layers, LANES)
            for p in range(parts)
        ]

    def make_source(group, row, size):
        for i in range(size):
            number = sums(count, row + i, 1)
            for slot in group:
                value = each(
                    lambda n, t, d, s: n * (t - d) - s,
                    number,
                    get(final, row + i, 1, slot),
                    straight[slot].row(y_first + shift + row + i),
                    sums(delay_sum, row + i, 1, slot),
                )
                put(src, row + i, 1, value, slot - group[0])

    def make_weight(group, row, size):
        grid = Grid(size, layers, depth)
        scale = each(lambda v: v * (1.0 / 6.0), get(speed, row + shift, size))
        for slot in group:
            field = get(final, row - 1, size + 2, slot)
            here = each(lambda f: f[1 : size + 1], field)

            def rise(value):
                return each(lambda v, h, s: jnp.maximum(v - h, 0.0) * s, value, here, scale)

            def keep(value, piece, edge):
                return [jnp.where(edge, 0.0, v) if p == piece else v for p, v in enumerate(value)]

            six = [
                grid.no_low(rise(grid.layer_before(here)), 0.0),
                grid.no_high(rise(grid.layer_after(here)), 0.0),
                rise(each(lambda f: f[:size], field)),
                rise(each(lambda f: f[2:], field)),
                keep(rise(grid.depth_before(here)), 0, grid.lane_low),
                keep(rise(grid.depth_after(here)), parts - 1, grid.lane_high),
            ]
            for n, value in enumerate(six):
                put(weight, row, size, value, slot - group[0], n)

    def multiply_add(value, factor, neighbour):
        return value + factor * neighbour

    def smooth(low, here, high):
        return (low + 2.0 * here + high) * 0.25

    def sweep(group, source, target, low, high):
        def body(row, size):
            grid = Grid(size, layers, depth)
            total = None if group[0] == 0 else get(density, row, size)
            for slot in range(len(group)):
                field = get(source, row - 1, size + 2, slot)
                here = each(lambda f: f[1 : size + 1], field)
                around = [
                    grid.layer_before(here),
                    grid.layer_after(here),
                    each(lambda f: f[:size], field),
                    each(lambda f: f[2:], field),
                    grid.depth_before(here),
                    grid.depth_after(here),
                ]
                value = get(src, row, size, slot)
                for n, neighbour in enumerate(around):
                    value = each(multiply_add, value, get(weight, row, size, slot, n), neighbour)
                if target is not None:
                    put(target, row, size, value, slot)
                else:
                    total = value if total is None else each(jnp.add, total, value)
            if target is None:
                if group[-1] == slots - 1:
                    value = each(lambda t, v: t / v, total, get(speed, row + shift, size))
                    low = grid.no_low(grid.layer_before(value), 0.0)
                    high = grid.no_high(grid.layer_after(value), 0.0)
                    total = each(smooth, low, value, high)
                put(density, row, size, total)

        loop(low, high, ADJ_ROWS, body, ADJ_UNROLL if slots <= 4 else 1)

    for first in range(0, slots, together):
        group = range(first, min(first + together, slots))
        loop(0, rows, 4, functools.partial(make_source, group))
        loop(1, rows - 1, 4, functools.partial(make_weight, group))
        fields = [src] + [(adj_a, adj_b)[i % 2] for i in range(ADJ_SWEEPS - 1)] + [None]
        for index in range(ADJ_SWEEPS):
            sweep(group, fields[index], fields[index + 1], index + 1, rows - 1 - index)

    def finish(row, size):
        grid = Grid(size, layers, depth)
        field = get(density, row + ADJ_SWEEPS, size + 2)
        value = each(lambda f: smooth(f[:size], f[1 : size + 1], f[2:]), field)
        low, high = grid.depth_before(value, 0.0), grid.depth_after(value, 0.0)
        flat.put(row, size, each(smooth, low, value, high))

    loop(0, own_rows, 4, finish)
    for m, out in enumerate(kernel_out):
        out[...] = flat.get_layer(lax.axis_index("space") ^ m, own_rows)


def join_kernel(times, *refs):
    blocks, (times_out, out, sems) = refs[:-3], refs[-3:]
    rows = blocks[0].shape[0]
    copies = [pltpu.make_async_copy(times, times_out, sems.at[0])]
    for m, block in enumerate(blocks):
        start = pl.multiple_of((lax.axis_index("space") ^ m) * rows, rows)
        copies.append(pltpu.make_async_copy(block, out.at[pl.ds(start, rows)], sems.at[m + 1]))
    for copy in copies:
        copy.start()
    for copy in copies:
        copy.wait()


def per_device(velocity, station_cells, event_cells, delays, active):
    _, grid_rows, depth = velocity.shape
    slots, layers = lax.axis_size("src"), lax.axis_size("space")
    chips = layers // 2
    events = event_cells.shape[1]
    line_rows = grid_rows // slots
    own_rows = line_rows // layers
    rows = own_rows + 2 * HALO
    adj_rows = own_rows + 2 * ADJ_HALO

    def to_line(array, j):
        return lax.ppermute(array, "src", [(i, i ^ j) for i in range(slots)])

    def to_chip(array, j):
        return lax.ppermute(array, "space", [(i, i ^ (2 * j)) for i in range(layers)])

    def to_core(array):
        return lax.ppermute(array, "space", [(i, i ^ 1) for i in range(layers)])

    f32 = jnp.float32
    def out(*shape):
        return jax.ShapeDtypeStruct(shape, f32)

    def scratch(*shape):
        return pltpu.VMEM(shape, f32)

    def field(*lead):
        return (*lead, layers, depth)

    other = to_core(velocity[0])
    active_other = to_core(active[:, 0])
    def fetch(name, *arrays):
        return call(
            fetch_kernel,
            name,
            [jax.ShapeDtypeStruct(a.shape, a.dtype) for a in arrays],
            arrays,
            [pltpu.SemaphoreType.DMA((len(arrays),))],
            hbm_in=range(len(arrays)),
        )

    delays, station_cells, active = fetch("fetch", delays, station_cells, active[:, 0])
    (payload,) = call(
        head_kernel,
        "head",
        [out(1, events + LANES * (1 + 2 * ROUNDS))],
        [delays, station_cells, active, active_other],
    )
    layer, payload = lax.optimization_barrier((velocity[0], payload))
    (layer,) = fetch("fetch_layer", layer)
    pays = [payload] + [to_line(payload, j) for j in range(1, slots)]

    height = 2 * rows + -(-slots * ROUNDS // 8) * 8
    packed = call(
        functools.partial(pack_kernel, rows, own_rows, slots),
        "pack",
        [out(height, depth)] * chips,
        [layer, other, *pays],
    )
    vel = [to_chip(packed[j], j) for j in range(chips - 1, 0, -1)] + [packed[0]]

    pays, cells, _ = lax.optimization_barrier((pays, event_cells, packed[0]))
    chunk = events
    while (1 + 2 * slots) * adj_rows * layers * chunk > EVENT_CHUNK * 2**11:
        chunk //= 2
    count, delay_sum, start = call(
        functools.partial(scatter_kernel, layers, own_rows, grid_rows, events),
        "events",
        [
            out(adj_rows * layers, depth),
            out(slots, adj_rows * layers, depth),
            out(*field(slots, rows + 2)),
        ],
        [cells, *pays],
        [pltpu.VMEM(((1 + 2 * slots) * adj_rows * layers, chunk), jnp.bfloat16)],
        microseconds=3.0,
    )

    pays, count, delay_sum, start = lax.optimization_barrier((pays, count, delay_sum, start))

    together = min(slots, 4)
    flat = scratch(depth // LANES, rows * layers, LANES)
    times, final, speed = call(
        functools.partial(sweep_kernel, layers, own_rows, grid_rows, slots, chips, events),
        "sweeps",
        [
            out(slots, layers, own_rows, depth),
            out(*field(slots, adj_rows)),
            out(*field(rows)),
        ],
        [*pays, start, *vel],
        [
            scratch(*field(rows)),
            scratch(*field(rows)),
            scratch(*field(rows)),
            scratch(*field(slots, rows + 2)),
            scratch(*field(slots, rows + 2)),
            scratch(slots * ROUNDS, layers, LANES),
            scratch(slots, ROUNDS, rows, layers, LANES),
            flat,
            scratch(slots, layers, own_rows, depth),
            pltpu.SemaphoreType.DMA((slots,)),
        ],
        hbm_out=(0,),
        microseconds=10.0,
    )
    kernel = call(
        functools.partial(adjoint_kernel, layers, own_rows, grid_rows, slots, events),
        "adjoint",
        [out(own_rows, depth)] * layers,
        [*pays, final, speed, count, delay_sum],
        [
            scratch(*field(together, 6, adj_rows)),
            scratch(*field(together, adj_rows)),
            scratch(*field(together, adj_rows)),
            scratch(*field(together, adj_rows)),
            scratch(*field(adj_rows)),
            flat,
        ],
        microseconds=7.0,
    )

    times = lax.all_to_all(
        times.reshape(slots * layers, own_rows, depth), ("src", "space"), 0, 0, tiled=True
    )
    blocks = [kernel[0]] + [
        lax.ppermute(kernel[m], "space", [(i, i ^ m) for i in range(layers)])
        for m in range(1, layers)
    ]
    times, kernel = call(
        join_kernel,
        "join",
        [out(grid_rows, depth), out(line_rows, depth)],
        [times.reshape(grid_rows, depth), *blocks],
        [pltpu.SemaphoreType.DMA((1 + layers,))],
        in_place=range(1 + layers),
        hbm_out=(0, 1),
    )
    return (times.reshape(1, 1, grid_rows, depth), kernel.reshape(1, line_rows, depth))


def solution(mesh):
    return jax.shard_map(
        per_device,
        mesh=mesh,
        in_specs=(
            P("space", None, None),
            P("src", None),
            P(),
            P("src", None),
            P(None, "src", "space", None),
        ),
        out_specs=(P("src", "space", None, None), P("space", "src", None)),
        check_vma=False,
    )
```
